256 devices in a mesh: phase: 2 (over z_hi), seq: 16 (over z_lo, x), head: 8 (over y, core).
Axes of the slice: x: 4, y: 4, z: 8 (z_hi: 2, z_lo: 4; z = z_hi * 4 + z_lo), core: 2. Of those that a mesh axis runs over, the one named last changes fastest.
Arguments:
- query_feats: bfloat16 [8192, 1024], P('seq', 'head'), may hold values from -4 to 4
- key_feats: bfloat16 [8192, 1024], P('seq', 'head'), may hold values from -4 to 4
- values: bfloat16 [8192, 8192], P('seq', 'head'), may hold values from -6 to 6
- keys_soft: bfloat16 [8192, 1024], P('seq', 'head'), may hold values from -320 to 320
- values_soft: bfloat16 [8192, 1024], P('seq', 'head'), may hold values from -6 to 6
- norm_gain: float32 [8192], P('head'), may hold values from 0.1 to 1.9
- doc_ids: int32 [8192], replicated, may hold values from 0 to 2, never falling along the last dimension, each value on 1 to 4096 neighbouring positions
Outputs:
- mixed: bfloat16 [2, 8192, 8192], P('phase', 'seq', 'head')
The draws below stay inside these ranges and needn't reach their ends.
Inputs may be any that keep to these rules, and one draw needn't show every extreme that they name: `doc_ids`: non-decreasing along the sequence; each document holds 1 to 4096 positions, and one holds exactly 4096.
All inputs are finite; a program needn't handle non-finite values.
Results may differ from the reference program's by a relative error of at most 0.01.
Values may be sent and summed in bfloat16 or wider, within the bound.
No kernel may reach another device: no remote copies, remote signals or barrier semaphores. Data moves between devices by JAX's collectives and lax.ppermute only.
A program may use at most 320 MiB of HBM per device.

```python
import math
import jax
import jax.numpy as jnp
import numpy as np
from jax import lax

H = 64
DH = 128
KVH = 8
F = 16
DOCS = 3
STRETCH = 512
L = 8192


def draw_keys_soft(key, part):
    key = jax.random.fold_in(key, 11)
    normal_key = jax.random.fold_in(key, 0)
    entries = jnp.clip(2.0 * jax.random.normal(normal_key, (L, KVH * DH), jnp.float32), -8.0, 8.0)
    return entries.astype(jnp.bfloat16)


def block_scale(key, shape, pieces, low, high):
    def one(position, parts):
        draws = jax.random.uniform(jax.random.fold_in(jax.random.fold_in(key, 6), position), (parts,), jnp.float32, low / len(pieces), high / len(pieces))
        return jnp.repeat(jnp.exp(draws), shape[position] // parts).reshape((-1,) + (1,) * (len(shape) - position - 1))

    loudness = one(*pieces[0])
    for cut in pieces[1:]:
        loudness = loudness * one(*cut)
    return loudness


def length_profile(number_of, total, bound, lean):
    loads = [(1 << 20) // math.isqrt(grade ** lean) + 1 for grade in range(2, number_of + 1)]
    surplus, holding = total - bound - (number_of - 1), [1] * (number_of - 1)
    while surplus > 0:
        movable = [i for i in range(number_of - 1) if holding[i] < bound]
        pool, remaining = sum([loads[i] for i in movable]), surplus
        for i in movable:
            extra = min(bound - holding[i], max(1, remaining * loads[i] // pool), surplus)
            holding[i] = holding[i] + extra
            surplus = surplus - extra
    return np.array([bound] + holding)


def ragged(own_key, amount, total, reach, lean):
    if amount == 2:
        one = jax.random.randint(own_key, (), max(1, total - reach), min(reach, total - 1) + 1)
        return jnp.stack([one, total - one])
    sizes = jnp.asarray(length_profile(amount, total, reach, lean), jnp.int32)
    couples = (amount - 1) // 2
    donor, taker = sizes[1:1 + 2 * couples:2], sizes[2:2 + 2 * couples:2]
    margin = jnp.minimum(donor - 1, reach - taker)
    shifted = jax.random.randint(jax.random.fold_in(own_key, 1), (couples,), 0, 1 << 20) % (margin + 1)
    sizes = sizes.at[1:1 + 2 * couples:2].set(donor - shifted).at[2:2 + 2 * couples:2].set(taker + shifted)
    return sizes[jax.random.permutation(jax.random.fold_in(own_key, 2), amount)]


def scatter_about(own_key, dims, deviation, most, pieces=(), kind=jnp.bfloat16):
    values = jax.random.normal(own_key, dims, jnp.float32) * deviation
    if len(pieces) > 0:
        values = block_scale(own_key, dims, pieces, -0.22, 0.18) * values
    return jnp.clip(values, min=-most, max=most).astype(kind)


def setup_inputs(seed: int = 0) -> dict:
    key_of = jax.random.split(jax.random.key(seed), 8)
    return {
        "query_feats": scatter_about(key_of[0], (L, H * F), 0.7, 4.0, ((0, 16), (1, 8))),
        "key_feats": scatter_about(key_of[1], (L, H * F), 0.7, 4.0, ((0, 16), (1, 8))),
        "values": scatter_about(key_of[2], (L, H * DH), 1.0, 6.0, ((0, 16), (1, 8))),
        "keys_soft": draw_keys_soft(jax.random.fold_in(key_of[7], 71), 0),
        "values_soft": scatter_about(key_of[4], (L, KVH * DH), 1.0, 6.0, ((0, 16), (1, 8))),
        "norm_gain": jnp.clip(1.0 + 0.18 * jax.random.normal(key_of[5], (H * DH,), jnp.float32), 0.1, 1.9),
        "doc_ids": jnp.searchsorted(jnp.cumsum(ragged(key_of[6], DOCS, L, L // 2, 0)), jnp.arange(L), side="right").astype(jnp.int32),
    }


precise = lax.Precision.HIGHEST
root_half = 0.5 ** 0.5
far_below = -1e+30

def taylor(vector):
    paired = (vector[..., :, None] * vector[..., None, :]).reshape(vector.shape[:-1] + (vector.shape[-1] * vector.shape[-1],))
    unity = jnp.ones_like(vector[..., :1])
    return jnp.concatenate([unity, vector, paired * root_half], -1)

def linear_head(queries, key_rows, value_rows, doc_ids):
    blocks = L // STRETCH
    query_blocks = queries.reshape(blocks, STRETCH, F)
    key_blocks = key_rows.reshape(blocks, STRETCH, F)
    value_blocks = value_rows.reshape(blocks, STRETCH, DH)
    doc_blocks = doc_ids.reshape(blocks, STRETCH)
    previous = jnp.concatenate([jnp.full((1,), -1, jnp.int32), doc_ids[STRETCH - 1:L - 1:STRETCH].astype(jnp.int32)])
    positions = jnp.arange(STRETCH)

    def step(carried_in, item):
        key_state, key_norm = carried_in
        query_now, key_now, value_now, doc_now, prior = item
        scores = jnp.dot(query_now, key_now.T, precision=precise)
        allowed = (positions[None, :] <= positions[:, None]) & (doc_now[None, :] == doc_now[:, None])
        weights = jnp.where(allowed, 1.0 + scores + 0.5 * scores * scores, 0.0)
        numerator = jnp.dot(weights, value_now, precision=precise)
        denominator = lax.optimization_barrier(jnp.sum(weights, 1))
        query_phi = taylor(query_now)
        usable = (doc_now == prior).astype(query_now.dtype)
        numerator = numerator + usable[:, None] * jnp.dot(query_phi, key_state, precision=precise)
        denominator = denominator + usable * jnp.dot(query_phi, key_norm, precision=precise)
        carried = (doc_now[-1] == prior).astype(query_now.dtype)
        select = (doc_now == doc_now[-1]).astype(query_now.dtype)
        key_phi = taylor(key_now) * select[:, None]
        key_state = carried * key_state + jnp.dot(key_phi.T, value_now, precision=precise)
        key_norm = carried * key_norm + lax.optimization_barrier(jnp.sum(key_phi, 0))
        return ((key_state, key_norm), numerator / denominator[:, None])
    initial = (jnp.zeros((1 + F + F * F, DH), queries.dtype), jnp.zeros((1 + F + F * F,), queries.dtype))
    unused_state, outputs = lax.scan(step, initial, (query_blocks, key_blocks, value_blocks, doc_blocks, previous))
    return outputs.reshape(L, DH)

def soft_head(index, queries_all, keys_all, values_all, doc_ids):
    group = H // KVH
    queries = queries_all[index]
    key_rows = lax.dynamic_index_in_dim(keys_all, index // group, keepdims=False)
    value_rows = lax.dynamic_index_in_dim(values_all, index // group, keepdims=False)
    positions = jnp.arange(L)
    allowed = (positions[None, :] <= positions[:, None]) & (doc_ids[None, :] == doc_ids[:, None])
    scores = jnp.dot(queries, key_rows.T, preferred_element_type=jnp.float32) / math.sqrt(DH)
    scores = jnp.where(allowed, scores, far_below)
    highest = lax.optimization_barrier(jnp.max(scores, 1, keepdims=True))
    expo = jnp.where(allowed, jnp.exp(scores - highest), 0.0)
    numerator = jnp.dot(expo.astype(jnp.bfloat16), value_rows, preferred_element_type=jnp.float32)
    return numerator / lax.optimization_barrier(jnp.sum(expo, 1, keepdims=True))

def reference(query_feats, key_feats, values, keys_soft, values_soft, norm_gain, doc_ids):
    query_heads = query_feats.astype(jnp.float32).reshape(L, H, F).transpose(1, 0, 2)
    key_heads = key_feats.astype(jnp.float32).reshape(L, H, F).transpose(1, 0, 2)
    value_heads = values.astype(jnp.float32).reshape(L, H, DH).transpose(1, 0, 2)
    linear_heads = lax.map(lambda item: linear_head(item[0], item[1], item[2], doc_ids), (query_heads, key_heads, value_heads))
    linear_out = linear_heads.transpose(1, 0, 2).reshape(L, H * DH).astype(jnp.bfloat16)
    widened = linear_out.astype(jnp.float32)
    total = lax.optimization_barrier(jnp.sum(widened * widened, 1))
    scale = lax.rsqrt(total / (H * DH) + 1e-06)
    queries = (widened * scale[:, None] * norm_gain[None, :]).astype(jnp.bfloat16)
    queries_all = queries.reshape(L, H, DH).transpose(1, 0, 2)
    keys_all = keys_soft.reshape(L, KVH, DH).transpose(1, 0, 2)
    values_all = values_soft.reshape(L, KVH, DH).transpose(1, 0, 2)
    soft_heads = lax.map(lambda index: soft_head(index, queries_all, keys_all, values_all, doc_ids), jnp.arange(H))
    soft_out = soft_heads.transpose(1, 0, 2).reshape(L, H * DH).astype(jnp.bfloat16)
    return jnp.stack([linear_out, soft_out])
```

```python
import math

import jax
import jax.numpy as jnp
from jax import lax
from jax.experimental import pallas as pl
from jax.experimental.pallas import tpu as pltpu
from jax.sharding import Mesh, PartitionSpec as P

DH = 128
F = 16
ROWS = 512
HEADS = 8
WIDE = HEADS * DH
ALL_WIDE = 64 * DH
USED = (F + 1) * (F + 2) // 2
FEATS = 160
QUARTER = HEADS * FEATS // 4
SLOTS = 9
LOG2E = math.log2(math.e)
FACTOR = LOG2E / math.sqrt(DH)
SAFE = 110.0
FAR = -1e30

NN = (((1,), (0,)), ((), ()))
NT = (((1,), (1,)), ((), ()))


def dot(a, b, dims=NN):
    return lax.dot_general(a, b, dims, preferred_element_type=jnp.float32)


def split(x):
    hi = x.astype(jnp.bfloat16)
    lo = (x - hi.astype(jnp.float32)).astype(jnp.bfloat16)
    return hi, lo


def doc_of(position, n1, n2):
    return (position >= n1).astype(jnp.int32) + (position >= n2).astype(jnp.int32)


def start_of(position, n1, n2):
    return jnp.where(position >= n2, n2, jnp.where(position >= n1, n1, 0))


def pair_of(e):
    gap = jnp.zeros_like(e)
    for k in range(1, F // 2 + 1):
        gap = gap + (e >= k * (F + 1)).astype(jnp.int32)
    m = e - gap * (F + 1)
    n = m + gap
    n = jnp.where(n > F, n - (F + 1), n)
    times = jnp.where((gap == 0) & (m < F), 1.0, 2.0)
    times = jnp.where(e < USED, times, 0.0)
    return m, n, times


def here():
    return lax.axis_index("z"), lax.axis_index("x")


def row_block(x, s):
    return lax.rem(x - s + 4, 4)


def last_doc(block, n1, n2):
    return doc_of(block * ROWS + ROWS - 1, n1, n2)


def flag(x):
    return x.astype(jnp.float32)


def row_sum_kernel(n_ref, p0_ref, p1_ref, p2_ref, p3_ref, out_ref):
    n1, n2 = n_ref[0], n_ref[1]
    z, x = here()
    end = last_doc(z * 4 + 3, n1, n2)
    total = jnp.zeros((QUARTER, DH), jnp.float32)
    for s, part in enumerate((p0_ref, p1_ref, p2_ref, p3_ref)):
        total = total + flag(last_doc(z * 4 + row_block(x, s), n1, n2) == end) * part[...]
    out_ref[...] = total


def prior_kernel(n_ref, p0_ref, p1_ref, p2_ref, p3_ref, near_ref, far_ref, *outs):
    n1, n2 = n_ref[0], n_ref[1]
    z, x = here()
    before = last_doc(z * 4 - 1, n1, n2)
    incoming = near_ref[...] + flag(last_doc(z * 4 - 5, n1, n2) == before) * far_ref[...]
    for t, out in enumerate(outs):
        target = lax.rem(x + t, 4)
        doc = last_doc(z * 4 + target - 1, n1, n2)
        prior = flag(before == doc) * incoming
        for s, part in enumerate((p0_ref, p1_ref, p2_ref, p3_ref)):
            block = row_block(x, s)
            prior = prior + flag((block < target) & (last_doc(z * 4 + block, n1, n2) == doc)) * part[...]
        out[...] = prior


def pack_kernel(own_hbm, near_hbm, far_hbm, o1_hbm, o2_hbm, o3_hbm, sems):
    z, x = here()
    upper, lower = pl.ds(0, 2 * ROWS), pl.ds(2 * ROWS, 2 * ROWS)
    for s, out in enumerate((o1_hbm, o2_hbm, o3_hbm)):
        later = lax.rem(x + s + 1, 4) > x
        pltpu.make_async_copy(near_hbm, out.at[upper], sems.at[s]).start()
        pl.when(later)(lambda: pltpu.make_async_copy(own_hbm, out.at[lower], sems.at[3 + s]).start())
        pl.when(jnp.logical_not(later))(lambda: pltpu.make_async_copy(far_hbm, out.at[lower], sems.at[3 + s]).start())
    for s, out in enumerate((o1_hbm, o2_hbm, o3_hbm)):
        pltpu.make_async_copy(near_hbm, out.at[upper], sems.at[s]).wait()
        pltpu.make_async_copy(own_hbm, out.at[lower], sems.at[3 + s]).wait()


def states_kernel(doc_hbm, kf_hbm, v_hbm, k_hbm, vs_hbm, c0_ref, c1_ref, c2_ref, c3_ref, kv_ref, n_ref, state_ref, doc_ref, kf_ref, v_ref, sems):
    pairs = [(doc_hbm, doc_ref), (kf_hbm, kf_ref), (v_hbm, v_ref), (k_hbm, kv_ref.at[:ROWS]), (vs_hbm, kv_ref.at[ROWS:])]
    copies = [pltpu.make_async_copy(src, dst, sems.at[i]) for i, (src, dst) in enumerate(pairs)]
    for copy in copies:
        copy.start()
    z, x = here()
    first = (z * 4 + x) * ROWS
    m, n, times = pair_of(lax.broadcasted_iota(jnp.int32, (FEATS, 2 * F), 0))
    col = lax.broadcasted_iota(jnp.int32, (FEATS, 2 * F), 1)
    e1 = ((col == m) & (times > 0)).astype(jnp.float32).astype(jnp.bfloat16)
    e2 = ((col == n) & (times > 0)).astype(jnp.float32).astype(jnp.bfloat16)
    lane = lax.broadcasted_iota(jnp.int32, (ROWS, DH), 1)
    norms = jnp.zeros((FEATS, DH), jnp.float32)
    copies[0].wait()
    n1 = jnp.sum((doc_ref[...] < 1).astype(jnp.int32))
    n2 = jnp.sum((doc_ref[...] < 2).astype(jnp.int32))
    n_ref[0] = n1
    n_ref[1] = n2
    pos = first + lax.broadcasted_iota(jnp.int32, (F, ROWS), 1)
    sel = (doc_of(pos, n1, n2) == doc_of(first + ROWS - 1, n1, n2)).astype(jnp.float32)
    copies[1].wait()
    kt = kf_ref[...].astype(jnp.float32).T
    copies[2].wait()
    for h in range(HEADS):
        rows = jnp.concatenate([kt[h * F : (h + 1) * F] * sel, sel], 0).astype(jnp.bfloat16)
        hi, lo = split(dot(e1, rows) * dot(e2, rows))
        unit = (lane == h).astype(jnp.bfloat16)
        rhs = jnp.concatenate([v_ref[:, h * DH : (h + 1) * DH], unit], 1)
        res = dot(hi, rhs) + dot(lo, rhs)
        state_ref[h * FEATS : (h + 1) * FEATS, :] = res[:, :DH]
        norms = norms + res[:, DH:]
    across = norms.T
    for h in range(HEADS):
        base = h * FEATS + USED
        state_ref[base : base + 1, :] = across[h : h + 1, :DH]
        state_ref[base + 1 : base + 2, : FEATS - DH] = across[h : h + 1, DH:]
    for s, out in enumerate((c0_ref, c1_ref, c2_ref, c3_ref)):
        chunk = lax.rem(x + s, 4)
        out[...] = state_ref[pl.ds(pl.multiple_of(chunk * QUARTER, QUARTER), QUARTER), :]
    copies[3].wait()
    copies[4].wait()


def local_kernel(n_ref, qf_ref, kf_ref, v_ref, num_ref, den_ref, hi_ref, lo_ref, mask_ref):
    n1, n2 = n_ref[0], n_ref[1]
    z, x = here()
    first = (z * 4 + x) * ROWS
    row = lax.broadcasted_iota(jnp.int32, (ROWS, ROWS), 0)
    col = lax.broadcasted_iota(jnp.int32, (ROWS, ROWS), 1)
    begin = start_of(first + lax.broadcasted_iota(jnp.int32, (ROWS, 1), 0), n1, n2) - first
    mask_ref[...] = ((col <= row) & (col >= begin)).astype(jnp.float32)
    lane = lax.broadcasted_iota(jnp.int32, (ROWS, DH), 1)
    one = (lane == 0).astype(jnp.bfloat16)
    kf = jnp.concatenate([kf_ref[...], one], 1)
    half = ROWS // 2
    dens = [jnp.zeros((half, DH), jnp.float32) for _ in range(2)]
    for h in range(HEADS):
        qh = jnp.where(lane // F == h, qf_ref[...], jnp.zeros((), jnp.bfloat16))
        qh = jnp.concatenate([qh, one], 1)
        unit = (lane == h).astype(jnp.bfloat16)
        rhs = jnp.concatenate([v_ref[:, h * DH : (h + 1) * DH], unit], 1)
        for r in range(2):
            span = (r + 1) * half
            s = dot(qh[r * half : (r + 1) * half], kf[:span], NT)
            w = (s * s + 1.0) * mask_ref[r * half : (r + 1) * half, :span]
            hi, lo = split(w)
            res = dot(hi, rhs[:span]) + dot(lo, rhs[:span])
            num_ref[r * half : (r + 1) * half, h * DH : (h + 1) * DH] = res[:, :DH]
            dens[r] = dens[r] + res[:, DH:]
    for r in range(2):
        den_ref[r * half : (r + 1) * half, :] = dens[r]
    m, n, times = pair_of(lax.broadcasted_iota(jnp.int32, (DH, 256), 1))
    lane_row = lax.broadcasted_iota(jnp.int32, (DH, 256), 0)
    m1, n1_, times1 = pair_of(lax.broadcasted_iota(jnp.int32, (1, 256), 1))
    ones_a = jnp.where(m1 == F, times1, 0.0)
    ones_b = jnp.where((n1_ == F) & (times1 > 0), 1.0, 0.0)
    once = (times > 0).astype(jnp.float32)
    q = qf_ref[...]
    for h in range(HEADS):
        e1 = jnp.where((lane_row == m + h * F) & (m < F), times, 0.0).astype(jnp.bfloat16)
        e2 = jnp.where((lane_row == n + h * F) & (n < F), once, 0.0).astype(jnp.bfloat16)
        hi, lo = split((dot(q, e1) + ones_a) * (dot(q, e2) + ones_b))
        hi_ref[:, h * 256 : (h + 1) * 256] = hi
        lo_ref[:, h * 256 : (h + 1) * 256] = lo


def finish_kernel(n_ref, hi_ref, lo_ref, num_ref, den_ref, p0_ref, p1_ref, p2_ref, p3_ref, out_ref, sq_ref, prior_ref):
    n1, n2 = n_ref[0], n_ref[1]
    z, x = here()
    first = (z * 4 + x) * ROWS
    pos = first + lax.broadcasted_iota(jnp.int32, (ROWS, 1), 0)
    usable = ((doc_of(pos, n1, n2) == doc_of(first - 1, n1, n2)) & (first > 0)).astype(jnp.float32)
    for s, part in enumerate((p0_ref, p1_ref, p2_ref, p3_ref)):
        chunk = lax.rem(x - s + 4, 4)
        prior_ref[pl.ds(pl.multiple_of(chunk * QUARTER, QUARTER), QUARTER), :] = part[...]
    spare = [jnp.zeros((DH - HEADS, DH), jnp.float32)]
    sums = [[prior_ref[h * FEATS + USED + i : h * FEATS + USED + i + 1, :] for h in range(HEADS)] for i in range(2)]
    norm = jnp.concatenate([jnp.concatenate(rows + spare, 0).T for rows in sums], 0)[:FEATS]
    norm_hi, norm_lo = split(norm)
    squares = jnp.zeros((ROWS, DH), jnp.float32)
    for h in range(HEADS):
        hi = hi_ref[:, h * 256 : h * 256 + FEATS]
        lo = lo_ref[:, h * 256 : h * 256 + FEATS]
        s_hi, s_lo = split(prior_ref[h * FEATS : (h + 1) * FEATS, :])
        r_hi = jnp.concatenate([s_hi, norm_hi], 1)
        r_lo = jnp.concatenate([s_lo, norm_lo], 1)
        res = (dot(hi, r_hi) + (dot(lo, r_hi) + dot(hi, r_lo))) * usable
        num = num_ref[:, h * DH : (h + 1) * DH] + res[:, :DH]
        den = den_ref[:, h : h + 1] + res[:, DH + h : DH + h + 1]
        out = (num / den).astype(jnp.bfloat16)
        out_ref[:, h * DH : (h + 1) * DH] = out
        wide = out.astype(jnp.float32)
        squares = squares + wide * wide
    sq_ref[...] = jnp.sum(squares.T, 0, keepdims=True)


def block_of(slot):
    z, x = here()
    src = lax.rem(x + 4 - lax.div(slot - 1, 2), 4)
    behind = jnp.where(lax.rem(slot, 2) == 1, 1, jnp.where(src < x, 0, 2))
    return jnp.where(slot < 3, z * 4 + x - 4 * slot, (z - behind) * 4 + src)


def active(slot, n1, n2):
    z, x = here()
    own = z * 4 + x
    low = start_of(own * ROWS, n1, n2) // ROWS
    return (block_of(slot) >= low) & (block_of(slot) < own) | (slot == 0)


def key_norms(kv_ref, slots, base, n1, n2):
    def one(slot, best):
        k = kv_ref[slot - base, :ROWS].astype(jnp.float32)
        norm = jnp.sum(k * k, 1, keepdims=True)
        return jnp.where(active(slot, n1, n2), jnp.maximum(best, norm), best)

    return jnp.max(lax.fori_loop(*slots, one, jnp.zeros((ROWS, 1), jnp.float32)))


def make_queries(lin_ref, total_ref, gain_ref, q_ref):
    scale = lax.rsqrt(total_ref[...] / ALL_WIDE + 1e-06)
    scale = jnp.broadcast_to(scale, (DH, ROWS)).T
    norm = jnp.zeros((ROWS, 1), jnp.float32)
    for h in range(HEADS):
        gain = gain_ref[0:1, h * DH : (h + 1) * DH]
        q = (lin_ref[:, h * DH : (h + 1) * DH].astype(jnp.float32) * scale * gain).astype(jnp.bfloat16)
        wide = q.astype(jnp.float32)
        norm = jnp.maximum(norm, jnp.sum(wide * wide, 1, keepdims=True))
        q_ref[h, :, :DH] = q
        q_ref[h, :, DH:] = jnp.zeros((ROWS, DH), jnp.bfloat16)
    return jnp.max(norm)


def ones_beside(v):
    return jnp.concatenate([v, jnp.ones((ROWS, DH), jnp.bfloat16)], 1)


def bounded_tile(kv_ref, slot, base, begin_first, q_ref, acc_ref):
    kk = jnp.concatenate([kv_ref[slot - base, :ROWS]] * 2, 1)
    key = block_of(slot) * ROWS + lax.broadcasted_iota(jnp.int32, (ROWS, 256), 0)
    inside = (key >= begin_first).astype(jnp.float32).astype(jnp.bfloat16)
    v = ones_beside(kv_ref[slot - base, ROWS:]) * inside
    for h in range(HEADS):
        p = jnp.exp2(dot(q_ref[h], kk, NT)).astype(jnp.bfloat16)
        acc_ref[h] += dot(p, v)


def make_mask(mask_ref, block, first, begin):
    row = lax.broadcasted_iota(jnp.int32, (ROWS, ROWS), 0)
    key = block * ROWS + lax.broadcasted_iota(jnp.int32, (ROWS, ROWS), 1)
    mask_ref[...] = jnp.where((key >= begin) & (key <= first + row), 0.0, FAR)


def any_tile(kv_ref, slot, base, first, begin, q_ref, acc_ref, mask_ref, top_ref):
    make_mask(mask_ref, block_of(slot), first, begin)
    kk = jnp.concatenate([kv_ref[slot - base, :ROWS]] * 2, 1)
    v = ones_beside(kv_ref[slot - base, ROWS:])

    def head(h, carry):
        s = jnp.maximum(dot(q_ref[h], kk, NT) * FACTOR + mask_ref[...], FAR)
        old = top_ref[h]
        new = jnp.maximum(old, jnp.max(s, 1, keepdims=True))
        p = jnp.exp2(s - jnp.concatenate([new] * 4, 1)).astype(jnp.bfloat16)
        fade = jnp.exp2(old - new)
        acc_ref[h] = acc_ref[h] * jnp.concatenate([fade] * 2, 1) + dot(p, v)
        top_ref[h] = new
        return carry

    lax.fori_loop(0, HEADS, head, 0)


def in_softmax_phase():
    return lax.axis_index("phase") == 1


def rows_of():
    z, x = here()
    first = (z * 4 + x) * ROWS
    return first, first + lax.broadcasted_iota(jnp.int32, (ROWS, 1), 0)


def open_kernel(n_ref, lin_ref, total_ref, gain_ref, near_hbm, far_hbm, q_ref, acc_ref, top_hbm, stat_ref, kv_ref, mask_ref, top_ref, sems):
    @pl.when(in_softmax_phase())
    def _():
        n1, n2 = n_ref[0], n_ref[1]
        first, positions = rows_of()
        copies = [pltpu.make_async_copy(src, kv_ref.at[i], sems.at[i]) for i, src in enumerate((near_hbm, far_hbm))]
        for copy in copies:
            copy.start()
        q_most = make_queries(lin_ref, total_ref, gain_ref, q_ref)
        acc_ref[...] = jnp.zeros_like(acc_ref)
        for copy in copies:
            copy.wait()
        safe = q_most * key_norms(kv_ref, (1, 3), 1, n1, n2) < (SAFE / FACTOR) ** 2
        stat_ref[0] = q_most
        stat_ref[1] = jnp.where(safe, 1.0, 0.0)

        @pl.when(safe)
        def _():
            for h in range(HEADS):
                hi, lo = split(q_ref[h, :, :DH].astype(jnp.float32) * FACTOR)
                q_ref[h, :, :DH] = hi
                q_ref[h, :, DH:] = lo
            begin_first = start_of(first, n1, n2)

            def step(slot, carry):
                pl.when(active(slot, n1, n2))(lambda: bounded_tile(kv_ref, slot, 1, begin_first, q_ref, acc_ref))
                return carry

            lax.fori_loop(1, 3, step, 0)

        @pl.when(jnp.logical_not(safe))
        def _():
            top_ref[...] = jnp.full(top_ref.shape, FAR, jnp.float32)
            begin = start_of(positions, n1, n2)

            def step(slot, carry):
                pl.when(active(slot, n1, n2))(
                    lambda: any_tile(kv_ref, slot, 1, first, begin, q_ref, acc_ref, mask_ref, top_ref)
                )
                return carry

            lax.fori_loop(1, 3, step, 0)
            copy = pltpu.make_async_copy(top_ref, top_hbm, sems.at[0])
            copy.start()
            copy.wait()


def close_kernel(n_ref, stat_ref, lin_ref, total_ref, gain_ref, q_ref, part_ref, top_hbm, *refs):
    kv_hbm, (out_hbm, kv_ref, raw_ref, acc_ref, mask_ref, top_ref, out_ref, kv_sems, out_sems) = refs[:4], refs[4:]

    @pl.when(jnp.logical_not(in_softmax_phase()))
    def _():
        copy = pltpu.make_async_copy(lin_ref, out_hbm, out_sems.at[0])
        copy.start()
        copy.wait()

    @pl.when(in_softmax_phase())
    def _():
        close(
            n_ref, stat_ref, lin_ref, total_ref, gain_ref, q_ref, part_ref, top_hbm, kv_hbm,
            out_hbm, kv_ref, raw_ref, acc_ref, mask_ref, top_ref, out_ref, kv_sems, out_sems,
        )


def close(
    n_ref, stat_ref, lin_ref, total_ref, gain_ref, q_ref, part_ref, top_hbm, kv_hbm,
    out_hbm, kv_ref, raw_ref, acc_ref, mask_ref, top_ref, out_ref, kv_sems, out_sems,
):
    n1, n2 = n_ref[0], n_ref[1]
    first, positions = rows_of()
    begin_first = start_of(first, n1, n2)
    begin = start_of(positions, n1, n2)
    base = 2

    def fetch(slot):
        if slot == 0:
            return pltpu.make_async_copy(kv_hbm[0], kv_ref.at[0], kv_sems.at[0])
        src = kv_hbm[(slot - 1) // 2].at[pl.ds((slot - 1) % 2 * 2 * ROWS, 2 * ROWS)]
        return pltpu.make_async_copy(src, kv_ref.at[slot - base], kv_sems.at[slot - base])

    here_slots = (0,) + tuple(range(3, SLOTS))
    for slot in here_slots:
        pl.when(active(slot, n1, n2))(lambda: fetch(slot).start())
    acc_ref[...] = part_ref[...]
    for slot in here_slots:
        pl.when(active(slot, n1, n2))(lambda: fetch(slot).wait())

    k_most = jnp.maximum(key_norms(kv_ref, (3, SLOTS), base, n1, n2), key_norms(kv_ref, (0, 1), 0, n1, n2))
    opened_safe = stat_ref[1] > 0.5
    safe = opened_safe & (stat_ref[0] * k_most < (SAFE / FACTOR) ** 2)

    @pl.when(safe)
    def _():
        def step(slot, carry):
            pl.when(active(slot, n1, n2))(lambda: bounded_tile(kv_ref, slot, base, begin_first, q_ref, acc_ref))
            return carry

        lax.fori_loop(3, SLOTS, step, 0)

        make_mask(mask_ref, block_of(0), first, begin)
        kk = jnp.concatenate([kv_ref[0, :ROWS]] * 2, 1)
        v = ones_beside(kv_ref[0, ROWS:])
        keep = (begin < first).astype(jnp.float32)
        half = ROWS // 2
        for h in range(HEADS):
            for r in range(2):
                rows, span = slice(r * half, (r + 1) * half), (r + 1) * half
                s = dot(q_ref[h, rows, :], kk[:span], NT) + mask_ref[rows, :span]
                p = jnp.exp2(s).astype(jnp.bfloat16)
                acc_ref[h, rows, :] = acc_ref[h, rows, :] * keep[rows] + dot(p, v[:span])

    @pl.when(jnp.logical_not(safe))
    def _():
        make_queries(lin_ref, total_ref, gain_ref, raw_ref)

        @pl.when(jnp.logical_not(opened_safe))
        def _():
            copy = pltpu.make_async_copy(top_hbm, top_ref, kv_sems.at[0])
            copy.start()
            copy.wait()

        @pl.when(opened_safe)
        def _():
            opened = active(1, n1, n2) | active(2, n1, n2)
            keep = (positions - first < jnp.where(opened, ROWS, 0)) & (begin == begin_first)
            for h in range(HEADS):
                top_ref[h] = jnp.where(jnp.broadcast_to(keep, (ROWS, DH)), 0.0, FAR)
                acc_ref[h] = jnp.where(jnp.broadcast_to(keep, (ROWS, 256)), acc_ref[h], 0.0)

        def step(slot, carry):
            pl.when(active(slot, n1, n2))(
                lambda: any_tile(kv_ref, slot, base, first, begin, raw_ref, acc_ref, mask_ref, top_ref)
            )
            return carry

        lax.fori_loop(3, SLOTS, step, 0)
        any_tile(kv_ref, 0, 0, first, begin, raw_ref, acc_ref, mask_ref, top_ref)

    copies = []
    for h in range(HEADS):
        lanes = slice(h * DH, (h + 1) * DH)
        out_ref[:, lanes] = (acc_ref[h, :, :DH] / acc_ref[h, :, DH:]).astype(jnp.bfloat16)
        copies.append(pltpu.make_async_copy(out_ref.at[:, lanes], out_hbm.at[:, lanes], out_sems.at[h]))
        copies[-1].start()
    for copy in copies:
        copy.wait()


VMEM = pl.BlockSpec(memory_space=pltpu.VMEM)
SMEM = pl.BlockSpec(memory_space=pltpu.SMEM)
ANY = pl.BlockSpec(memory_space=pl.ANY)


def call(kernel, outs, out_specs, args, in_specs, scratch, flops, limit):
    return pl.pallas_call(
        kernel,
        out_shape=tuple(outs),
        in_specs=in_specs,
        out_specs=tuple(out_specs),
        scratch_shapes=scratch,
        compiler_params=pltpu.CompilerParams(vmem_limit_bytes=limit << 20),
        cost_estimate=pl.CostEstimate(flops=flops, bytes_accessed=0, transcendentals=0),
    )(*args)


def shape(dims, dtype=jnp.float32):
    return jax.ShapeDtypeStruct(dims, dtype)


def row_sum(counts, parts):
    return call(row_sum_kernel, [shape((QUARTER, DH))], [VMEM], (counts,) + tuple(parts), [SMEM] + [VMEM] * 4, [], 0, 8)[0]


def priors_of(counts, parts, near, far):
    return call(
        prior_kernel,
        [shape((QUARTER, DH))] * 4,
        [VMEM] * 4,
        (counts,) + tuple(parts) + (near, far),
        [SMEM] + [VMEM] * 6,
        [],
        1000000000,
        8,
    )


def pack(own_kv, near_kv, far_kv):
    return call(
        pack_kernel,
        [shape((4 * ROWS, DH), own_kv.dtype)] * 3,
        [ANY] * 3,
        (own_kv, near_kv, far_kv),
        [ANY] * 3,
        [pltpu.SemaphoreType.DMA((6,))],
        5000000000,
        4,
    )


def states(doc_ids, key_feats, values, keys_soft, values_soft):
    bf16 = jnp.bfloat16
    return call(
        states_kernel,
        [shape((QUARTER, DH))] * 4 + [shape((2 * ROWS, DH), bf16), shape((8,), jnp.int32)],
        [VMEM] * 5 + [SMEM],
        (doc_ids.reshape(-1, DH), key_feats, values, keys_soft, values_soft),
        [ANY] * 5,
        [
            pltpu.VMEM((HEADS * FEATS, DH), jnp.float32),
            pltpu.VMEM((doc_ids.shape[0] // DH, DH), jnp.int32),
            pltpu.VMEM((ROWS, DH), bf16),
            pltpu.VMEM((ROWS, WIDE), bf16),
            pltpu.SemaphoreType.DMA((5,)),
        ],
        0,
        60,
    )


def local_part(counts, query_feats, key_feats, values):
    bf16 = jnp.bfloat16
    return call(
        local_kernel,
        [shape((ROWS, WIDE)), shape((ROWS, DH)), shape((ROWS, HEADS * 256), bf16), shape((ROWS, HEADS * 256), bf16)],
        [VMEM] * 4,
        (counts, query_feats, key_feats, values),
        [SMEM] + [VMEM] * 3,
        [pltpu.VMEM((ROWS, ROWS), jnp.float32)],
        0,
        24,
    )


def finish(counts, feats_hi, feats_lo, num, den, parts):
    return call(
        finish_kernel,
        [shape((ROWS, WIDE), jnp.bfloat16), shape((1, ROWS))],
        [VMEM] * 2,
        (counts, feats_hi, feats_lo, num, den) + tuple(parts),
        [SMEM] + [VMEM] * 8,
        [pltpu.VMEM((HEADS * FEATS, DH), jnp.float32)],
        8000000000,
        20,
    )


def soft_open(counts, linear_out, total, gain, near_kv, far_kv):
    bf16 = jnp.bfloat16
    return call(
        open_kernel,
        [shape((HEADS, ROWS, 256), bf16), shape((HEADS, ROWS, 256)), shape((HEADS, ROWS, DH)), shape((8,))],
        [VMEM, VMEM, ANY, SMEM],
        (counts, linear_out, total, gain, near_kv, far_kv),
        [SMEM] + [VMEM] * 3 + [ANY] * 2,
        [
            pltpu.VMEM((2, 2 * ROWS, DH), bf16),
            pltpu.VMEM((ROWS, ROWS), jnp.float32),
            pltpu.VMEM((HEADS, ROWS, DH), jnp.float32),
            pltpu.SemaphoreType.DMA((2,)),
        ],
        0,
        28,
    )


def soft_close(counts, stat, linear_out, total, gain, queries, part, top, pieces):
    bf16 = jnp.bfloat16
    return call(
        close_kernel,
        [shape((ROWS, WIDE), bf16)],
        [ANY],
        (counts, stat, linear_out, total, gain, queries, part, top) + tuple(pieces),
        [SMEM] * 2 + [VMEM] * 5 + [ANY] * 5,
        [
            pltpu.VMEM((SLOTS - 2, 2 * ROWS, DH), bf16),
            pltpu.VMEM((HEADS, ROWS, 256), bf16),
            pltpu.VMEM((HEADS, ROWS, 256), jnp.float32),
            pltpu.VMEM((ROWS, ROWS), jnp.float32),
            pltpu.VMEM((HEADS, ROWS, DH), jnp.float32),
            pltpu.VMEM((ROWS, WIDE), bf16),
            pltpu.SemaphoreType.DMA((SLOTS - 2,)),
            pltpu.SemaphoreType.DMA((HEADS,)),
        ],
        0,
        32,
    )[0]


def shift(x, axis, by):
    size = lax.axis_size(axis)
    return lax.ppermute(x, axis, [(i, (i + by) % size) for i in range(size)])


def after(x, *others):
    return lax.optimization_barrier((x,) + others)[0]


def local(query_feats, key_feats, values, keys_soft, values_soft, norm_gain, doc_ids):
    zs = lax.axis_size("z")
    *chunks, own_kv, counts = states(doc_ids, key_feats, values, keys_soft, values_soft)

    parts = [chunks[0]] + [shift(chunks[s], "x", s) for s in (1, 2, 3)]

    near_kv = lax.ppermute(own_kv, ("phase", "z"), [(zs + i, zs + i + 1) for i in range(zs - 1)])
    far_kv = lax.ppermute(own_kv, ("phase", "z"), [(i, zs + i + 2) for i in range(zs - 2)])

    local_sums = local_part(counts, query_feats, key_feats, values)
    total = row_sum(counts, parts)
    near = lax.ppermute(total, "z", [(i, i + 1) for i in range(zs - 1)])
    far = lax.ppermute(
        total,
        ("phase", "z"),
        [((1 - p) * zs + i, p * zs + i + 2) for p in range(2) for i in range(zs - 2)],
    )

    messages = lax.optimization_barrier((total,) + tuple(pack(own_kv, near_kv, far_kv)))[1:]
    others = [
        lax.ppermute(message, ("phase", "x"), [(4 + i, 4 + (i + s) % 4) for i in range(4)])
        for s, message in zip((1, 2, 3), messages)
    ]

    near = after(near, *local_sums)
    priors = priors_of(counts, parts, near, far)
    arrived = [priors[0]] + [shift(priors[s], "x", s) for s in (1, 2, 3)]
    num, den, feats_hi, feats_lo = local_sums
    linear_out, squares = finish(counts, feats_hi, feats_lo, num, den, arrived)
    total = squares + shift(squares, "core", 1)
    for pairs in ((1, 0, 3, 2), (3, 2, 1, 0)):
        total = total + lax.ppermute(total, "y", list(enumerate(pairs)))
    gain = norm_gain[None]
    queries, part, top, stat = soft_open(counts, linear_out, total, gain, near_kv, far_kv)
    return soft_close(counts, stat, linear_out, total, gain, queries, part, top, [own_kv] + others)[None]


def solution(mesh):
    fine = Mesh(mesh.devices.reshape(2, 4, 4, 4, 2), ("phase", "z", "x", "y", "core"))
    seq, head = ("z", "x"), ("y", "core")
    return jax.shard_map(
        local,
        mesh=fine,
        in_specs=(
            P(seq, head),
            P(seq, head),
            P(seq, head),
            P(seq, head),
            P(seq, head),
            P(head),
            P(),
        ),
        out_specs=P("phase", seq, head),
        check_vma=False,
    )
```

```python
import math

import jax
import jax.numpy as jnp
from jax import lax
from jax.experimental import pallas as pl
from jax.experimental.pallas import tpu as pltpu
from jax.sharding import Mesh, PartitionSpec as P

DH = 128
F = 16
ROWS = 512
HEADS = 8
WIDE = HEADS * DH
ALL_WIDE = 64 * DH
USED = (F + 1) * (F + 2) // 2
FEATS = 160
QUARTER = HEADS * FEATS // 4
SLOTS = 9
LOG2E = math.log2(math.e)
FACTOR = LOG2E / math.sqrt(DH)
SAFE = 108.0
FAR = -1e30

NN = (((1,), (0,)), ((), ()))
NT = (((1,), (1,)), ((), ()))


def dot(a, b, dims=NN):
    return lax.dot_general(a, b, dims, preferred_element_type=jnp.float32)


def split(x):
    hi = x.astype(jnp.bfloat16)
    lo = (x - hi.astype(jnp.float32)).astype(jnp.bfloat16)
    return hi, lo


def doc_of(position, n1, n2):
    return (position >= n1).astype(jnp.int32) + (position >= n2).astype(jnp.int32)


def start_of(position, n1, n2):
    return jnp.where(position >= n2, n2, jnp.where(position >= n1, n1, 0))


def pair_of(e):
    gap = jnp.zeros_like(e)
    for k in range(1, F // 2 + 1):
        gap = gap + (e >= k * (F + 1)).astype(jnp.int32)
    m = e - gap * (F + 1)
    n = m + gap
    n = jnp.where(n > F, n - (F + 1), n)
    times = jnp.where((gap == 0) & (m < F), 1.0, 2.0)
    times = jnp.where(e < USED, times, 0.0)
    return m, n, times


def here():
    return lax.axis_index("z"), lax.axis_index("x")


def last_doc(block, n1, n2):
    return doc_of(block * ROWS + ROWS - 1, n1, n2)


def flag(x):
    return x.astype(jnp.float32)


def chunk_of(parts_ref, s):
    return parts_ref[s * QUARTER : (s + 1) * QUARTER, :]


def row_sum_kernel(n_ref, parts_ref, out_ref):
    n1, n2 = n_ref[0], n_ref[1]
    z, x = here()
    end = last_doc(z * 4 + 3, n1, n2)
    total = jnp.zeros((QUARTER, DH), jnp.float32)
    for s in range(4):
        total = total + flag(last_doc(z * 4 + s, n1, n2) == end) * chunk_of(parts_ref, s)
    out_ref[...] = total


def prior_kernel(n_ref, parts_ref, near_ref, far_ref, *outs):
    n1, n2 = n_ref[0], n_ref[1]
    z, x = here()
    before = last_doc(z * 4 - 1, n1, n2)
    incoming = near_ref[...] + flag(last_doc(z * 4 - 5, n1, n2) == before) * far_ref[...]
    for t, out in enumerate(outs):
        target = lax.rem(x + t, 4)
        doc = last_doc(z * 4 + target - 1, n1, n2)
        prior = flag(before == doc) * incoming
        for s in range(4):
            use = (s < target) & (last_doc(z * 4 + s, n1, n2) == doc)
            prior = prior + flag(use) * chunk_of(parts_ref, s)
        out[...] = prior


def pack_kernel(own_hbm, near_hbm, far_hbm, o1_hbm, o2_hbm, o3_hbm, sems):
    z, x = here()
    upper, lower = pl.ds(0, 2 * ROWS), pl.ds(2 * ROWS, 2 * ROWS)
    for s, out in enumerate((o1_hbm, o2_hbm, o3_hbm)):
        later = lax.rem(x + s + 1, 4) > x
        pltpu.make_async_copy(near_hbm, out.at[upper], sems.at[s]).start()
        pl.when(later)(lambda: pltpu.make_async_copy(own_hbm, out.at[lower], sems.at[3 + s]).start())
        pl.when(jnp.logical_not(later))(lambda: pltpu.make_async_copy(far_hbm, out.at[lower], sems.at[3 + s]).start())
    for s, out in enumerate((o1_hbm, o2_hbm, o3_hbm)):
        pltpu.make_async_copy(near_hbm, out.at[upper], sems.at[s]).wait()
        pltpu.make_async_copy(own_hbm, out.at[lower], sems.at[3 + s]).wait()


def states_kernel(doc_hbm, kf_hbm, v_hbm, k_hbm, vs_hbm, state_ref, kv_ref, n_ref, doc_ref, kf_ref, v_ref, sems):
    pairs = [(doc_hbm, doc_ref), (kf_hbm, kf_ref), (v_hbm, v_ref), (k_hbm, kv_ref.at[:ROWS]), (vs_hbm, kv_ref.at[ROWS:])]
    copies = [pltpu.make_async_copy(src, dst, sems.at[i]) for i, (src, dst) in enumerate(pairs)]
    for copy in copies:
        copy.start()
    z, x = here()
    first = (z * 4 + x) * ROWS
    m, n, times = pair_of(lax.broadcasted_iota(jnp.int32, (FEATS, 2 * F), 0))
    col = lax.broadcasted_iota(jnp.int32, (FEATS, 2 * F), 1)
    e1 = ((col == m) & (times > 0)).astype(jnp.float32).astype(jnp.bfloat16)
    e2 = ((col == n) & (times > 0)).astype(jnp.float32).astype(jnp.bfloat16)
    lane = lax.broadcasted_iota(jnp.int32, (ROWS, DH), 1)
    norms = jnp.zeros((FEATS, DH), jnp.float32)
    copies[0].wait()
    n1 = jnp.sum((doc_ref[...] < 1).astype(jnp.int32))
    n2 = jnp.sum((doc_ref[...] < 2).astype(jnp.int32))
    n_ref[0] = n1
    n_ref[1] = n2
    pos = first + lax.broadcasted_iota(jnp.int32, (F, ROWS), 1)
    sel = (doc_of(pos, n1, n2) == doc_of(first + ROWS - 1, n1, n2)).astype(jnp.float32)
    copies[1].wait()
    kt = kf_ref[...].astype(jnp.float32).T
    copies[2].wait()
    for h in range(HEADS):
        rows = jnp.concatenate([kt[h * F : (h + 1) * F] * sel, sel], 0).astype(jnp.bfloat16)
        hi, lo = split(dot(e1, rows) * dot(e2, rows))
        unit = (lane == h).astype(jnp.bfloat16)
        rhs = jnp.concatenate([v_ref[:, h * DH : (h + 1) * DH], unit], 1)
        res = dot(hi, rhs) + dot(lo, rhs)
        state_ref[h * FEATS : (h + 1) * FEATS, :] = res[:, :DH]
        norms = norms + res[:, DH:]
    across = norms.T
    for h in range(HEADS):
        base = h * FEATS + USED
        state_ref[base : base + 1, :] = across[h : h + 1, :DH]
        state_ref[base + 1 : base + 2, : FEATS - DH] = across[h : h + 1, DH:]
    copies[3].wait()
    copies[4].wait()


def local_kernel(n_ref, qf_ref, kf_ref, v_ref, num_ref, den_ref, hi_ref, lo_ref, mask_ref):
    n1, n2 = n_ref[0], n_ref[1]
    z, x = here()
    first = (z * 4 + x) * ROWS
    row = lax.broadcasted_iota(jnp.int32, (ROWS, ROWS), 0)
    col = lax.broadcasted_iota(jnp.int32, (ROWS, ROWS), 1)
    begin = start_of(first + lax.broadcasted_iota(jnp.int32, (ROWS, 1), 0), n1, n2) - first
    mask_ref[...] = ((col <= row) & (col >= begin)).astype(jnp.float32)
    lane = lax.broadcasted_iota(jnp.int32, (ROWS, DH), 1)
    one = (lane == 0).astype(jnp.bfloat16)
    kf = jnp.concatenate([kf_ref[...], one], 1)
    half = ROWS // 2
    dens = [jnp.zeros((half, DH), jnp.float32) for _ in range(2)]
    for h in range(HEADS):
        qh = jnp.where(lane // F == h, qf_ref[...], jnp.zeros((), jnp.bfloat16))
        qh = jnp.concatenate([qh, one], 1)
        unit = (lane == h).astype(jnp.bfloat16)
        rhs = jnp.concatenate([v_ref[:, h * DH : (h + 1) * DH], unit], 1)
        for r in range(2):
            span = (r + 1) * half
            s = dot(qh[r * half : (r + 1) * half], kf[:span], NT)
            w = (s * s + 1.0) * mask_ref[r * half : (r + 1) * half, :span]
            hi, lo = split(w)
            res = dot(hi, rhs[:span]) + dot(lo, rhs[:span])
            num_ref[r * half : (r + 1) * half, h * DH : (h + 1) * DH] = res[:, :DH]
            dens[r] = dens[r] + res[:, DH:]
    for r in range(2):
        den_ref[r * half : (r + 1) * half, :] = dens[r]
    m, n, times = pair_of(lax.broadcasted_iota(jnp.int32, (DH, 256), 1))
    lane_row = lax.broadcasted_iota(jnp.int32, (DH, 256), 0)
    m1, n1_, times1 = pair_of(lax.broadcasted_iota(jnp.int32, (1, 256), 1))
    ones_a = jnp.where(m1 == F, times1, 0.0)
    ones_b = jnp.where((n1_ == F) & (times1 > 0), 1.0, 0.0)
    once = (times > 0).astype(jnp.float32)
    q = qf_ref[...]
    for h in range(HEADS):
        e1 = jnp.where((lane_row == m + h * F) & (m < F), times, 0.0).astype(jnp.bfloat16)
        e2 = jnp.where((lane_row == n + h * F) & (n < F), once, 0.0).astype(jnp.bfloat16)
        hi, lo = split((dot(q, e1) + ones_a) * (dot(q, e2) + ones_b))
        hi_ref[:, h * 256 : (h + 1) * 256] = hi
        lo_ref[:, h * 256 : (h + 1) * 256] = lo


def finish_kernel(n_ref, hi_ref, lo_ref, num_ref, den_ref, p0_ref, p1_ref, p2_ref, p3_ref, out_ref, sq_ref, prior_ref):
    n1, n2 = n_ref[0], n_ref[1]
    z, x = here()
    first = (z * 4 + x) * ROWS
    pos = first + lax.broadcasted_iota(jnp.int32, (ROWS, 1), 0)
    usable = ((doc_of(pos, n1, n2) == doc_of(first - 1, n1, n2)) & (first > 0)).astype(jnp.float32)
    for s, part in enumerate((p0_ref, p1_ref, p2_ref, p3_ref)):
        chunk = lax.rem(x - s + 4, 4)
        prior_ref[pl.ds(pl.multiple_of(chunk * QUARTER, QUARTER), QUARTER), :] = part[...]
    spare = [jnp.zeros((DH - HEADS, DH), jnp.float32)]
    sums = [[prior_ref[h * FEATS + USED + i : h * FEATS + USED + i + 1, :] for h in range(HEADS)] for i in range(2)]
    norm = jnp.concatenate([jnp.concatenate(rows + spare, 0).T for rows in sums], 0)[:FEATS]
    norm_hi, norm_lo = split(norm)
    squares = jnp.zeros((ROWS, DH), jnp.float32)
    for h in range(HEADS):
        hi = hi_ref[:, h * 256 : h * 256 + FEATS]
        lo = lo_ref[:, h * 256 : h * 256 + FEATS]
        s_hi, s_lo = split(prior_ref[h * FEATS : (h + 1) * FEATS, :])
        r_hi = jnp.concatenate([s_hi, norm_hi], 1)
        r_lo = jnp.concatenate([s_lo, norm_lo], 1)
        res = (dot(hi, r_hi) + (dot(lo, r_hi) + dot(hi, r_lo))) * usable
        num = num_ref[:, h * DH : (h + 1) * DH] + res[:, :DH]
        den = den_ref[:, h : h + 1] + res[:, DH + h : DH + h + 1]
        out = (num / den).astype(jnp.bfloat16)
        out_ref[:, h * DH : (h + 1) * DH] = out
        wide = out.astype(jnp.float32)
        squares = squares + wide * wide
    sq_ref[...] = jnp.broadcast_to(jnp.sum(squares.T, 0, keepdims=True), (8, ROWS))


def block_of(slot):
    z, x = here()
    src = lax.rem(x + 4 - lax.div(slot - 1, 2), 4)
    behind = jnp.where(lax.rem(slot, 2) == 1, 1, jnp.where(src < x, 0, 2))
    return jnp.where(slot < 3, z * 4 + x - 4 * slot, (z - behind) * 4 + src)


def active(slot, n1, n2):
    z, x = here()
    own = z * 4 + x
    low = start_of(own * ROWS, n1, n2) // ROWS
    return (block_of(slot) >= low) & (block_of(slot) < own) | (slot == 0)


def row_norms(x):
    return dot((x * x).astype(jnp.bfloat16), jnp.ones((DH, DH), jnp.bfloat16))


def key_norms(kv_ref, slots, base, n1, n2):
    def one(slot, best):
        norm = row_norms(kv_ref[slot - base, :ROWS].astype(jnp.float32))
        return jnp.where(active(slot, n1, n2), jnp.maximum(best, norm), best)

    return jnp.max(lax.fori_loop(*slots, one, jnp.zeros((ROWS, DH), jnp.float32)))


def make_queries(lin_ref, total_ref, gain_ref, q_ref):
    scale = lax.rsqrt(jnp.sum(total_ref[...], 0, keepdims=True) / ALL_WIDE + 1e-06)
    scale = jnp.broadcast_to(scale, (DH, ROWS)).T
    norm = jnp.zeros((ROWS, DH), jnp.float32)
    for h in range(HEADS):
        gain = gain_ref[0:1, h * DH : (h + 1) * DH]
        q = (lin_ref[:, h * DH : (h + 1) * DH].astype(jnp.float32) * scale * gain).astype(jnp.bfloat16)
        norm = jnp.maximum(norm, row_norms(q.astype(jnp.float32)))
        q_ref[h, :, :DH] = q
        q_ref[h, :, DH:] = jnp.zeros((ROWS, DH), jnp.bfloat16)
    return jnp.max(norm)


def ones_beside(v):
    return jnp.concatenate([v, jnp.ones((ROWS, DH), jnp.bfloat16)], 1)


def bounded_tile(kv_ref, slot, base, begin_first, q_ref, acc_ref):
    kk = jnp.concatenate([kv_ref[slot - base, :ROWS]] * 2, 1)
    key = block_of(slot) * ROWS + lax.broadcasted_iota(jnp.int32, (ROWS, 256), 0)
    inside = (key >= begin_first).astype(jnp.float32).astype(jnp.bfloat16)
    v = ones_beside(kv_ref[slot - base, ROWS:]) * inside
    for h in range(0, HEADS, 2):
        q = q_ref[h : h + 2].reshape(2 * ROWS, 256)
        p = jnp.exp2(dot(q, kk, NT)).astype(jnp.bfloat16)
        acc_ref[h : h + 2] += dot(p, v).reshape(2, ROWS, 256)


def make_mask(mask_ref, block, first, begin):
    row = lax.broadcasted_iota(jnp.int32, (ROWS, ROWS), 0)
    key = block * ROWS + lax.broadcasted_iota(jnp.int32, (ROWS, ROWS), 1)
    mask_ref[...] = jnp.where((key >= begin) & (key <= first + row), 0.0, FAR)


def any_tile(kv_ref, slot, base, first, begin, q_ref, acc_ref, mask_ref, top_ref):
    make_mask(mask_ref, block_of(slot), first, begin)
    kk = jnp.concatenate([kv_ref[slot - base, :ROWS]] * 2, 1)
    v = ones_beside(kv_ref[slot - base, ROWS:])

    def head(h, carry):
        s = jnp.maximum(dot(q_ref[h], kk, NT) * FACTOR + mask_ref[...], FAR)
        old = top_ref[h]
        new = jnp.maximum(old, jnp.max(s, 1, keepdims=True))
        p = jnp.exp2(s - jnp.concatenate([new] * 4, 1)).astype(jnp.bfloat16)
        fade = jnp.exp2(old - new)
        acc_ref[h] = acc_ref[h] * jnp.concatenate([fade] * 2, 1) + dot(p, v)
        top_ref[h] = new
        return carry

    lax.fori_loop(0, HEADS, head, 0)


def in_softmax_phase():
    return lax.axis_index("phase") == 1


def rows_of():
    z, x = here()
    first = (z * 4 + x) * ROWS
    return first, first + lax.broadcasted_iota(jnp.int32, (ROWS, 1), 0)


def open_kernel(n_ref, lin_ref, total_ref, gain_ref, near_hbm, far_hbm, q_ref, acc_ref, top_hbm, stat_ref, kv_ref, mask_ref, top_ref, sems):
    @pl.when(in_softmax_phase())
    def _():
        n1, n2 = n_ref[0], n_ref[1]
        first, positions = rows_of()
        copies = [pltpu.make_async_copy(src, kv_ref.at[i], sems.at[i]) for i, src in enumerate((near_hbm, far_hbm))]
        for copy in copies:
            copy.start()
        q_most = make_queries(lin_ref, total_ref, gain_ref, q_ref)
        acc_ref[...] = jnp.zeros_like(acc_ref)
        for copy in copies:
            copy.wait()
        safe = q_most * key_norms(kv_ref, (1, 3), 1, n1, n2) < (SAFE / FACTOR) ** 2
        stat_ref[0] = q_most
        stat_ref[1] = jnp.where(safe, 1.0, 0.0)

        @pl.when(safe)
        def _():
            for h in range(HEADS):
                hi, lo = split(q_ref[h, :, :DH].astype(jnp.float32) * FACTOR)
                q_ref[h, :, :DH] = hi
                q_ref[h, :, DH:] = lo
            begin_first = start_of(first, n1, n2)

            def step(slot, carry):
                pl.when(active(slot, n1, n2))(lambda: bounded_tile(kv_ref, slot, 1, begin_first, q_ref, acc_ref))
                return carry

            lax.fori_loop(1, 3, step, 0)

        @pl.when(jnp.logical_not(safe))
        def _():
            top_ref[...] = jnp.full(top_ref.shape, FAR, jnp.float32)
            begin = start_of(positions, n1, n2)

            def step(slot, carry):
                pl.when(active(slot, n1, n2))(
                    lambda: any_tile(kv_ref, slot, 1, first, begin, q_ref, acc_ref, mask_ref, top_ref)
                )
                return carry

            lax.fori_loop(1, 3, step, 0)
            copy = pltpu.make_async_copy(top_ref, top_hbm, sems.at[0])
            copy.start()
            copy.wait()


def close_kernel(n_ref, stat_ref, lin_ref, total_ref, gain_ref, q_ref, part_ref, top_hbm, *refs):
    kv_hbm, (out_hbm, kv_ref, raw_ref, acc_ref, mask_ref, top_ref, out_ref, kv_sems, out_sems) = refs[:4], refs[4:]

    @pl.when(jnp.logical_not(in_softmax_phase()))
    def _():
        copy = pltpu.make_async_copy(lin_ref, out_hbm, out_sems.at[0])
        copy.start()
        copy.wait()

    @pl.when(in_softmax_phase())
    def _():
        close(
            n_ref, stat_ref, lin_ref, total_ref, gain_ref, q_ref, part_ref, top_hbm, kv_hbm,
            out_hbm, kv_ref, raw_ref, acc_ref, mask_ref, top_ref, out_ref, kv_sems, out_sems,
        )


def close(
    n_ref, stat_ref, lin_ref, total_ref, gain_ref, q_ref, part_ref, top_hbm, kv_hbm,
    out_hbm, kv_ref, raw_ref, acc_ref, mask_ref, top_ref, out_ref, kv_sems, out_sems,
):
    n1, n2 = n_ref[0], n_ref[1]
    first, positions = rows_of()
    begin_first = start_of(first, n1, n2)
    begin = start_of(positions, n1, n2)
    base = 2

    def fetch(slot):
        if slot == 0:
            return pltpu.make_async_copy(kv_hbm[0], kv_ref.at[0], kv_sems.at[0])
        src = kv_hbm[(slot - 1) // 2].at[pl.ds((slot - 1) % 2 * 2 * ROWS, 2 * ROWS)]
        return pltpu.make_async_copy(src, kv_ref.at[slot - base], kv_sems.at[slot - base])

    here_slots = (0,) + tuple(range(3, SLOTS))
    for slot in here_slots:
        pl.when(active(slot, n1, n2))(lambda: fetch(slot).start())
    acc_ref[...] = part_ref[...]
    for slot in here_slots:
        pl.when(active(slot, n1, n2))(lambda: fetch(slot).wait())

    k_most = jnp.maximum(key_norms(kv_ref, (3, SLOTS), base, n1, n2), key_norms(kv_ref, (0, 1), 0, n1, n2))
    opened_safe = stat_ref[1] > 0.5
    safe = opened_safe & (stat_ref[0] * k_most < (SAFE / FACTOR) ** 2)

    @pl.when(safe)
    def _():
        def step(slot, carry):
            pl.when(active(slot, n1, n2))(lambda: bounded_tile(kv_ref, slot, base, begin_first, q_ref, acc_ref))
            return carry

        lax.fori_loop(3, SLOTS, step, 0)

        make_mask(mask_ref, block_of(0), first, begin)
        kk = jnp.concatenate([kv_ref[0, :ROWS]] * 2, 1)
        v = ones_beside(kv_ref[0, ROWS:])
        keep = (begin < first).astype(jnp.float32)
        half = ROWS // 2
        for h in range(HEADS):
            for r in range(2):
                rows, span = slice(r * half, (r + 1) * half), (r + 1) * half
                s = dot(q_ref[h, rows, :], kk[:span], NT) + mask_ref[rows, :span]
                p = jnp.exp2(s).astype(jnp.bfloat16)
                acc_ref[h, rows, :] = acc_ref[h, rows, :] * keep[rows] + dot(p, v[:span])

    @pl.when(jnp.logical_not(safe))
    def _():
        make_queries(lin_ref, total_ref, gain_ref, raw_ref)

        @pl.when(jnp.logical_not(opened_safe))
        def _():
            copy = pltpu.make_async_copy(top_hbm, top_ref, kv_sems.at[0])
            copy.start()
            copy.wait()

        @pl.when(opened_safe)
        def _():
            opened = active(1, n1, n2) | active(2, n1, n2)
            keep = (positions - first < jnp.where(opened, ROWS, 0)) & (begin == begin_first)
            for h in range(HEADS):
                top_ref[h] = jnp.where(jnp.broadcast_to(keep, (ROWS, DH)), 0.0, FAR)
                acc_ref[h] = jnp.where(jnp.broadcast_to(keep, (ROWS, 256)), acc_ref[h], 0.0)

        def step(slot, carry):
            pl.when(active(slot, n1, n2))(
                lambda: any_tile(kv_ref, slot, base, first, begin, raw_ref, acc_ref, mask_ref, top_ref)
            )
            return carry

        lax.fori_loop(3, SLOTS, step, 0)
        any_tile(kv_ref, 0, 0, first, begin, raw_ref, acc_ref, mask_ref, top_ref)

    copies = []
    for h in range(HEADS):
        lanes = slice(h * DH, (h + 1) * DH)
        out_ref[:, lanes] = (acc_ref[h, :, :DH] / acc_ref[h, :, DH:]).astype(jnp.bfloat16)
        copies.append(pltpu.make_async_copy(out_ref.at[:, lanes], out_hbm.at[:, lanes], out_sems.at[h]))
        copies[-1].start()
    for copy in copies:
        copy.wait()


VMEM = pl.BlockSpec(memory_space=pltpu.VMEM)
SMEM = pl.BlockSpec(memory_space=pltpu.SMEM)
ANY = pl.BlockSpec(memory_space=pl.ANY)


def call(kernel, outs, out_specs, args, in_specs, scratch, flops, limit):
    return pl.pallas_call(
        kernel,
        out_shape=tuple(outs),
        in_specs=in_specs,
        out_specs=tuple(out_specs),
        scratch_shapes=scratch,
        compiler_params=pltpu.CompilerParams(vmem_limit_bytes=limit << 20),
        cost_estimate=pl.CostEstimate(flops=flops, bytes_accessed=0, transcendentals=0),
    )(*args)


def shape(dims, dtype=jnp.float32):
    return jax.ShapeDtypeStruct(dims, dtype)


def row_sum(counts, parts):
    return call(row_sum_kernel, [shape((QUARTER, DH))], [VMEM], (counts, parts), [SMEM, VMEM], [], 0, 8)[0]


def priors_of(counts, parts, near, far):
    return call(
        prior_kernel,
        [shape((QUARTER, DH))] * 4,
        [VMEM] * 4,
        (counts, parts, near, far),
        [SMEM] + [VMEM] * 3,
        [],
        1000000000,
        8,
    )


def pack(own_kv, near_kv, far_kv):
    return call(
        pack_kernel,
        [shape((4 * ROWS, DH), own_kv.dtype)] * 3,
        [ANY] * 3,
        (own_kv, near_kv, far_kv),
        [ANY] * 3,
        [pltpu.SemaphoreType.DMA((6,))],
        5000000000,
        4,
    )


def states(doc_ids, key_feats, values, keys_soft, values_soft):
    bf16 = jnp.bfloat16
    return call(
        states_kernel,
        [shape((HEADS * FEATS, DH)), shape((2 * ROWS, DH), bf16), shape((8,), jnp.int32)],
        [VMEM] * 2 + [SMEM],
        (doc_ids.reshape(-1, DH), key_feats, values, keys_soft, values_soft),
        [ANY] * 5,
        [
            pltpu.VMEM((doc_ids.shape[0] // DH, DH), jnp.int32),
            pltpu.VMEM((ROWS, DH), bf16),
            pltpu.VMEM((ROWS, WIDE), bf16),
            pltpu.SemaphoreType.DMA((5,)),
        ],
        0,
        60,
    )


def local_part(counts, query_feats, key_feats, values):
    bf16 = jnp.bfloat16
    return call(
        local_kernel,
        [shape((ROWS, WIDE)), shape((ROWS, DH)), shape((ROWS, HEADS * 256), bf16), shape((ROWS, HEADS * 256), bf16)],
        [VMEM] * 4,
        (counts, query_feats, key_feats, values),
        [SMEM] + [VMEM] * 3,
        [pltpu.VMEM((ROWS, ROWS), jnp.float32)],
        0,
        24,
    )


def finish(counts, feats_hi, feats_lo, num, den, parts):
    return call(
        finish_kernel,
        [shape((ROWS, WIDE), jnp.bfloat16), shape((8, ROWS))],
        [VMEM] * 2,
        (counts, feats_hi, feats_lo, num, den) + tuple(parts),
        [SMEM] + [VMEM] * 8,
        [pltpu.VMEM((HEADS * FEATS, DH), jnp.float32)],
        8000000000,
        20,
    )


def soft_open(counts, linear_out, total, gain, near_kv, far_kv):
    bf16 = jnp.bfloat16
    return call(
        open_kernel,
        [shape((HEADS, ROWS, 256), bf16), shape((HEADS, ROWS, 256)), shape((HEADS, ROWS, DH)), shape((8,))],
        [VMEM, VMEM, ANY, SMEM],
        (counts, linear_out, total, gain, near_kv, far_kv),
        [SMEM] + [VMEM] * 3 + [ANY] * 2,
        [
            pltpu.VMEM((2, 2 * ROWS, DH), bf16),
            pltpu.VMEM((ROWS, ROWS), jnp.float32),
            pltpu.VMEM((HEADS, ROWS, DH), jnp.float32),
            pltpu.SemaphoreType.DMA((2,)),
        ],
        0,
        28,
    )


def soft_close(counts, stat, linear_out, total, gain, queries, part, top, pieces):
    bf16 = jnp.bfloat16
    return call(
        close_kernel,
        [shape((ROWS, WIDE), bf16)],
        [ANY],
        (counts, stat, linear_out, total, gain, queries, part, top) + tuple(pieces),
        [SMEM] * 2 + [VMEM] * 5 + [ANY] * 5,
        [
            pltpu.VMEM((SLOTS - 2, 2 * ROWS, DH), bf16),
            pltpu.VMEM((HEADS, ROWS, 256), bf16),
            pltpu.VMEM((HEADS, ROWS, 256), jnp.float32),
            pltpu.VMEM((ROWS, ROWS), jnp.float32),
            pltpu.VMEM((HEADS, ROWS, DH), jnp.float32),
            pltpu.VMEM((ROWS, WIDE), bf16),
            pltpu.SemaphoreType.DMA((SLOTS - 2,)),
            pltpu.SemaphoreType.DMA((HEADS,)),
        ],
        0,
        32,
    )[0]


def shift(x, axis, by):
    size = lax.axis_size(axis)
    return lax.ppermute(x, axis, [(i, (i + by) % size) for i in range(size)])


def after(x, *others):
    return lax.optimization_barrier((x,) + others)[0]


def local(query_feats, key_feats, values, keys_soft, values_soft, norm_gain, doc_ids):
    zs = lax.axis_size("z")
    state, own_kv, counts = states(doc_ids, key_feats, values, keys_soft, values_soft)

    parts = lax.all_to_all(state, "x", 0, 0, tiled=True)

    near_kv = lax.ppermute(own_kv, ("phase", "z"), [(zs + i, zs + i + 1) for i in range(zs - 1)])
    far_kv = lax.ppermute(own_kv, ("phase", "z"), [(i, zs + i + 2) for i in range(zs - 2)])

    local_sums = local_part(counts, query_feats, key_feats, values)
    total = row_sum(counts, parts)
    near = lax.ppermute(total, "z", [(i, i + 1) for i in range(zs - 1)])
    far = lax.ppermute(
        total,
        ("phase", "z"),
        [((1 - p) * zs + i, p * zs + i + 2) for p in range(2) for i in range(zs - 2)],
    )

    messages = lax.optimization_barrier((total,) + tuple(pack(own_kv, near_kv, far_kv)))[1:]
    others = [
        lax.ppermute(message, ("phase", "x"), [(4 + i, 4 + (i + s) % 4) for i in range(4)])
        for s, message in zip((1, 2, 3), messages)
    ]

    near = after(near, *local_sums)
    priors = priors_of(counts, parts, near, far)
    arrived = [priors[0]] + [shift(priors[s], "x", s) for s in (1, 2, 3)]
    num, den, feats_hi, feats_lo = local_sums
    linear_out, squares = finish(counts, feats_hi, feats_lo, num, den, arrived)
    total = lax.all_to_all(squares, ("y", "core"), 0, 0, tiled=True)
    gain = norm_gain[None]
    queries, part, top, stat = soft_open(counts, linear_out, total, gain, near_kv, far_kv)
    return soft_close(counts, stat, linear_out, total, gain, queries, part, top, [own_kv] + others)[None]


def solution(mesh):
    fine = Mesh(mesh.devices.reshape(2, 4, 4, 4, 2), ("phase", "z", "x", "y", "core"))
    seq, head = ("z", "x"), ("y", "core")
    return jax.shard_map(
        local,
        mesh=fine,
        in_specs=(
            P(seq, head),
            P(seq, head),
            P(seq, head),
            P(seq, head),
            P(seq, head),
            P(head),
            P(),
        ),
        out_specs=P("phase", seq, head),
        check_vma=False,
    )
```

```python
import math

import jax
import jax.numpy as jnp
from jax import lax
from jax.experimental import pallas as pl
from jax.experimental.pallas import tpu as pltpu
from jax.sharding import Mesh, PartitionSpec as P

DH = 128
F = 16
ROWS = 512
HEADS = 8
WIDE = HEADS * DH
ALL_WIDE = 64 * DH
USED = (F + 1) * (F + 2) // 2
FEATS = 160
QUARTER = HEADS * FEATS // 4
SLOTS = 9
DOC_ROW = USED + 2
LOG2E = math.log2(math.e)
FACTOR = LOG2E / math.sqrt(DH)
SAFE = 110.0
FAR = -1e30

NN = (((1,), (0,)), ((), ()))
NT = (((1,), (1,)), ((), ()))


def dot(a, b, dims=NN):
    return lax.dot_general(a, b, dims, preferred_element_type=jnp.float32)


def split(x):
    hi = x.astype(jnp.bfloat16)
    lo = (x - hi.astype(jnp.float32)).astype(jnp.bfloat16)
    return hi, lo


def doc_of(position, n1, n2):
    return (position >= n1).astype(jnp.int32) + (position >= n2).astype(jnp.int32)


def start_of(position, n1, n2):
    return jnp.where(position >= n2, n2, jnp.where(position >= n1, n1, 0))


def pair_of(e):
    gap = jnp.zeros_like(e)
    for k in range(1, F // 2 + 1):
        gap = gap + (e >= k * (F + 1)).astype(jnp.int32)
    m = e - gap * (F + 1)
    n = m + gap
    n = jnp.where(n > F, n - (F + 1), n)
    times = jnp.where((gap == 0) & (m < F), 1.0, 2.0)
    times = jnp.where(e < USED, times, 0.0)
    return m, n, times


def here():
    return lax.axis_index("z"), lax.axis_index("x")


def row_block(x, s):
    return lax.rem(x - s + 4, 4)


def same(a, b):
    return (a == b).astype(jnp.float32)


def doc_row(ref):
    return ref[DOC_ROW : DOC_ROW + 1, :]


def row_sum_kernel(p0_ref, p1_ref, p2_ref, p3_ref, out_ref):
    parts = (p0_ref, p1_ref, p2_ref, p3_ref)
    end = doc_row(p0_ref)
    for part in parts[1:]:
        end = jnp.maximum(end, doc_row(part))
    total = jnp.zeros((QUARTER, DH), jnp.float32)
    for part in parts:
        total = total + same(doc_row(part), end) * part[...]
    out_ref[...] = total
    out_ref[DOC_ROW : DOC_ROW + 1, :] = end


def prior_kernel(p0_ref, p1_ref, p2_ref, p3_ref, near_ref, far_ref, *outs):
    z, x = here()
    parts = (p0_ref, p1_ref, p2_ref, p3_ref)
    before = doc_row(near_ref)
    incoming = near_ref[...] + same(doc_row(far_ref), before) * far_ref[...]
    for t, out in enumerate(outs):
        target = lax.rem(x + t, 4)
        doc = before
        for s, part in enumerate(parts):
            doc = jnp.where(row_block(x, s) == target - 1, doc_row(part), doc)
        prior = same(before, doc) * incoming
        for s, part in enumerate(parts):
            use = jnp.where(row_block(x, s) < target, same(doc_row(part), doc), 0.0)
            prior = prior + use * part[...]
        out[...] = prior


def stash_kernel(src_hbm, out_ref, sem):
    copy = pltpu.make_async_copy(src_hbm, out_ref, sem)
    copy.start()
    copy.wait()


def pack_kernel(own_hbm, near_hbm, far_hbm, o1_hbm, o2_hbm, o3_hbm, sems):
    z, x = here()
    upper, lower = pl.ds(0, 2 * ROWS), pl.ds(2 * ROWS, 2 * ROWS)
    for s, out in enumerate((o1_hbm, o2_hbm, o3_hbm)):
        later = lax.rem(x + s + 1, 4) > x
        pltpu.make_async_copy(near_hbm, out.at[upper], sems.at[s]).start()
        pl.when(later)(lambda: pltpu.make_async_copy(own_hbm, out.at[lower], sems.at[3 + s]).start())
        pl.when(jnp.logical_not(later))(lambda: pltpu.make_async_copy(far_hbm, out.at[lower], sems.at[3 + s]).start())
    for s, out in enumerate((o1_hbm, o2_hbm, o3_hbm)):
        pltpu.make_async_copy(near_hbm, out.at[upper], sems.at[s]).wait()
        pltpu.make_async_copy(own_hbm, out.at[lower], sems.at[3 + s]).wait()


def states_kernel(doc_hbm, kf_hbm, v_hbm, k_hbm, vs_hbm, c0_ref, c1_ref, c2_ref, c3_ref, kv_ref, n_ref, state_ref, doc_ref, kf_ref, v_ref, sems):
    pairs = [(doc_hbm, doc_ref), (kf_hbm, kf_ref), (v_hbm, v_ref), (k_hbm, kv_ref.at[:ROWS]), (vs_hbm, kv_ref.at[ROWS:])]
    copies = [pltpu.make_async_copy(src, dst, sems.at[i]) for i, (src, dst) in enumerate(pairs)]
    for copy in copies:
        copy.start()
    z, x = here()
    first = (z * 4 + x) * ROWS
    m, n, times = pair_of(lax.broadcasted_iota(jnp.int32, (FEATS, 2 * F), 0))
    col = lax.broadcasted_iota(jnp.int32, (FEATS, 2 * F), 1)
    e1 = ((col == m) & (times > 0)).astype(jnp.float32).astype(jnp.bfloat16)
    e2 = ((col == n) & (times > 0)).astype(jnp.float32).astype(jnp.bfloat16)
    lane = lax.broadcasted_iota(jnp.int32, (ROWS, DH), 1)
    norms = jnp.zeros((FEATS, DH), jnp.float32)
    copies[0].wait()
    n1 = jnp.sum((doc_ref[...] < 1).astype(jnp.int32))
    n2 = jnp.sum((doc_ref[...] < 2).astype(jnp.int32))
    n_ref[0] = n1
    n_ref[1] = n2
    pos = first + lax.broadcasted_iota(jnp.int32, (F, ROWS), 1)
    sel = (doc_of(pos, n1, n2) == doc_of(first + ROWS - 1, n1, n2)).astype(jnp.float32)
    copies[1].wait()
    kt = kf_ref[...].astype(jnp.float32).T
    copies[2].wait()
    for h in range(HEADS):
        rows = jnp.concatenate([kt[h * F : (h + 1) * F] * sel, sel], 0).astype(jnp.bfloat16)
        hi, lo = split(dot(e1, rows) * dot(e2, rows))
        unit = (lane == h).astype(jnp.bfloat16)
        rhs = jnp.concatenate([v_ref[:, h * DH : (h + 1) * DH], unit], 1)
        res = dot(hi, rhs) + dot(lo, rhs)
        state_ref[h * FEATS : (h + 1) * FEATS, :] = res[:, :DH]
        norms = norms + res[:, DH:]
    across = norms.T
    for h in range(HEADS):
        base = h * FEATS + USED
        state_ref[base : base + 1, :] = across[h : h + 1, :DH]
        state_ref[base + 1 : base + 2, : FEATS - DH] = across[h : h + 1, DH:]
        last = doc_of(first + ROWS - 1, n1, n2).astype(jnp.float32)
        state_ref[base + 2 : base + 3, :] = jnp.full((1, DH), last, jnp.float32)
    for s, out in enumerate((c0_ref, c1_ref, c2_ref, c3_ref)):
        chunk = lax.rem(x + s, 4)
        out[...] = state_ref[pl.ds(pl.multiple_of(chunk * QUARTER, QUARTER), QUARTER), :]
    copies[3].wait()
    copies[4].wait()


def local_kernel(n_ref, qf_ref, kf_ref, v_ref, num_ref, den_ref, hi_ref, lo_ref, mask_ref):
    n1, n2 = n_ref[0], n_ref[1]
    z, x = here()
    first = (z * 4 + x) * ROWS
    row = lax.broadcasted_iota(jnp.int32, (ROWS, ROWS), 0)
    col = lax.broadcasted_iota(jnp.int32, (ROWS, ROWS), 1)
    begin = start_of(first + lax.broadcasted_iota(jnp.int32, (ROWS, 1), 0), n1, n2) - first
    mask_ref[...] = ((col <= row) & (col >= begin)).astype(jnp.float32)
    lane = lax.broadcasted_iota(jnp.int32, (ROWS, DH), 1)
    one = (lane == 0).astype(jnp.bfloat16)
    kf = jnp.concatenate([kf_ref[...], one], 1)
    half = ROWS // 2
    dens = [jnp.zeros((half, DH), jnp.float32) for _ in range(2)]
    for h in range(HEADS):
        qh = jnp.where(lane // F == h, qf_ref[...], jnp.zeros((), jnp.bfloat16))
        qh = jnp.concatenate([qh, one], 1)
        unit = (lane == h).astype(jnp.bfloat16)
        rhs = jnp.concatenate([v_ref[:, h * DH : (h + 1) * DH], unit], 1)
        for r in range(2):
            span = (r + 1) * half
            s = dot(qh[r * half : (r + 1) * half], kf[:span], NT)
            w = (s * s + 1.0) * mask_ref[r * half : (r + 1) * half, :span]
            hi, lo = split(w)
            res = dot(hi, rhs[:span]) + dot(lo, rhs[:span])
            num_ref[r * half : (r + 1) * half, h * DH : (h + 1) * DH] = res[:, :DH]
            dens[r] = dens[r] + res[:, DH:]
    for r in range(2):
        den_ref[r * half : (r + 1) * half, :] = dens[r]
    m, n, times = pair_of(lax.broadcasted_iota(jnp.int32, (DH, 256), 1))
    lane_row = lax.broadcasted_iota(jnp.int32, (DH, 256), 0)
    m1, n1_, times1 = pair_of(lax.broadcasted_iota(jnp.int32, (1, 256), 1))
    ones_a = jnp.where(m1 == F, times1, 0.0)
    ones_b = jnp.where((n1_ == F) & (times1 > 0), 1.0, 0.0)
    once = (times > 0).astype(jnp.float32)
    q = qf_ref[...]
    for h in range(HEADS):
        e1 = jnp.where((lane_row == m + h * F) & (m < F), times, 0.0).astype(jnp.bfloat16)
        e2 = jnp.where((lane_row == n + h * F) & (n < F), once, 0.0).astype(jnp.bfloat16)
        hi, lo = split((dot(q, e1) + ones_a) * (dot(q, e2) + ones_b))
        hi_ref[:, h * 256 : (h + 1) * 256] = hi
        lo_ref[:, h * 256 : (h + 1) * 256] = lo


def finish_kernel(n_ref, hi_ref, lo_ref, num_ref, den_ref, p0_ref, p1_ref, p2_ref, p3_ref, out_ref, sq_ref, prior_ref):
    n1, n2 = n_ref[0], n_ref[1]
    z, x = here()
    first = (z * 4 + x) * ROWS
    pos = first + lax.broadcasted_iota(jnp.int32, (ROWS, 1), 0)
    usable = ((doc_of(pos, n1, n2) == doc_of(first - 1, n1, n2)) & (first > 0)).astype(jnp.float32)
    for s, part in enumerate((p0_ref, p1_ref, p2_ref, p3_ref)):
        chunk = lax.rem(x - s + 4, 4)
        prior_ref[pl.ds(pl.multiple_of(chunk * QUARTER, QUARTER), QUARTER), :] = part[...]
    spare = [jnp.zeros((DH - HEADS, DH), jnp.float32)]
    sums = [[prior_ref[h * FEATS + USED + i : h * FEATS + USED + i + 1, :] for h in range(HEADS)] for i in range(2)]
    norm = jnp.concatenate([jnp.concatenate(rows + spare, 0).T for rows in sums], 0)[:FEATS]
    norm_hi, norm_lo = split(norm)
    squares = jnp.zeros((ROWS, DH), jnp.float32)
    for h in range(HEADS):
        hi = hi_ref[:, h * 256 : h * 256 + FEATS]
        lo = lo_ref[:, h * 256 : h * 256 + FEATS]
        s_hi, s_lo = split(prior_ref[h * FEATS : (h + 1) * FEATS, :])
        r_hi = jnp.concatenate([s_hi, norm_hi], 1)
        r_lo = jnp.concatenate([s_lo, norm_lo], 1)
        res = (dot(hi, r_hi) + (dot(lo, r_hi) + dot(hi, r_lo))) * usable
        num = num_ref[:, h * DH : (h + 1) * DH] + res[:, :DH]
        den = den_ref[:, h : h + 1] + res[:, DH + h : DH + h + 1]
        out = (num / den).astype(jnp.bfloat16)
        out_ref[:, h * DH : (h + 1) * DH] = out
        wide = out.astype(jnp.float32)
        squares = squares + wide * wide
    sq_ref[...] = jnp.sum(squares.T, 0, keepdims=True)


def block_of(slot):
    z, x = here()
    src = lax.rem(x + 4 - lax.div(slot - 1, 2), 4)
    behind = jnp.where(lax.rem(slot, 2) == 1, 1, jnp.where(src < x, 0, 2))
    return jnp.where(slot < 3, z * 4 + x - 4 * slot, (z - behind) * 4 + src)


def active(slot, n1, n2):
    z, x = here()
    own = z * 4 + x
    low = start_of(own * ROWS, n1, n2) // ROWS
    return (block_of(slot) >= low) & (block_of(slot) < own) | (slot == 0)


def key_norms(kv_ref, slots, base, n1, n2):
    def one(slot, best):
        k = kv_ref[slot - base, :ROWS].astype(jnp.float32)
        norm = jnp.sum(k * k, 1, keepdims=True)
        return jnp.where(active(slot, n1, n2), jnp.maximum(best, norm), best)

    return jnp.max(lax.fori_loop(*slots, one, jnp.zeros((ROWS, 1), jnp.float32)))


def gauge_kernel(n_ref, lin_ref, gain_ref, near_ref, far_ref, rows_ref, stat_ref):
    most = jnp.zeros((ROWS, 1), jnp.float32)
    for h in range(HEADS):
        lanes = slice(h * DH, (h + 1) * DH)
        q = lin_ref[:, lanes].astype(jnp.float32) * gain_ref[0:1, lanes]
        most = jnp.maximum(most, jnp.sum(q * q, 1, keepdims=True))
    rows_ref[...] = jnp.broadcast_to(most, (ROWS, DH)).T[:8]
    stat_ref[0] = 0.0
    for slot, kv_ref in ((1, near_ref), (2, far_ref)):
        k = kv_ref[:ROWS].astype(jnp.float32)
        norm = jnp.max(jnp.sum(k * k, 1, keepdims=True))
        stat_ref[0] = jnp.where(active(slot, n_ref[0], n_ref[1]), jnp.maximum(stat_ref[0], norm), stat_ref[0])


def scale_of(total_ref):
    return lax.rsqrt(total_ref[...] / ALL_WIDE + 1e-06)


def make_queries(lin_ref, total_ref, gain_ref, q_ref, double):
    scale = jnp.broadcast_to(scale_of(total_ref), (DH, ROWS)).T
    for h in range(HEADS):
        lanes = slice(h * DH, (h + 1) * DH)
        q = (lin_ref[:, lanes].astype(jnp.float32) * scale * gain_ref[0:1, lanes]).astype(jnp.bfloat16)
        lo = jnp.zeros((ROWS, DH), jnp.bfloat16)
        if double:
            q, lo = split(q.astype(jnp.float32) * FACTOR)
        q_ref[h, :, :DH] = q
        q_ref[h, :, DH:] = lo


def ones_beside(v):
    return jnp.concatenate([v, jnp.ones((ROWS, DH), jnp.bfloat16)], 1)


def bounded_tile(kv_ref, slot, base, begin_first, q_ref, acc_ref):
    kk = jnp.concatenate([kv_ref[slot - base, :ROWS]] * 2, 1)
    key = block_of(slot) * ROWS + lax.broadcasted_iota(jnp.int32, (ROWS, 256), 0)
    inside = (key >= begin_first).astype(jnp.float32).astype(jnp.bfloat16)
    v = ones_beside(kv_ref[slot - base, ROWS:]) * inside
    for h in range(HEADS):
        p = jnp.exp2(dot(q_ref[h], kk, NT)).astype(jnp.bfloat16)
        acc_ref[h] += dot(p, v)


def make_mask(mask_ref, block, first, begin):
    row = lax.broadcasted_iota(jnp.int32, (ROWS, ROWS), 0)
    key = block * ROWS + lax.broadcasted_iota(jnp.int32, (ROWS, ROWS), 1)
    mask_ref[...] = jnp.where((key >= begin) & (key <= first + row), 0.0, FAR)


def any_tile(kv_ref, slot, base, first, begin, q_ref, acc_ref, mask_ref, top_ref):
    make_mask(mask_ref, block_of(slot), first, begin)
    kk = jnp.concatenate([kv_ref[slot - base, :ROWS]] * 2, 1)
    v = ones_beside(kv_ref[slot - base, ROWS:])

    def head(h, carry):
        s = jnp.maximum(dot(q_ref[h], kk, NT) * FACTOR + mask_ref[...], FAR)
        old = top_ref[h]
        new = jnp.maximum(old, jnp.max(s, 1, keepdims=True))
        p = jnp.exp2(s - jnp.concatenate([new] * 4, 1)).astype(jnp.bfloat16)
        fade = jnp.exp2(old - new)
        acc_ref[h] = acc_ref[h] * jnp.concatenate([fade] * 2, 1) + dot(p, v)
        top_ref[h] = new
        return carry

    lax.fori_loop(0, HEADS, head, 0)


def in_softmax_phase():
    return lax.axis_index("phase") == 1


def rows_of():
    z, x = here()
    first = (z * 4 + x) * ROWS
    return first, first + lax.broadcasted_iota(jnp.int32, (ROWS, 1), 0)


def open_kernel(n_ref, gauge_ref, lin_ref, total_ref, gain_ref, rows_ref, near_hbm, far_hbm, q_ref, acc_ref, top_hbm, stat_ref, kv_ref, mask_ref, top_ref, sems):
    @pl.when(in_softmax_phase())
    def _():
        n1, n2 = n_ref[0], n_ref[1]
        first, positions = rows_of()
        copies = [pltpu.make_async_copy(src, kv_ref.at[i], sems.at[i]) for i, src in enumerate((near_hbm, far_hbm))]
        for copy in copies:
            copy.start()
        scale = scale_of(total_ref)
        q_most = 1.02 * jnp.max(scale * scale * rows_ref[0:1, :])
        safe = q_most * gauge_ref[0] < (SAFE / FACTOR) ** 2
        stat_ref[0] = q_most
        stat_ref[1] = jnp.where(safe, 1.0, 0.0)
        acc_ref[...] = jnp.zeros_like(acc_ref)

        @pl.when(safe)
        def _():
            make_queries(lin_ref, total_ref, gain_ref, q_ref, True)
            for copy in copies:
                copy.wait()
            begin_first = start_of(first, n1, n2)

            def step(slot, carry):
                pl.when(active(slot, n1, n2))(lambda: bounded_tile(kv_ref, slot, 1, begin_first, q_ref, acc_ref))
                return carry

            lax.fori_loop(1, 3, step, 0)

        @pl.when(jnp.logical_not(safe))
        def _():
            make_queries(lin_ref, total_ref, gain_ref, q_ref, False)
            top_ref[...] = jnp.full(top_ref.shape, FAR, jnp.float32)
            begin = start_of(positions, n1, n2)
            for copy in copies:
                copy.wait()

            def step(slot, carry):
                pl.when(active(slot, n1, n2))(
                    lambda: any_tile(kv_ref, slot, 1, first, begin, q_ref, acc_ref, mask_ref, top_ref)
                )
                return carry

            lax.fori_loop(1, 3, step, 0)
            copy = pltpu.make_async_copy(top_ref, top_hbm, sems.at[0])
            copy.start()
            copy.wait()


def close_kernel(n_ref, stat_ref, lin_ref, total_ref, gain_ref, q_ref, part_ref, top_hbm, *refs):
    kv_hbm, (out_hbm, kv_ref, raw_ref, acc_ref, mask_ref, top_ref, out_ref, kv_sems, out_sems) = refs[:4], refs[4:]

    @pl.when(jnp.logical_not(in_softmax_phase()))
    def _():
        copy = pltpu.make_async_copy(lin_ref, out_hbm, out_sems.at[0])
        copy.start()
        copy.wait()

    @pl.when(in_softmax_phase())
    def _():
        close(
            n_ref, stat_ref, lin_ref, total_ref, gain_ref, q_ref, part_ref, top_hbm, kv_hbm,
            out_hbm, kv_ref, raw_ref, acc_ref, mask_ref, top_ref, out_ref, kv_sems, out_sems,
        )


def close(
    n_ref, stat_ref, lin_ref, total_ref, gain_ref, q_ref, part_ref, top_hbm, kv_hbm,
    out_hbm, kv_ref, raw_ref, acc_ref, mask_ref, top_ref, out_ref, kv_sems, out_sems,
):
    n1, n2 = n_ref[0], n_ref[1]
    first, positions = rows_of()
    begin_first = start_of(first, n1, n2)
    begin = start_of(positions, n1, n2)
    base = 2

    def fetch(slot):
        if slot == 0:
            return pltpu.make_async_copy(kv_hbm[0], kv_ref.at[0], kv_sems.at[0])
        src = kv_hbm[(slot - 1) // 2].at[pl.ds((slot - 1) % 2 * 2 * ROWS, 2 * ROWS)]
        return pltpu.make_async_copy(src, kv_ref.at[slot - base], kv_sems.at[slot - base])

    here_slots = (0,) + tuple(range(3, SLOTS))
    for slot in here_slots:
        pl.when(active(slot, n1, n2))(lambda: fetch(slot).start())
    acc_ref[...] = part_ref[...]
    for slot in here_slots:
        pl.when(active(slot, n1, n2))(lambda: fetch(slot).wait())

    k_most = jnp.maximum(key_norms(kv_ref, (3, SLOTS), base, n1, n2), key_norms(kv_ref, (0, 1), 0, n1, n2))
    opened_safe = stat_ref[1] > 0.5
    safe = opened_safe & (stat_ref[0] * k_most < (SAFE / FACTOR) ** 2)

    @pl.when(safe)
    def _():
        def step(slot, carry):
            pl.when(active(slot, n1, n2))(lambda: bounded_tile(kv_ref, slot, base, begin_first, q_ref, acc_ref))
            return carry

        lax.fori_loop(3, SLOTS, step, 0)

        make_mask(mask_ref, block_of(0), first, begin)
        kk = jnp.concatenate([kv_ref[0, :ROWS]] * 2, 1)
        v = ones_beside(kv_ref[0, ROWS:])
        keep = (begin < first).astype(jnp.float32)
        half = ROWS // 2
        for h in range(HEADS):
            for r in range(2):
                rows, span = slice(r * half, (r + 1) * half), (r + 1) * half
                s = dot(q_ref[h, rows, :], kk[:span], NT) + mask_ref[rows, :span]
                p = jnp.exp2(s).astype(jnp.bfloat16)
                acc_ref[h, rows, :] = acc_ref[h, rows, :] * keep[rows] + dot(p, v[:span])

    @pl.when(jnp.logical_not(safe))
    def _():
        make_queries(lin_ref, total_ref, gain_ref, raw_ref, False)

        @pl.when(jnp.logical_not(opened_safe))
        def _():
            copy = pltpu.make_async_copy(top_hbm, top_ref, kv_sems.at[0])
            copy.start()
            copy.wait()

        @pl.when(opened_safe)
        def _():
            opened = active(1, n1, n2) | active(2, n1, n2)
            keep = (positions - first < jnp.where(opened, ROWS, 0)) & (begin == begin_first)
            for h in range(HEADS):
                top_ref[h] = jnp.where(jnp.broadcast_to(keep, (ROWS, DH)), 0.0, FAR)
                acc_ref[h] = jnp.where(jnp.broadcast_to(keep, (ROWS, 256)), acc_ref[h], 0.0)

        def step(slot, carry):
            pl.when(active(slot, n1, n2))(
                lambda: any_tile(kv_ref, slot, base, first, begin, raw_ref, acc_ref, mask_ref, top_ref)
            )
            return carry

        lax.fori_loop(3, SLOTS, step, 0)
        any_tile(kv_ref, 0, 0, first, begin, raw_ref, acc_ref, mask_ref, top_ref)

    copies = []
    for h in range(HEADS):
        lanes = slice(h * DH, (h + 1) * DH)
        out_ref[:, lanes] = (acc_ref[h, :, :DH] / acc_ref[h, :, DH:]).astype(jnp.bfloat16)
        copies.append(pltpu.make_async_copy(out_ref.at[:, lanes], out_hbm.at[:, lanes], out_sems.at[h]))
        copies[-1].start()
    for copy in copies:
        copy.wait()


VMEM = pl.BlockSpec(memory_space=pltpu.VMEM)
SMEM = pl.BlockSpec(memory_space=pltpu.SMEM)
ANY = pl.BlockSpec(memory_space=pl.ANY)


def call(kernel, outs, out_specs, args, in_specs, scratch, flops, limit):
    return pl.pallas_call(
        kernel,
        out_shape=tuple(outs),
        in_specs=in_specs,
        out_specs=tuple(out_specs),
        scratch_shapes=scratch,
        compiler_params=pltpu.CompilerParams(vmem_limit_bytes=limit << 20),
        cost_estimate=pl.CostEstimate(flops=flops, bytes_accessed=0, transcendentals=0),
    )(*args)


def shape(dims, dtype=jnp.float32):
    return jax.ShapeDtypeStruct(dims, dtype)


def stash(chunk):
    return call(stash_kernel, [shape(chunk.shape)], [VMEM], (chunk,), [ANY], [pltpu.SemaphoreType.DMA], 0, 4)[0]


def row_sum(parts):
    return call(row_sum_kernel, [shape((QUARTER, DH))], [VMEM], tuple(parts), [VMEM] * 4, [], 0, 8)[0]


def priors_of(parts, near, far):
    return call(
        prior_kernel, [shape((QUARTER, DH))] * 4, [VMEM] * 4, tuple(parts) + (near, far), [VMEM] * 6, [], 1000000000, 8
    )


def pack(own_kv, near_kv, far_kv):
    return call(
        pack_kernel,
        [shape((4 * ROWS, DH), own_kv.dtype)] * 3,
        [ANY] * 3,
        (own_kv, near_kv, far_kv),
        [ANY] * 3,
        [pltpu.SemaphoreType.DMA((6,))],
        5000000000,
        4,
    )


def states(doc_ids, key_feats, values, keys_soft, values_soft):
    bf16 = jnp.bfloat16
    return call(
        states_kernel,
        [shape((QUARTER, DH))] * 4 + [shape((2 * ROWS, DH), bf16), shape((8,), jnp.int32)],
        [VMEM] * 5 + [SMEM],
        (doc_ids.reshape(-1, DH), key_feats, values, keys_soft, values_soft),
        [ANY] * 5,
        [
            pltpu.VMEM((HEADS * FEATS, DH), jnp.float32),
            pltpu.VMEM((doc_ids.shape[0] // DH, DH), jnp.int32),
            pltpu.VMEM((ROWS, DH), bf16),
            pltpu.VMEM((ROWS, WIDE), bf16),
            pltpu.SemaphoreType.DMA((5,)),
        ],
        0,
        60,
    )


def local_part(counts, query_feats, key_feats, values):
    bf16 = jnp.bfloat16
    return call(
        local_kernel,
        [shape((ROWS, WIDE)), shape((ROWS, DH)), shape((ROWS, HEADS * 256), bf16), shape((ROWS, HEADS * 256), bf16)],
        [VMEM] * 4,
        (counts, query_feats, key_feats, values),
        [SMEM] + [VMEM] * 3,
        [pltpu.VMEM((ROWS, ROWS), jnp.float32)],
        0,
        24,
    )


def finish(counts, feats_hi, feats_lo, num, den, parts):
    return call(
        finish_kernel,
        [shape((ROWS, WIDE), jnp.bfloat16), shape((1, ROWS))],
        [VMEM] * 2,
        (counts, feats_hi, feats_lo, num, den) + tuple(parts),
        [SMEM] + [VMEM] * 8,
        [pltpu.VMEM((HEADS * FEATS, DH), jnp.float32)],
        8000000000,
        20,
    )


def gauge(counts, linear_out, gain, near_kv, far_kv):
    return call(
        gauge_kernel,
        [shape((8, ROWS)), shape((8,))],
        [VMEM, SMEM],
        (counts, linear_out, gain, near_kv, far_kv),
        [SMEM] + [VMEM] * 4,
        [],
        0,
        8,
    )


def soft_open(counts, gauged, linear_out, total, gain, rows, near_kv, far_kv):
    bf16 = jnp.bfloat16
    return call(
        open_kernel,
        [shape((HEADS, ROWS, 256), bf16), shape((HEADS, ROWS, 256)), shape((HEADS, ROWS, DH)), shape((8,))],
        [VMEM, VMEM, ANY, SMEM],
        (counts, gauged, linear_out, total, gain, rows, near_kv, far_kv),
        [SMEM] * 2 + [VMEM] * 4 + [ANY] * 2,
        [
            pltpu.VMEM((2, 2 * ROWS, DH), bf16),
            pltpu.VMEM((ROWS, ROWS), jnp.float32),
            pltpu.VMEM((HEADS, ROWS, DH), jnp.float32),
            pltpu.SemaphoreType.DMA((2,)),
        ],
        0,
        28,
    )


def soft_close(counts, stat, linear_out, total, gain, queries, part, top, pieces):
    bf16 = jnp.bfloat16
    return call(
        close_kernel,
        [shape((ROWS, WIDE), bf16)],
        [ANY],
        (counts, stat, linear_out, total, gain, queries, part, top) + tuple(pieces),
        [SMEM] * 2 + [VMEM] * 5 + [ANY] * 5,
        [
            pltpu.VMEM((SLOTS - 2, 2 * ROWS, DH), bf16),
            pltpu.VMEM((HEADS, ROWS, 256), bf16),
            pltpu.VMEM((HEADS, ROWS, 256), jnp.float32),
            pltpu.VMEM((ROWS, ROWS), jnp.float32),
            pltpu.VMEM((HEADS, ROWS, DH), jnp.float32),
            pltpu.VMEM((ROWS, WIDE), bf16),
            pltpu.SemaphoreType.DMA((SLOTS - 2,)),
            pltpu.SemaphoreType.DMA((HEADS,)),
        ],
        0,
        32,
    )[0]


def shift(x, axis, by):
    size = lax.axis_size(axis)
    return lax.ppermute(x, axis, [(i, (i + by) % size) for i in range(size)])


def after(x, *others):
    return lax.optimization_barrier((x,) + others)[0]


def local(query_feats, key_feats, values, keys_soft, values_soft, norm_gain, doc_ids):
    zs = lax.axis_size("z")
    *chunks, own_kv, counts = states(doc_ids, key_feats, values, keys_soft, values_soft)

    parts = [stash(chunks[0])] + [shift(chunks[s], "x", s) for s in (1, 2, 3)]

    near_kv = lax.ppermute(own_kv, ("phase", "z"), [(zs + i, zs + i + 1) for i in range(zs - 1)])
    far_kv = lax.ppermute(own_kv, ("phase", "z"), [(i, zs + i + 2) for i in range(zs - 2)])

    local_sums = local_part(counts, query_feats, key_feats, values)
    total = row_sum(parts)
    near = lax.ppermute(total, "z", [(i, i + 1) for i in range(zs - 1)])
    far = lax.ppermute(
        total,
        ("phase", "z"),
        [((1 - p) * zs + i, p * zs + i + 2) for p in range(2) for i in range(zs - 2)],
    )

    messages = lax.optimization_barrier((total,) + tuple(pack(own_kv, near_kv, far_kv)))[1:]
    others = [
        lax.ppermute(message, ("phase", "x"), [(4 + i, 4 + (i + s) % 4) for i in range(4)])
        for s, message in zip((1, 2, 3), messages)
    ]

    near = after(near, *local_sums)
    priors = priors_of(parts, near, far)
    arrived = [priors[0]] + [shift(priors[s], "x", s) for s in (1, 2, 3)]
    num, den, feats_hi, feats_lo = local_sums
    linear_out, squares = finish(counts, feats_hi, feats_lo, num, den, arrived)
    total = squares + shift(squares, "core", 1)
    gain = norm_gain[None]
    rows, gauged = gauge(counts, linear_out, gain, near_kv, far_kv)
    total = total + lax.ppermute(total, "y", list(enumerate((1, 0, 3, 2))))
    total = after(total, rows)
    total = total + lax.ppermute(total, "y", list(enumerate((3, 2, 1, 0))))
    queries, part, top, stat = soft_open(counts, gauged, linear_out, total, gain, rows, near_kv, far_kv)
    return soft_close(counts, stat, linear_out, total, gain, queries, part, top, [own_kv] + others)[None]


def solution(mesh):
    fine = Mesh(mesh.devices.reshape(2, 4, 4, 4, 2), ("phase", "z", "x", "y", "core"))
    seq, head = ("z", "x"), ("y", "core")
    return jax.shard_map(
        local,
        mesh=fine,
        in_specs=(
            P(seq, head),
            P(seq, head),
            P(seq, head),
            P(seq, head),
            P(seq, head),
            P(head),
            P(),
        ),
        out_specs=P("phase", seq, head),
        check_vma=False,
    )
```

```python
import math

import jax
import jax.numpy as jnp
from jax import lax
from jax.experimental import pallas as pl
from jax.experimental.pallas import tpu as pltpu
from jax.sharding import Mesh, PartitionSpec as P

DH = 128
F = 16
ROWS = 512
HEADS = 8
WIDE = HEADS * DH
ALL_WIDE = 64 * DH
USED = (F + 1) * (F + 2) // 2
FEATS = 160
QUARTER = HEADS * FEATS // 4
SLOTS = 9
DOC_ROW = USED + 2
LOG2E = math.log2(math.e)
FACTOR = LOG2E / math.sqrt(DH)
SAFE = 110.0
FAR = -1e30

NN = (((1,), (0,)), ((), ()))
NT = (((1,), (1,)), ((), ()))


def dot(a, b, dims=NN):
    return lax.dot_general(a, b, dims, preferred_element_type=jnp.float32)


def split(x):
    hi = x.astype(jnp.bfloat16)
    lo = (x - hi.astype(jnp.float32)).astype(jnp.bfloat16)
    return hi, lo


def doc_of(position, n1, n2):
    return (position >= n1).astype(jnp.int32) + (position >= n2).astype(jnp.int32)


def start_of(position, n1, n2):
    return jnp.where(position >= n2, n2, jnp.where(position >= n1, n1, 0))


def pair_of(e):
    gap = jnp.zeros_like(e)
    for k in range(1, F // 2 + 1):
        gap = gap + (e >= k * (F + 1)).astype(jnp.int32)
    m = e - gap * (F + 1)
    n = m + gap
    n = jnp.where(n > F, n - (F + 1), n)
    times = jnp.where((gap == 0) & (m < F), 1.0, 2.0)
    times = jnp.where(e < USED, times, 0.0)
    return m, n, times


def here():
    return lax.axis_index("z"), lax.axis_index("x")


def row_block(x, s):
    return lax.rem(x - s + 4, 4)


def same(a, b):
    return (a == b).astype(jnp.float32)


def doc_row(ref):
    return ref[DOC_ROW : DOC_ROW + 1, :]


def row_sum_kernel(p0_ref, p1_ref, p2_ref, p3_ref, out_ref):
    parts = (p0_ref, p1_ref, p2_ref, p3_ref)
    end = doc_row(p0_ref)
    for part in parts[1:]:
        end = jnp.maximum(end, doc_row(part))
    total = jnp.zeros((QUARTER, DH), jnp.float32)
    for part in parts:
        total = total + same(doc_row(part), end) * part[...]
    out_ref[...] = total
    out_ref[DOC_ROW : DOC_ROW + 1, :] = end


def prior_kernel(p0_ref, p1_ref, p2_ref, p3_ref, near_ref, far_ref, *outs):
    z, x = here()
    parts = (p0_ref, p1_ref, p2_ref, p3_ref)
    before = doc_row(near_ref)
    incoming = near_ref[...] + same(doc_row(far_ref), before) * far_ref[...]
    for t, out in enumerate(outs):
        target = lax.rem(x + t, 4)
        doc = before
        for s, part in enumerate(parts):
            doc = jnp.where(row_block(x, s) == target - 1, doc_row(part), doc)
        prior = same(before, doc) * incoming
        for s, part in enumerate(parts):
            use = jnp.where(row_block(x, s) < target, same(doc_row(part), doc), 0.0)
            prior = prior + use * part[...]
        out[...] = prior


def stash_kernel(src_hbm, out_ref, sem):
    copy = pltpu.make_async_copy(src_hbm, out_ref, sem)
    copy.start()
    copy.wait()


def pack_kernel(own_hbm, near_hbm, far_hbm, o1_hbm, o2_hbm, o3_hbm, sems):
    z, x = here()
    upper, lower = pl.ds(0, 2 * ROWS), pl.ds(2 * ROWS, 2 * ROWS)
    for s, out in enumerate((o1_hbm, o2_hbm, o3_hbm)):
        later = lax.rem(x + s + 1, 4) > x
        pltpu.make_async_copy(near_hbm, out.at[upper], sems.at[s]).start()
        pl.when(later)(lambda: pltpu.make_async_copy(own_hbm, out.at[lower], sems.at[3 + s]).start())
        pl.when(jnp.logical_not(later))(lambda: pltpu.make_async_copy(far_hbm, out.at[lower], sems.at[3 + s]).start())
    for s, out in enumerate((o1_hbm, o2_hbm, o3_hbm)):
        pltpu.make_async_copy(near_hbm, out.at[upper], sems.at[s]).wait()
        pltpu.make_async_copy(own_hbm, out.at[lower], sems.at[3 + s]).wait()


def states_kernel(doc_hbm, kf_hbm, v_hbm, k_hbm, vs_hbm, c0_ref, c1_ref, c2_ref, c3_ref, kv_ref, n_ref, state_ref, doc_ref, kf_ref, v_ref, sems):
    pairs = [(doc_hbm, doc_ref), (kf_hbm, kf_ref), (v_hbm, v_ref), (k_hbm, kv_ref.at[:ROWS]), (vs_hbm, kv_ref.at[ROWS:])]
    copies = [pltpu.make_async_copy(src, dst, sems.at[i]) for i, (src, dst) in enumerate(pairs)]
    for copy in copies:
        copy.start()
    z, x = here()
    first = (z * 4 + x) * ROWS
    m, n, times = pair_of(lax.broadcasted_iota(jnp.int32, (FEATS, 2 * F), 0))
    col = lax.broadcasted_iota(jnp.int32, (FEATS, 2 * F), 1)
    e1 = ((col == m) & (times > 0)).astype(jnp.float32).astype(jnp.bfloat16)
    e2 = ((col == n) & (times > 0)).astype(jnp.float32).astype(jnp.bfloat16)
    lane = lax.broadcasted_iota(jnp.int32, (ROWS, DH), 1)
    norms = jnp.zeros((FEATS, DH), jnp.float32)
    copies[0].wait()
    n1 = jnp.sum((doc_ref[...] < 1).astype(jnp.int32))
    n2 = jnp.sum((doc_ref[...] < 2).astype(jnp.int32))
    n_ref[0] = n1
    n_ref[1] = n2
    pos = first + lax.broadcasted_iota(jnp.int32, (F, ROWS), 1)
    sel = (doc_of(pos, n1, n2) == doc_of(first + ROWS - 1, n1, n2)).astype(jnp.float32)
    copies[1].wait()
    kt = kf_ref[...].astype(jnp.float32).T
    copies[2].wait()
    for h in range(HEADS):
        rows = jnp.concatenate([kt[h * F : (h + 1) * F] * sel, sel], 0).astype(jnp.bfloat16)
        hi, lo = split(dot(e1, rows) * dot(e2, rows))
        unit = (lane == h).astype(jnp.bfloat16)
        rhs = jnp.concatenate([v_ref[:, h * DH : (h + 1) * DH], unit], 1)
        res = dot(hi, rhs) + dot(lo, rhs)
        state_ref[h * FEATS : (h + 1) * FEATS, :] = res[:, :DH]
        norms = norms + res[:, DH:]
    across = norms.T
    for h in range(HEADS):
        base = h * FEATS + USED
        state_ref[base : base + 1, :] = across[h : h + 1, :DH]
        state_ref[base + 1 : base + 2, : FEATS - DH] = across[h : h + 1, DH:]
        last = doc_of(first + ROWS - 1, n1, n2).astype(jnp.float32)
        state_ref[base + 2 : base + 3, :] = jnp.full((1, DH), last, jnp.float32)
    for s, out in enumerate((c0_ref, c1_ref, c2_ref, c3_ref)):
        chunk = lax.rem(x + s, 4)
        out[...] = state_ref[pl.ds(pl.multiple_of(chunk * QUARTER, QUARTER), QUARTER), :]
    copies[3].wait()
    copies[4].wait()


def local_kernel(n_ref, qf_ref, kf_ref, v_ref, num_ref, den_ref, hi_ref, lo_ref, mask_ref):
    n1, n2 = n_ref[0], n_ref[1]
    z, x = here()
    first = (z * 4 + x) * ROWS
    row = lax.broadcasted_iota(jnp.int32, (ROWS, ROWS), 0)
    col = lax.broadcasted_iota(jnp.int32, (ROWS, ROWS), 1)
    begin = start_of(first + lax.broadcasted_iota(jnp.int32, (ROWS, 1), 0), n1, n2) - first
    mask_ref[...] = ((col <= row) & (col >= begin)).astype(jnp.float32)
    lane = lax.broadcasted_iota(jnp.int32, (ROWS, DH), 1)
    one = (lane == 0).astype(jnp.bfloat16)
    kf = jnp.concatenate([kf_ref[...], one], 1)
    half = ROWS // 2
    dens = [jnp.zeros((half, DH), jnp.float32) for _ in range(2)]
    for h in range(HEADS):
        qh = jnp.where(lane // F == h, qf_ref[...], jnp.zeros((), jnp.bfloat16))
        qh = jnp.concatenate([qh, one], 1)
        unit = (lane == h).astype(jnp.bfloat16)
        rhs = jnp.concatenate([v_ref[:, h * DH : (h + 1) * DH], unit], 1)
        for r in range(2):
            span = (r + 1) * half
            s = dot(qh[r * half : (r + 1) * half], kf[:span], NT)
            w = (s * s + 1.0) * mask_ref[r * half : (r + 1) * half, :span]
            hi, lo = split(w)
            res = dot(hi, rhs[:span]) + dot(lo, rhs[:span])
            num_ref[r * half : (r + 1) * half, h * DH : (h + 1) * DH] = res[:, :DH]
            dens[r] = dens[r] + res[:, DH:]
    for r in range(2):
        den_ref[r * half : (r + 1) * half, :] = dens[r]
    m, n, times = pair_of(lax.broadcasted_iota(jnp.int32, (DH, 256), 1))
    lane_row = lax.broadcasted_iota(jnp.int32, (DH, 256), 0)
    m1, n1_, times1 = pair_of(lax.broadcasted_iota(jnp.int32, (1, 256), 1))
    ones_a = jnp.where(m1 == F, times1, 0.0)
    ones_b = jnp.where((n1_ == F) & (times1 > 0), 1.0, 0.0)
    once = (times > 0).astype(jnp.float32)
    q = qf_ref[...]
    for h in range(HEADS):
        e1 = jnp.where((lane_row == m + h * F) & (m < F), times, 0.0).astype(jnp.bfloat16)
        e2 = jnp.where((lane_row == n + h * F) & (n < F), once, 0.0).astype(jnp.bfloat16)
        hi, lo = split((dot(q, e1) + ones_a) * (dot(q, e2) + ones_b))
        hi_ref[:, h * 256 : (h + 1) * 256] = hi
        lo_ref[:, h * 256 : (h + 1) * 256] = lo


def finish_kernel(n_ref, hi_ref, lo_ref, num_ref, den_ref, p0_ref, p1_ref, p2_ref, p3_ref, out_ref, sq_ref, prior_ref):
    n1, n2 = n_ref[0], n_ref[1]
    z, x = here()
    first = (z * 4 + x) * ROWS
    pos = first + lax.broadcasted_iota(jnp.int32, (ROWS, 1), 0)
    usable = ((doc_of(pos, n1, n2) == doc_of(first - 1, n1, n2)) & (first > 0)).astype(jnp.float32)
    for s, part in enumerate((p0_ref, p1_ref, p2_ref, p3_ref)):
        chunk = lax.rem(x - s + 4, 4)
        prior_ref[pl.ds(pl.multiple_of(chunk * QUARTER, QUARTER), QUARTER), :] = part[...]
    spare = [jnp.zeros((DH - HEADS, DH), jnp.float32)]
    sums = [[prior_ref[h * FEATS + USED + i : h * FEATS + USED + i + 1, :] for h in range(HEADS)] for i in range(2)]
    norm = jnp.concatenate([jnp.concatenate(rows + spare, 0).T for rows in sums], 0)[:FEATS]
    norm_hi, norm_lo = split(norm)
    squares = jnp.zeros((ROWS, DH), jnp.float32)
    for h in range(HEADS):
        hi = hi_ref[:, h * 256 : h * 256 + FEATS]
        lo = lo_ref[:, h * 256 : h * 256 + FEATS]
        s_hi, s_lo = split(prior_ref[h * FEATS : (h + 1) * FEATS, :])
        r_hi = jnp.concatenate([s_hi, norm_hi], 1)
        r_lo = jnp.concatenate([s_lo, norm_lo], 1)
        res = (dot(hi, r_hi) + (dot(lo, r_hi) + dot(hi, r_lo))) * usable
        num = num_ref[:, h * DH : (h + 1) * DH] + res[:, :DH]
        den = den_ref[:, h : h + 1] + res[:, DH + h : DH + h + 1]
        out = (num / den).astype(jnp.bfloat16)
        out_ref[:, h * DH : (h + 1) * DH] = out
        wide = out.astype(jnp.float32)
        squares = squares + wide * wide
    sq_ref[...] = jnp.sum(squares.T, 0, keepdims=True)


def block_of(slot):
    z, x = here()
    src = lax.rem(x + 4 - lax.div(slot - 1, 2), 4)
    behind = jnp.where(lax.rem(slot, 2) == 1, 1, jnp.where(src < x, 0, 2))
    return jnp.where(slot < 3, z * 4 + x - 4 * slot, (z - behind) * 4 + src)


def active(slot, n1, n2):
    z, x = here()
    own = z * 4 + x
    low = start_of(own * ROWS, n1, n2) // ROWS
    return (block_of(slot) >= low) & (block_of(slot) < own) | (slot == 0)


def key_norm(kv_ref, place):
    k = kv_ref[place, :ROWS].astype(jnp.float32)
    return jnp.sum(k * k, 1, keepdims=True)


def gauge_kernel(n_ref, lin_ref, gain_ref, own_ref, near_ref, far_ref, rows_ref, stat_ref):
    most = jnp.zeros((ROWS, 1), jnp.float32)
    for h in range(HEADS):
        lanes = slice(h * DH, (h + 1) * DH)
        q = lin_ref[:, lanes].astype(jnp.float32) * gain_ref[0:1, lanes]
        most = jnp.maximum(most, jnp.sum(q * q, 1, keepdims=True))
    rows_ref[...] = jnp.broadcast_to(most, (ROWS, DH)).T[:8]
    stat_ref[0] = 0.0
    for slot, kv_ref in enumerate((own_ref, near_ref, far_ref)):
        k = kv_ref[:ROWS].astype(jnp.float32)
        norm = jnp.max(jnp.sum(k * k, 1, keepdims=True))
        stat_ref[0] = jnp.where(active(slot, n_ref[0], n_ref[1]), jnp.maximum(stat_ref[0], norm), stat_ref[0])


def scale_of(total_ref):
    return lax.rsqrt(total_ref[...] / ALL_WIDE + 1e-06)


def make_queries(lin_ref, total_ref, gain_ref, q_ref, double):
    scale = jnp.broadcast_to(scale_of(total_ref), (DH, ROWS)).T
    for h in range(HEADS):
        lanes = slice(h * DH, (h + 1) * DH)
        q = (lin_ref[:, lanes].astype(jnp.float32) * scale * gain_ref[0:1, lanes]).astype(jnp.bfloat16)
        lo = jnp.zeros((ROWS, DH), jnp.bfloat16)
        if double:
            q, lo = split(q.astype(jnp.float32) * FACTOR)
        q_ref[h, :, :DH] = q
        q_ref[h, :, DH:] = lo


def ones_beside(v):
    return jnp.concatenate([v, jnp.ones((ROWS, DH), jnp.bfloat16)], 1)


def bounded_tile(kv_ref, place, slot, begin_first, q_ref, acc_ref, keep):
    kk = jnp.concatenate([kv_ref[place, :ROWS]] * 2, 1)
    key = block_of(slot) * ROWS + lax.broadcasted_iota(jnp.int32, (ROWS, 256), 0)
    inside = (key >= begin_first).astype(jnp.float32).astype(jnp.bfloat16)
    v = ones_beside(kv_ref[place, ROWS:]) * inside
    for h in range(HEADS):
        p = jnp.exp2(dot(q_ref[h], kk, NT)).astype(jnp.bfloat16)
        res = dot(p, v)
        acc_ref[h] += res if keep is None else res * keep


def bounded_tiles(slots, kv_ref, base, n1, n2, q_ref, acc_ref, before_use):
    first, positions = rows_of()
    begin_first = start_of(first, n1, n2)
    mixed = start_of(first + ROWS - 1, n1, n2) != begin_first

    def run(keep):
        def one(slot):
            before_use(slot)
            bounded_tile(kv_ref, slot - base, slot, begin_first, q_ref, acc_ref, keep)

        def step(slot, carry):
            pl.when(active(slot, n1, n2))(lambda: one(slot))
            return carry

        lax.fori_loop(*slots, step, 0)

    pl.when(jnp.logical_not(mixed))(lambda: run(None))
    pl.when(mixed)(lambda: run((start_of(positions, n1, n2) == begin_first).astype(jnp.float32)))


def make_mask(mask_ref, block, first, begin):
    row = lax.broadcasted_iota(jnp.int32, (ROWS, ROWS), 0)
    key = block * ROWS + lax.broadcasted_iota(jnp.int32, (ROWS, ROWS), 1)
    mask_ref[...] = jnp.where((key >= begin) & (key <= first + row), 0.0, FAR)


def any_tile(kv_ref, slot, base, first, begin, q_ref, acc_ref, mask_ref, top_ref):
    make_mask(mask_ref, block_of(slot), first, begin)
    kk = jnp.concatenate([kv_ref[slot - base, :ROWS]] * 2, 1)
    v = ones_beside(kv_ref[slot - base, ROWS:])

    def head(h, carry):
        s = jnp.maximum(dot(q_ref[h], kk, NT) * FACTOR + mask_ref[...], FAR)
        old = top_ref[h]
        new = jnp.maximum(old, jnp.max(s, 1, keepdims=True))
        p = jnp.exp2(s - jnp.concatenate([new] * 4, 1)).astype(jnp.bfloat16)
        fade = jnp.exp2(old - new)
        acc_ref[h] = acc_ref[h] * jnp.concatenate([fade] * 2, 1) + dot(p, v)
        top_ref[h] = new
        return carry

    lax.fori_loop(0, HEADS, head, 0)


def in_softmax_phase():
    return lax.axis_index("phase") == 1


def rows_of():
    z, x = here()
    first = (z * 4 + x) * ROWS
    return first, first + lax.broadcasted_iota(jnp.int32, (ROWS, 1), 0)


def open_kernel(
    n_ref, gauge_ref, lin_ref, total_ref, gain_ref, rows_ref, own_hbm, near_hbm, far_hbm,
    q_ref, acc_ref, top_hbm, stat_ref, kv_ref, mask_ref, top_ref, sems,
):
    @pl.when(in_softmax_phase())
    def _():
        n1, n2 = n_ref[0], n_ref[1]
        first, positions = rows_of()
        begin = start_of(positions, n1, n2)
        copies = [
            pltpu.make_async_copy(src, kv_ref.at[i], sems.at[i]) for i, src in enumerate((own_hbm, near_hbm, far_hbm))
        ]
        for copy in copies:
            copy.start()
        scale = scale_of(total_ref)
        q_most = 1.02 * jnp.max(scale * scale * rows_ref[0:1, :])
        safe = q_most * gauge_ref[0] < (SAFE / FACTOR) ** 2
        stat_ref[0] = q_most
        stat_ref[1] = jnp.where(safe, 1.0, 0.0)

        @pl.when(safe)
        def _():
            make_queries(lin_ref, total_ref, gain_ref, q_ref, True)
            make_mask(mask_ref, block_of(0), first, begin)
            for copy in copies:
                copy.wait()
            kk = jnp.concatenate([kv_ref[0, :ROWS]] * 2, 1)
            v = ones_beside(kv_ref[0, ROWS:])
            half = ROWS // 2
            for h in range(HEADS):
                for r in range(2):
                    rows, span = slice(r * half, (r + 1) * half), (r + 1) * half
                    s = dot(q_ref[h, rows, :], kk[:span], NT) + mask_ref[rows, :span]
                    acc_ref[h, rows, :] = dot(jnp.exp2(s).astype(jnp.bfloat16), v[:span])
            bounded_tiles((1, 3), kv_ref, 0, n1, n2, q_ref, acc_ref, lambda slot: None)

        @pl.when(jnp.logical_not(safe))
        def _():
            make_queries(lin_ref, total_ref, gain_ref, q_ref, False)
            acc_ref[...] = jnp.zeros_like(acc_ref)
            top_ref[...] = jnp.full(top_ref.shape, FAR, jnp.float32)
            for copy in copies:
                copy.wait()

            def step(slot, carry):
                pl.when(active(slot, n1, n2))(
                    lambda: any_tile(kv_ref, slot, 0, first, begin, q_ref, acc_ref, mask_ref, top_ref)
                )
                return carry

            lax.fori_loop(0, 3, step, 0)
            copy = pltpu.make_async_copy(top_ref, top_hbm, sems.at[0])
            copy.start()
            copy.wait()


def close_kernel(n_ref, stat_ref, lin_ref, total_ref, gain_ref, q_ref, part_ref, top_hbm, *refs):
    kv_hbm, (out_hbm, kv_ref, raw_ref, acc_ref, mask_ref, top_ref, norm_ref, out_ref, kv_sems, out_sems) = refs[:3], refs[3:]

    @pl.when(jnp.logical_not(in_softmax_phase()))
    def _():
        copy = pltpu.make_async_copy(lin_ref, out_hbm, out_sems.at[0])
        copy.start()
        copy.wait()

    @pl.when(in_softmax_phase())
    def _():
        close(
            n_ref, stat_ref, lin_ref, total_ref, gain_ref, q_ref, part_ref, top_hbm, kv_hbm,
            out_hbm, kv_ref, raw_ref, acc_ref, mask_ref, top_ref, norm_ref, out_ref, kv_sems, out_sems,
        )


def close(
    n_ref, stat_ref, lin_ref, total_ref, gain_ref, q_ref, part_ref, top_hbm, kv_hbm,
    out_hbm, kv_ref, raw_ref, acc_ref, mask_ref, top_ref, norm_ref, out_ref, kv_sems, out_sems,
):
    n1, n2 = n_ref[0], n_ref[1]
    base = 3

    def fetch(slot):
        src = kv_hbm[(slot - base) // 2].at[pl.ds((slot - base) % 2 * 2 * ROWS, 2 * ROWS)]
        return pltpu.make_async_copy(src, kv_ref.at[slot - base], kv_sems.at[slot - base])

    def arrived(slot):
        place = kv_ref.at[slot - base]
        pltpu.make_async_copy(place, place, kv_sems.at[slot - base]).wait()

    for slot in range(base, SLOTS):
        pl.when(active(slot, n1, n2))(lambda: fetch(slot).start())
    acc_ref[...] = part_ref[...]
    norm_ref[...] = jnp.zeros_like(norm_ref)
    opened_safe = stat_ref[1] > 0.5

    def before_use(slot):
        arrived(slot)
        norm_ref[...] = jnp.maximum(norm_ref[...], key_norm(kv_ref, slot - base))

    @pl.when(opened_safe)
    def _():
        bounded_tiles((base, SLOTS), kv_ref, base, n1, n2, q_ref, acc_ref, before_use)

    @pl.when(jnp.logical_not(opened_safe))
    def _():
        for slot in range(base, SLOTS):
            pl.when(active(slot, n1, n2))(lambda: arrived(slot))

    safe = opened_safe & (stat_ref[0] * jnp.max(norm_ref[...]) < (SAFE / FACTOR) ** 2)

    @pl.when(jnp.logical_not(safe))
    def _():
        first, positions = rows_of()
        begin = start_of(positions, n1, n2)
        make_queries(lin_ref, total_ref, gain_ref, raw_ref, False)
        acc_ref[...] = part_ref[...]
        top_ref[...] = jnp.zeros_like(top_ref)

        @pl.when(jnp.logical_not(opened_safe))
        def _():
            copy = pltpu.make_async_copy(top_hbm, top_ref, kv_sems.at[0])
            copy.start()
            copy.wait()

        def step(slot, carry):
            pl.when(active(slot, n1, n2))(
                lambda: any_tile(kv_ref, slot, base, first, begin, raw_ref, acc_ref, mask_ref, top_ref)
            )
            return carry

        lax.fori_loop(base, SLOTS, step, 0)

    copies = []
    for h in range(HEADS):
        lanes = slice(h * DH, (h + 1) * DH)
        out_ref[:, lanes] = (acc_ref[h, :, :DH] / acc_ref[h, :, DH:]).astype(jnp.bfloat16)
        copies.append(pltpu.make_async_copy(out_ref.at[:, lanes], out_hbm.at[:, lanes], out_sems.at[h]))
        copies[-1].start()
    for copy in copies:
        copy.wait()


VMEM = pl.BlockSpec(memory_space=pltpu.VMEM)
SMEM = pl.BlockSpec(memory_space=pltpu.SMEM)
ANY = pl.BlockSpec(memory_space=pl.ANY)


def call(kernel, outs, out_specs, args, in_specs, scratch, flops, limit):
    return pl.pallas_call(
        kernel,
        out_shape=tuple(outs),
        in_specs=in_specs,
        out_specs=tuple(out_specs),
        scratch_shapes=scratch,
        compiler_params=pltpu.CompilerParams(vmem_limit_bytes=limit << 20),
        cost_estimate=pl.CostEstimate(flops=flops, bytes_accessed=0, transcendentals=0),
    )(*args)


def shape(dims, dtype=jnp.float32):
    return jax.ShapeDtypeStruct(dims, dtype)


def stash(chunk):
    return call(stash_kernel, [shape(chunk.shape)], [VMEM], (chunk,), [ANY], [pltpu.SemaphoreType.DMA], 0, 4)[0]


def row_sum(parts):
    return call(row_sum_kernel, [shape((QUARTER, DH))], [VMEM], tuple(parts), [VMEM] * 4, [], 0, 8)[0]


def priors_of(parts, near, far):
    return call(
        prior_kernel, [shape((QUARTER, DH))] * 4, [VMEM] * 4, tuple(parts) + (near, far), [VMEM] * 6, [], 1000000000, 8
    )


def pack(own_kv, near_kv, far_kv):
    return call(
        pack_kernel,
        [shape((4 * ROWS, DH), own_kv.dtype)] * 3,
        [ANY] * 3,
        (own_kv, near_kv, far_kv),
        [ANY] * 3,
        [pltpu.SemaphoreType.DMA((6,))],
        5000000000,
        4,
    )


def states(doc_ids, key_feats, values, keys_soft, values_soft):
    bf16 = jnp.bfloat16
    return call(
        states_kernel,
        [shape((QUARTER, DH))] * 4 + [shape((2 * ROWS, DH), bf16), shape((8,), jnp.int32)],
        [VMEM] * 5 + [SMEM],
        (doc_ids.reshape(-1, DH), key_feats, values, keys_soft, values_soft),
        [ANY] * 5,
        [
            pltpu.VMEM((HEADS * FEATS, DH), jnp.float32),
            pltpu.VMEM((doc_ids.shape[0] // DH, DH), jnp.int32),
            pltpu.VMEM((ROWS, DH), bf16),
            pltpu.VMEM((ROWS, WIDE), bf16),
            pltpu.SemaphoreType.DMA((5,)),
        ],
        0,
        60,
    )


def local_part(counts, query_feats, key_feats, values):
    bf16 = jnp.bfloat16
    return call(
        local_kernel,
        [shape((ROWS, WIDE)), shape((ROWS, DH)), shape((ROWS, HEADS * 256), bf16), shape((ROWS, HEADS * 256), bf16)],
        [VMEM] * 4,
        (counts, query_feats, key_feats, values),
        [SMEM] + [VMEM] * 3,
        [pltpu.VMEM((ROWS, ROWS), jnp.float32)],
        0,
        24,
    )


def finish(counts, feats_hi, feats_lo, num, den, parts):
    return call(
        finish_kernel,
        [shape((ROWS, WIDE), jnp.bfloat16), shape((1, ROWS))],
        [VMEM] * 2,
        (counts, feats_hi, feats_lo, num, den) + tuple(parts),
        [SMEM] + [VMEM] * 8,
        [pltpu.VMEM((HEADS * FEATS, DH), jnp.float32)],
        8000000000,
        20,
    )


def gauge(counts, linear_out, gain, own_kv, near_kv, far_kv):
    return call(
        gauge_kernel,
        [shape((8, ROWS)), shape((8,))],
        [VMEM, SMEM],
        (counts, linear_out, gain, own_kv, near_kv, far_kv),
        [SMEM] + [VMEM] * 5,
        [],
        0,
        8,
    )


def soft_open(counts, gauged, linear_out, total, gain, rows, own_kv, near_kv, far_kv):
    bf16 = jnp.bfloat16
    return call(
        open_kernel,
        [shape((HEADS, ROWS, 256), bf16), shape((HEADS, ROWS, 256)), shape((HEADS, ROWS, DH)), shape((8,))],
        [VMEM, VMEM, ANY, SMEM],
        (counts, gauged, linear_out, total, gain, rows, own_kv, near_kv, far_kv),
        [SMEM] * 2 + [VMEM] * 4 + [ANY] * 3,
        [
            pltpu.VMEM((3, 2 * ROWS, DH), bf16),
            pltpu.VMEM((ROWS, ROWS), jnp.float32),
            pltpu.VMEM((HEADS, ROWS, DH), jnp.float32),
            pltpu.SemaphoreType.DMA((3,)),
        ],
        0,
        28,
    )


def soft_close(counts, stat, linear_out, total, gain, queries, part, top, pieces):
    bf16 = jnp.bfloat16
    return call(
        close_kernel,
        [shape((ROWS, WIDE), bf16)],
        [ANY],
        (counts, stat, linear_out, total, gain, queries, part, top) + tuple(pieces),
        [SMEM] * 2 + [VMEM] * 5 + [ANY] * 4,
        [
            pltpu.VMEM((SLOTS - 3, 2 * ROWS, DH), bf16),
            pltpu.VMEM((HEADS, ROWS, 256), bf16),
            pltpu.VMEM((HEADS, ROWS, 256), jnp.float32),
            pltpu.VMEM((ROWS, ROWS), jnp.float32),
            pltpu.VMEM((HEADS, ROWS, DH), jnp.float32),
            pltpu.VMEM((ROWS, 1), jnp.float32),
            pltpu.VMEM((ROWS, WIDE), bf16),
            pltpu.SemaphoreType.DMA((SLOTS - 3,)),
            pltpu.SemaphoreType.DMA((HEADS,)),
        ],
        0,
        32,
    )[0]


def shift(x, axis, by):
    size = lax.axis_size(axis)
    return lax.ppermute(x, axis, [(i, (i + by) % size) for i in range(size)])


def after(x, *others):
    return lax.optimization_barrier((x,) + others)[0]


def local(query_feats, key_feats, values, keys_soft, values_soft, norm_gain, doc_ids):
    zs = lax.axis_size("z")
    *chunks, own_kv, counts = states(doc_ids, key_feats, values, keys_soft, values_soft)

    parts = [stash(chunks[0])] + [shift(chunks[s], "x", s) for s in (1, 2, 3)]

    near_kv = lax.ppermute(own_kv, ("phase", "z"), [(zs + i, zs + i + 1) for i in range(zs - 1)])
    far_kv = lax.ppermute(own_kv, ("phase", "z"), [(i, zs + i + 2) for i in range(zs - 2)])

    local_sums = local_part(counts, query_feats, key_feats, values)
    total = row_sum(parts)
    near = lax.ppermute(total, "z", [(i, i + 1) for i in range(zs - 1)])
    far = lax.ppermute(
        total,
        ("phase", "z"),
        [((1 - p) * zs + i, p * zs + i + 2) for p in range(2) for i in range(zs - 2)],
    )

    messages = lax.optimization_barrier((total,) + tuple(pack(own_kv, near_kv, far_kv)))[1:]
    others = [
        lax.ppermute(message, ("phase", "x"), [(4 + i, 4 + (i + s) % 4) for i in range(4)])
        for s, message in zip((1, 2, 3), messages)
    ]

    near = after(near, *local_sums)
    priors = priors_of(parts, near, far)
    arrived = [priors[0]] + [shift(priors[s], "x", s) for s in (1, 2, 3)]
    num, den, feats_hi, feats_lo = local_sums
    linear_out, squares = finish(counts, feats_hi, feats_lo, num, den, arrived)
    total = squares + shift(squares, "core", 1)
    gain = norm_gain[None]
    rows, gauged = gauge(counts, linear_out, gain, own_kv, near_kv, far_kv)
    total = total + lax.ppermute(total, "y", list(enumerate((1, 0, 3, 2))))
    total = after(total, rows)
    total = total + lax.ppermute(total, "y", list(enumerate((3, 2, 1, 0))))
    queries, part, top, stat = soft_open(counts, gauged, linear_out, total, gain, rows, own_kv, near_kv, far_kv)
    return soft_close(counts, stat, linear_out, total, gain, queries, part, top, others)[None]


def solution(mesh):
    fine = Mesh(mesh.devices.reshape(2, 4, 4, 4, 2), ("phase", "z", "x", "y", "core"))
    seq, head = ("z", "x"), ("y", "core")
    return jax.shard_map(
        local,
        mesh=fine,
        in_specs=(
            P(seq, head),
            P(seq, head),
            P(seq, head),
            P(seq, head),
            P(seq, head),
            P(head),
            P(),
        ),
        out_specs=P("phase", seq, head),
        check_vma=False,
    )
```

```python
import math

import jax
import jax.numpy as jnp
from jax import lax
from jax.experimental import pallas as pl
from jax.experimental.pallas import tpu as pltpu
from jax.sharding import Mesh, PartitionSpec as P

DH = 128
F = 16
ROWS = 512
HEADS = 8
WIDE = HEADS * DH
ALL_WIDE = 64 * DH
USED = (F + 1) * (F + 2) // 2
FEATS = 160
QUARTER = HEADS * FEATS // 4
SLOTS = 9
DOC_ROW = USED + 2
LOG2E = math.log2(math.e)
FACTOR = LOG2E / math.sqrt(DH)
SAFE = 110.0
FAR = -1e30

NN = (((1,), (0,)), ((), ()))
NT = (((1,), (1,)), ((), ()))


def dot(a, b, dims=NN):
    return lax.dot_general(a, b, dims, preferred_element_type=jnp.float32)


def split(x):
    hi = x.astype(jnp.bfloat16)
    lo = (x - hi.astype(jnp.float32)).astype(jnp.bfloat16)
    return hi, lo


def doc_of(position, n1, n2):
    return (position >= n1).astype(jnp.int32) + (position >= n2).astype(jnp.int32)


def start_of(position, n1, n2):
    return jnp.where(position >= n2, n2, jnp.where(position >= n1, n1, 0))


def pair_of(e):
    gap = jnp.zeros_like(e)
    for k in range(1, F // 2 + 1):
        gap = gap + (e >= k * (F + 1)).astype(jnp.int32)
    m = e - gap * (F + 1)
    n = m + gap
    n = jnp.where(n > F, n - (F + 1), n)
    times = jnp.where((gap == 0) & (m < F), 1.0, 2.0)
    times = jnp.where(e < USED, times, 0.0)
    return m, n, times


def here():
    return lax.axis_index("z"), lax.axis_index("x")


def row_block(x, s):
    return lax.rem(x - s + 4, 4)


def same(a, b):
    return (a == b).astype(jnp.float32)


def doc_row(ref):
    return ref[DOC_ROW : DOC_ROW + 1, :]


def row_sum_kernel(p0_ref, p1_ref, p2_ref, p3_ref, out_ref):
    parts = (p0_ref, p1_ref, p2_ref, p3_ref)
    end = doc_row(p0_ref)
    for part in parts[1:]:
        end = jnp.maximum(end, doc_row(part))
    total = jnp.zeros((QUARTER, DH), jnp.float32)
    for part in parts:
        total = total + same(doc_row(part), end) * part[...]
    out_ref[...] = total
    out_ref[DOC_ROW : DOC_ROW + 1, :] = end


def prior_kernel(p0_ref, p1_ref, p2_ref, p3_ref, near_ref, far_ref, *outs):
    z, x = here()
    parts = (p0_ref, p1_ref, p2_ref, p3_ref)
    before = doc_row(near_ref)
    incoming = near_ref[...] + same(doc_row(far_ref), before) * far_ref[...]
    for t, out in enumerate(outs):
        target = lax.rem(x + t, 4)
        doc = before
        for s, part in enumerate(parts):
            doc = jnp.where(row_block(x, s) == target - 1, doc_row(part), doc)
        prior = same(before, doc) * incoming
        for s, part in enumerate(parts):
            use = jnp.where(row_block(x, s) < target, same(doc_row(part), doc), 0.0)
            prior = prior + use * part[...]
        out[...] = prior


def stash_kernel(src_hbm, out_ref, sem):
    copy = pltpu.make_async_copy(src_hbm, out_ref, sem)
    copy.start()
    copy.wait()


def pack_kernel(own_hbm, near_hbm, far_hbm, o1_hbm, o2_hbm, o3_hbm, sems):
    z, x = here()
    upper, lower = pl.ds(0, 2 * ROWS), pl.ds(2 * ROWS, 2 * ROWS)
    for s, out in enumerate((o1_hbm, o2_hbm, o3_hbm)):
        later = lax.rem(x + s + 1, 4) > x
        pltpu.make_async_copy(near_hbm, out.at[upper], sems.at[s]).start()
        pl.when(later)(lambda: pltpu.make_async_copy(own_hbm, out.at[lower], sems.at[3 + s]).start())
        pl.when(jnp.logical_not(later))(lambda: pltpu.make_async_copy(far_hbm, out.at[lower], sems.at[3 + s]).start())
    for s, out in enumerate((o1_hbm, o2_hbm, o3_hbm)):
        pltpu.make_async_copy(near_hbm, out.at[upper], sems.at[s]).wait()
        pltpu.make_async_copy(own_hbm, out.at[lower], sems.at[3 + s]).wait()


def states_kernel(doc_hbm, kf_hbm, v_hbm, k_hbm, vs_hbm, c0_ref, c1_ref, c2_ref, c3_ref, kv_ref, n_ref, state_ref, doc_ref, kf_ref, v_ref, sems):
    pairs = [(doc_hbm, doc_ref), (kf_hbm, kf_ref), (v_hbm, v_ref), (k_hbm, kv_ref.at[:ROWS]), (vs_hbm, kv_ref.at[ROWS:])]
    copies = [pltpu.make_async_copy(src, dst, sems.at[i]) for i, (src, dst) in enumerate(pairs)]
    for copy in copies:
        copy.start()
    z, x = here()
    first = (z * 4 + x) * ROWS
    m, n, times = pair_of(lax.broadcasted_iota(jnp.int32, (FEATS, 2 * F), 0))
    col = lax.broadcasted_iota(jnp.int32, (FEATS, 2 * F), 1)
    e1 = ((col == m) & (times > 0)).astype(jnp.float32).astype(jnp.bfloat16)
    e2 = ((col == n) & (times > 0)).astype(jnp.float32).astype(jnp.bfloat16)
    lane = lax.broadcasted_iota(jnp.int32, (ROWS, DH), 1)
    norms = jnp.zeros((FEATS, DH), jnp.float32)
    copies[0].wait()
    n1 = jnp.sum((doc_ref[...] < 1).astype(jnp.int32))
    n2 = jnp.sum((doc_ref[...] < 2).astype(jnp.int32))
    n_ref[0] = n1
    n_ref[1] = n2
    pos = first + lax.broadcasted_iota(jnp.int32, (F, ROWS), 1)
    sel = (doc_of(pos, n1, n2) == doc_of(first + ROWS - 1, n1, n2)).astype(jnp.float32)
    copies[1].wait()
    kt = kf_ref[...].astype(jnp.float32).T
    copies[2].wait()
    for h in range(HEADS):
        rows = jnp.concatenate([kt[h * F : (h + 1) * F] * sel, sel], 0).astype(jnp.bfloat16)
        hi, lo = split(dot(e1, rows) * dot(e2, rows))
        unit = (lane == h).astype(jnp.bfloat16)
        rhs = jnp.concatenate([v_ref[:, h * DH : (h + 1) * DH], unit], 1)
        res = dot(hi, rhs) + dot(lo, rhs)
        state_ref[h * FEATS : (h + 1) * FEATS, :] = res[:, :DH]
        norms = norms + res[:, DH:]
    across = norms.T
    for h in range(HEADS):
        base = h * FEATS + USED
        state_ref[base : base + 1, :] = across[h : h + 1, :DH]
        state_ref[base + 1 : base + 2, : FEATS - DH] = across[h : h + 1, DH:]
        last = doc_of(first + ROWS - 1, n1, n2).astype(jnp.float32)
        state_ref[base + 2 : base + 3, :] = jnp.full((1, DH), last, jnp.float32)
    for s, out in enumerate((c0_ref, c1_ref, c2_ref, c3_ref)):
        chunk = lax.rem(x + s, 4)
        out[...] = state_ref[pl.ds(pl.multiple_of(chunk * QUARTER, QUARTER), QUARTER), :]
    copies[3].wait()
    copies[4].wait()


def local_kernel(n_ref, qf_ref, kf_ref, v_ref, num_ref, den_ref, hi_ref, lo_ref, mask_ref):
    n1, n2 = n_ref[0], n_ref[1]
    z, x = here()
    first = (z * 4 + x) * ROWS
    row = lax.broadcasted_iota(jnp.int32, (ROWS, ROWS), 0)
    col = lax.broadcasted_iota(jnp.int32, (ROWS, ROWS), 1)
    begin = start_of(first + lax.broadcasted_iota(jnp.int32, (ROWS, 1), 0), n1, n2) - first
    mask_ref[...] = ((col <= row) & (col >= begin)).astype(jnp.float32)
    lane = lax.broadcasted_iota(jnp.int32, (ROWS, DH), 1)
    one = (lane == 0).astype(jnp.bfloat16)
    kf = jnp.concatenate([kf_ref[...], one], 1)
    half = ROWS // 2
    dens = [jnp.zeros((half, DH), jnp.float32) for _ in range(2)]
    for h in range(HEADS):
        qh = jnp.where(lane // F == h, qf_ref[...], jnp.zeros((), jnp.bfloat16))
        qh = jnp.concatenate([qh, one], 1)
        unit = (lane == h).astype(jnp.bfloat16)
        rhs = jnp.concatenate([v_ref[:, h * DH : (h + 1) * DH], unit], 1)
        for r in range(2):
            span = (r + 1) * half
            s = dot(qh[r * half : (r + 1) * half], kf[:span], NT)
            w = (s * s + 1.0) * mask_ref[r * half : (r + 1) * half, :span]
            hi, lo = split(w)
            res = dot(hi, rhs[:span]) + dot(lo, rhs[:span])
            num_ref[r * half : (r + 1) * half, h * DH : (h + 1) * DH] = res[:, :DH]
            dens[r] = dens[r] + res[:, DH:]
    for r in range(2):
        den_ref[r * half : (r + 1) * half, :] = dens[r]
    m, n, times = pair_of(lax.broadcasted_iota(jnp.int32, (DH, 256), 1))
    lane_row = lax.broadcasted_iota(jnp.int32, (DH, 256), 0)
    m1, n1_, times1 = pair_of(lax.broadcasted_iota(jnp.int32, (1, 256), 1))
    ones_a = jnp.where(m1 == F, times1, 0.0)
    ones_b = jnp.where((n1_ == F) & (times1 > 0), 1.0, 0.0)
    once = (times > 0).astype(jnp.float32)
    q = qf_ref[...]
    for h in range(HEADS):
        e1 = jnp.where((lane_row == m + h * F) & (m < F), times, 0.0).astype(jnp.bfloat16)
        e2 = jnp.where((lane_row == n + h * F) & (n < F), once, 0.0).astype(jnp.bfloat16)
        hi, lo = split((dot(q, e1) + ones_a) * (dot(q, e2) + ones_b))
        hi_ref[:, h * 256 : (h + 1) * 256] = hi
        lo_ref[:, h * 256 : (h + 1) * 256] = lo


def finish_kernel(n_ref, hi_ref, lo_ref, num_ref, den_ref, p0_ref, p1_ref, p2_ref, p3_ref, out_ref, sq_ref, prior_ref):
    n1, n2 = n_ref[0], n_ref[1]
    z, x = here()
    first = (z * 4 + x) * ROWS
    pos = first + lax.broadcasted_iota(jnp.int32, (ROWS, 1), 0)
    usable = ((doc_of(pos, n1, n2) == doc_of(first - 1, n1, n2)) & (first > 0)).astype(jnp.float32)
    for s, part in enumerate((p0_ref, p1_ref, p2_ref, p3_ref)):
        chunk = lax.rem(x - s + 4, 4)
        prior_ref[pl.ds(pl.multiple_of(chunk * QUARTER, QUARTER), QUARTER), :] = part[...]
    spare = [jnp.zeros((DH - HEADS, DH), jnp.float32)]
    sums = [[prior_ref[h * FEATS + USED + i : h * FEATS + USED + i + 1, :] for h in range(HEADS)] for i in range(2)]
    norm = jnp.concatenate([jnp.concatenate(rows + spare, 0).T for rows in sums], 0)[:FEATS]
    norm_hi, norm_lo = split(norm)
    squares = jnp.zeros((ROWS, DH), jnp.float32)
    for h in range(HEADS):
        hi = hi_ref[:, h * 256 : h * 256 + FEATS]
        lo = lo_ref[:, h * 256 : h * 256 + FEATS]
        s_hi, s_lo = split(prior_ref[h * FEATS : (h + 1) * FEATS, :])
        r_hi = jnp.concatenate([s_hi, norm_hi], 1)
        r_lo = jnp.concatenate([s_lo, norm_lo], 1)
        res = (dot(hi, r_hi) + (dot(lo, r_hi) + dot(hi, r_lo))) * usable
        num = num_ref[:, h * DH : (h + 1) * DH] + res[:, :DH]
        den = den_ref[:, h : h + 1] + res[:, DH + h : DH + h + 1]
        out = (num / den).astype(jnp.bfloat16)
        out_ref[:, h * DH : (h + 1) * DH] = out
        wide = out.astype(jnp.float32)
        squares = squares + wide * wide
    sq_ref[...] = jnp.sum(squares.T, 0, keepdims=True)


def block_of(slot):
    z, x = here()
    src = lax.rem(x + 4 - lax.div(slot - 1, 2), 4)
    behind = jnp.where(lax.rem(slot, 2) == 1, 1, jnp.where(src < x, 0, 2))
    return jnp.where(slot < 3, z * 4 + x - 4 * slot, (z - behind) * 4 + src)


def active(slot, n1, n2):
    z, x = here()
    own = z * 4 + x
    low = start_of(own * ROWS, n1, n2) // ROWS
    return (block_of(slot) >= low) & (block_of(slot) < own) | (slot == 0)


def key_norm(kv_ref, place):
    k = kv_ref[place, :ROWS].astype(jnp.float32)
    return jnp.sum(k * k, 1, keepdims=True)


def gauge_kernel(n_ref, lin_ref, gain_ref, own_ref, near_ref, far_ref, rows_ref, stat_ref):
    most = jnp.zeros((ROWS, 1), jnp.float32)
    for h in range(HEADS):
        lanes = slice(h * DH, (h + 1) * DH)
        q = lin_ref[:, lanes].astype(jnp.float32) * gain_ref[0:1, lanes]
        most = jnp.maximum(most, jnp.sum(q * q, 1, keepdims=True))
    rows_ref[...] = jnp.broadcast_to(most, (ROWS, DH)).T[:8]
    stat_ref[0] = 0.0
    for slot, kv_ref in enumerate((own_ref, near_ref, far_ref)):
        k = kv_ref[:ROWS].astype(jnp.float32)
        norm = jnp.max(jnp.sum(k * k, 1, keepdims=True))
        stat_ref[0] = jnp.where(active(slot, n_ref[0], n_ref[1]), jnp.maximum(stat_ref[0], norm), stat_ref[0])


def scale_of(total_ref):
    return lax.rsqrt(total_ref[...] / ALL_WIDE + 1e-06)


def each_head(body):
    def two(pair, carry):
        body(2 * pair)
        body(2 * pair + 1)
        return carry

    lax.fori_loop(0, HEADS // 2, two, 0)


def make_queries(lin_ref, total_ref, gain_ref, q_ref, double):
    scale = jnp.broadcast_to(scale_of(total_ref), (DH, ROWS)).T

    def one(h):
        lanes = pl.ds(pl.multiple_of(h * DH, DH), DH)
        q = (lin_ref[:, lanes].astype(jnp.float32) * scale * gain_ref[0:1, lanes]).astype(jnp.bfloat16)
        lo = jnp.zeros((ROWS, DH), jnp.bfloat16)
        if double:
            q, lo = split(q.astype(jnp.float32) * FACTOR)
        q_ref[h, :, :DH] = q
        q_ref[h, :, DH:] = lo

    each_head(one)


def ones_beside(v):
    return jnp.concatenate([v, jnp.ones((ROWS, DH), jnp.bfloat16)], 1)


def bounded_tile(kv_ref, place, slot, begin_first, q_ref, acc_ref, keep):
    kk = jnp.concatenate([kv_ref[place, :ROWS]] * 2, 1)
    key = block_of(slot) * ROWS + lax.broadcasted_iota(jnp.int32, (ROWS, 256), 0)
    inside = (key >= begin_first).astype(jnp.float32).astype(jnp.bfloat16)
    v = ones_beside(kv_ref[place, ROWS:]) * inside

    def one(h):
        p = jnp.exp2(dot(q_ref[h], kk, NT)).astype(jnp.bfloat16)
        res = dot(p, v)
        acc_ref[h] += res if keep is None else res * keep

    each_head(one)


def bounded_tiles(slots, kv_ref, base, n1, n2, q_ref, acc_ref, before_use):
    first, positions = rows_of()
    begin_first = start_of(first, n1, n2)
    mixed = start_of(first + ROWS - 1, n1, n2) != begin_first

    def run(keep):
        def one(slot):
            before_use(slot)
            bounded_tile(kv_ref, slot - base, slot, begin_first, q_ref, acc_ref, keep)

        def step(slot, carry):
            pl.when(active(slot, n1, n2))(lambda: one(slot))
            return carry

        lax.fori_loop(*slots, step, 0)

    pl.when(jnp.logical_not(mixed))(lambda: run(None))
    pl.when(mixed)(lambda: run((start_of(positions, n1, n2) == begin_first).astype(jnp.float32)))


def make_mask(mask_ref, block, first, begin):
    row = lax.broadcasted_iota(jnp.int32, (ROWS, ROWS), 0)
    key = block * ROWS + lax.broadcasted_iota(jnp.int32, (ROWS, ROWS), 1)
    mask_ref[...] = jnp.where((key >= begin) & (key <= first + row), 0.0, FAR)


def any_tile(kv_ref, slot, base, first, begin, q_ref, acc_ref, mask_ref, top_ref):
    make_mask(mask_ref, block_of(slot), first, begin)
    kk = jnp.concatenate([kv_ref[slot - base, :ROWS]] * 2, 1)
    v = ones_beside(kv_ref[slot - base, ROWS:])

    def head(h, carry):
        s = jnp.maximum(dot(q_ref[h], kk, NT) * FACTOR + mask_ref[...], FAR)
        old = top_ref[h]
        new = jnp.maximum(old, jnp.max(s, 1, keepdims=True))
        p = jnp.exp2(s - jnp.concatenate([new] * 4, 1)).astype(jnp.bfloat16)
        fade = jnp.exp2(old - new)
        acc_ref[h] = acc_ref[h] * jnp.concatenate([fade] * 2, 1) + dot(p, v)
        top_ref[h] = new
        return carry

    lax.fori_loop(0, HEADS, head, 0)


def in_softmax_phase():
    return lax.axis_index("phase") == 1


def rows_of():
    z, x = here()
    first = (z * 4 + x) * ROWS
    return first, first + lax.broadcasted_iota(jnp.int32, (ROWS, 1), 0)


def open_kernel(
    n_ref, gauge_ref, lin_ref, total_ref, gain_ref, rows_ref, own_hbm, near_hbm, far_hbm,
    q_ref, acc_ref, top_hbm, stat_ref, kv_ref, mask_ref, top_ref, sems,
):
    @pl.when(in_softmax_phase())
    def _():
        n1, n2 = n_ref[0], n_ref[1]
        first, positions = rows_of()
        begin = start_of(positions, n1, n2)
        copies = [
            pltpu.make_async_copy(src, kv_ref.at[i], sems.at[i]) for i, src in enumerate((own_hbm, near_hbm, far_hbm))
        ]
        for copy in copies:
            copy.start()
        scale = scale_of(total_ref)
        q_most = 1.02 * jnp.max(scale * scale * rows_ref[0:1, :])
        safe = q_most * gauge_ref[0] < (SAFE / FACTOR) ** 2
        stat_ref[0] = q_most
        stat_ref[1] = jnp.where(safe, 1.0, 0.0)

        @pl.when(safe)
        def _():
            make_queries(lin_ref, total_ref, gain_ref, q_ref, True)
            make_mask(mask_ref, block_of(0), first, begin)
            for copy in copies:
                copy.wait()
            kk = jnp.concatenate([kv_ref[0, :ROWS]] * 2, 1)
            v = ones_beside(kv_ref[0, ROWS:])
            half = ROWS // 2

            def diagonal(h):
                for r in range(2):
                    rows, span = slice(r * half, (r + 1) * half), (r + 1) * half
                    s = dot(q_ref[h, rows, :], kk[:span], NT) + mask_ref[rows, :span]
                    acc_ref[h, rows, :] = dot(jnp.exp2(s).astype(jnp.bfloat16), v[:span])
            each_head(diagonal)
            bounded_tiles((1, 3), kv_ref, 0, n1, n2, q_ref, acc_ref, lambda slot: None)

        @pl.when(jnp.logical_not(safe))
        def _():
            make_queries(lin_ref, total_ref, gain_ref, q_ref, False)
            acc_ref[...] = jnp.zeros_like(acc_ref)
            top_ref[...] = jnp.full(top_ref.shape, FAR, jnp.float32)
            for copy in copies:
                copy.wait()

            def step(slot, carry):
                pl.when(active(slot, n1, n2))(
                    lambda: any_tile(kv_ref, slot, 0, first, begin, q_ref, acc_ref, mask_ref, top_ref)
                )
                return carry

            lax.fori_loop(0, 3, step, 0)
            copy = pltpu.make_async_copy(top_ref, top_hbm, sems.at[0])
            copy.start()
            copy.wait()


def close_kernel(n_ref, stat_ref, lin_ref, total_ref, gain_ref, q_ref, part_ref, top_hbm, *refs):
    kv_hbm, (out_hbm, kv_ref, raw_ref, acc_ref, mask_ref, top_ref, norm_ref, out_ref, kv_sems, out_sems) = refs[:3], refs[3:]

    @pl.when(jnp.logical_not(in_softmax_phase()))
    def _():
        copy = pltpu.make_async_copy(lin_ref, out_hbm, out_sems.at[0])
        copy.start()
        copy.wait()

    @pl.when(in_softmax_phase())
    def _():
        close(
            n_ref, stat_ref, lin_ref, total_ref, gain_ref, q_ref, part_ref, top_hbm, kv_hbm,
            out_hbm, kv_ref, raw_ref, acc_ref, mask_ref, top_ref, norm_ref, out_ref, kv_sems, out_sems,
        )


def close(
    n_ref, stat_ref, lin_ref, total_ref, gain_ref, q_ref, part_ref, top_hbm, kv_hbm,
    out_hbm, kv_ref, raw_ref, acc_ref, mask_ref, top_ref, norm_ref, out_ref, kv_sems, out_sems,
):
    n1, n2 = n_ref[0], n_ref[1]
    base = 3

    def fetch(slot):
        src = kv_hbm[(slot - base) // 2].at[pl.ds((slot - base) % 2 * 2 * ROWS, 2 * ROWS)]
        return pltpu.make_async_copy(src, kv_ref.at[slot - base], kv_sems.at[slot - base])

    def arrived(slot):
        place = kv_ref.at[slot - base]
        pltpu.make_async_copy(place, place, kv_sems.at[slot - base]).wait()

    for slot in range(base, SLOTS):
        pl.when(active(slot, n1, n2))(lambda: fetch(slot).start())
    acc_ref[...] = part_ref[...]
    norm_ref[...] = jnp.zeros_like(norm_ref)
    opened_safe = stat_ref[1] > 0.5

    def before_use(slot):
        arrived(slot)
        norm_ref[...] = jnp.maximum(norm_ref[...], key_norm(kv_ref, slot - base))

    @pl.when(opened_safe)
    def _():
        bounded_tiles((base, SLOTS), kv_ref, base, n1, n2, q_ref, acc_ref, before_use)

    @pl.when(jnp.logical_not(opened_safe))
    def _():
        for slot in range(base, SLOTS):
            pl.when(active(slot, n1, n2))(lambda: arrived(slot))

    safe = opened_safe & (stat_ref[0] * jnp.max(norm_ref[...]) < (SAFE / FACTOR) ** 2)

    @pl.when(jnp.logical_not(safe))
    def _():
        first, positions = rows_of()
        begin = start_of(positions, n1, n2)
        make_queries(lin_ref, total_ref, gain_ref, raw_ref, False)
        acc_ref[...] = part_ref[...]
        top_ref[...] = jnp.zeros_like(top_ref)

        @pl.when(jnp.logical_not(opened_safe))
        def _():
            copy = pltpu.make_async_copy(top_hbm, top_ref, kv_sems.at[0])
            copy.start()
            copy.wait()

        def step(slot, carry):
            pl.when(active(slot, n1, n2))(
                lambda: any_tile(kv_ref, slot, base, first, begin, raw_ref, acc_ref, mask_ref, top_ref)
            )
            return carry

        lax.fori_loop(base, SLOTS, step, 0)

    copies = []
    for h in range(HEADS):
        lanes = slice(h * DH, (h + 1) * DH)
        out_ref[:, lanes] = (acc_ref[h, :, :DH] / acc_ref[h, :, DH:]).astype(jnp.bfloat16)
        copies.append(pltpu.make_async_copy(out_ref.at[:, lanes], out_hbm.at[:, lanes], out_sems.at[h]))
        copies[-1].start()
    for copy in copies:
        copy.wait()


VMEM = pl.BlockSpec(memory_space=pltpu.VMEM)
SMEM = pl.BlockSpec(memory_space=pltpu.SMEM)
ANY = pl.BlockSpec(memory_space=pl.ANY)


def call(kernel, outs, out_specs, args, in_specs, scratch, flops, limit):
    return pl.pallas_call(
        kernel,
        out_shape=tuple(outs),
        in_specs=in_specs,
        out_specs=tuple(out_specs),
        scratch_shapes=scratch,
        compiler_params=pltpu.CompilerParams(vmem_limit_bytes=limit << 20),
        cost_estimate=pl.CostEstimate(flops=flops, bytes_accessed=0, transcendentals=0),
    )(*args)


def shape(dims, dtype=jnp.float32):
    return jax.ShapeDtypeStruct(dims, dtype)


def stash(chunk):
    return call(stash_kernel, [shape(chunk.shape)], [VMEM], (chunk,), [ANY], [pltpu.SemaphoreType.DMA], 0, 4)[0]


def row_sum(parts):
    return call(row_sum_kernel, [shape((QUARTER, DH))], [VMEM], tuple(parts), [VMEM] * 4, [], 0, 8)[0]


def priors_of(parts, near, far):
    return call(
        prior_kernel, [shape((QUARTER, DH))] * 4, [VMEM] * 4, tuple(parts) + (near, far), [VMEM] * 6, [], 1000000000, 8
    )


def pack(own_kv, near_kv, far_kv):
    return call(
        pack_kernel,
        [shape((4 * ROWS, DH), own_kv.dtype)] * 3,
        [ANY] * 3,
        (own_kv, near_kv, far_kv),
        [ANY] * 3,
        [pltpu.SemaphoreType.DMA((6,))],
        5000000000,
        4,
    )


def states(doc_ids, key_feats, values, keys_soft, values_soft):
    bf16 = jnp.bfloat16
    return call(
        states_kernel,
        [shape((QUARTER, DH))] * 4 + [shape((2 * ROWS, DH), bf16), shape((8,), jnp.int32)],
        [VMEM] * 5 + [SMEM],
        (doc_ids.reshape(-1, DH), key_feats, values, keys_soft, values_soft),
        [ANY] * 5,
        [
            pltpu.VMEM((HEADS * FEATS, DH), jnp.float32),
            pltpu.VMEM((doc_ids.shape[0] // DH, DH), jnp.int32),
            pltpu.VMEM((ROWS, DH), bf16),
            pltpu.VMEM((ROWS, WIDE), bf16),
            pltpu.SemaphoreType.DMA((5,)),
        ],
        0,
        60,
    )


def local_part(counts, query_feats, key_feats, values):
    bf16 = jnp.bfloat16
    return call(
        local_kernel,
        [shape((ROWS, WIDE)), shape((ROWS, DH)), shape((ROWS, HEADS * 256), bf16), shape((ROWS, HEADS * 256), bf16)],
        [VMEM] * 4,
        (counts, query_feats, key_feats, values),
        [SMEM] + [VMEM] * 3,
        [pltpu.VMEM((ROWS, ROWS), jnp.float32)],
        0,
        24,
    )


def finish(counts, feats_hi, feats_lo, num, den, parts):
    return call(
        finish_kernel,
        [shape((ROWS, WIDE), jnp.bfloat16), shape((1, ROWS))],
        [VMEM] * 2,
        (counts, feats_hi, feats_lo, num, den) + tuple(parts),
        [SMEM] + [VMEM] * 8,
        [pltpu.VMEM((HEADS * FEATS, DH), jnp.float32)],
        8000000000,
        20,
    )


def gauge(counts, linear_out, gain, own_kv, near_kv, far_kv):
    return call(
        gauge_kernel,
        [shape((8, ROWS)), shape((8,))],
        [VMEM, SMEM],
        (counts, linear_out, gain, own_kv, near_kv, far_kv),
        [SMEM] + [VMEM] * 5,
        [],
        0,
        8,
    )


def soft_open(counts, gauged, linear_out, total, gain, rows, own_kv, near_kv, far_kv):
    bf16 = jnp.bfloat16
    return call(
        open_kernel,
        [shape((HEADS, ROWS, 256), bf16), shape((HEADS, ROWS, 256)), shape((HEADS, ROWS, DH)), shape((8,))],
        [VMEM, VMEM, ANY, SMEM],
        (counts, gauged, linear_out, total, gain, rows, own_kv, near_kv, far_kv),
        [SMEM] * 2 + [VMEM] * 4 + [ANY] * 3,
        [
            pltpu.VMEM((3, 2 * ROWS, DH), bf16),
            pltpu.VMEM((ROWS, ROWS), jnp.float32),
            pltpu.VMEM((HEADS, ROWS, DH), jnp.float32),
            pltpu.SemaphoreType.DMA((3,)),
        ],
        0,
        28,
    )


def soft_close(counts, stat, linear_out, total, gain, queries, part, top, pieces):
    bf16 = jnp.bfloat16
    return call(
        close_kernel,
        [shape((ROWS, WIDE), bf16)],
        [ANY],
        (counts, stat, linear_out, total, gain, queries, part, top) + tuple(pieces),
        [SMEM] * 2 + [VMEM] * 5 + [ANY] * 4,
        [
            pltpu.VMEM((SLOTS - 3, 2 * ROWS, DH), bf16),
            pltpu.VMEM((HEADS, ROWS, 256), bf16),
            pltpu.VMEM((HEADS, ROWS, 256), jnp.float32),
            pltpu.VMEM((ROWS, ROWS), jnp.float32),
            pltpu.VMEM((HEADS, ROWS, DH), jnp.float32),
            pltpu.VMEM((ROWS, 1), jnp.float32),
            pltpu.VMEM((ROWS, WIDE), bf16),
            pltpu.SemaphoreType.DMA((SLOTS - 3,)),
            pltpu.SemaphoreType.DMA((HEADS,)),
        ],
        0,
        32,
    )[0]


def shift(x, axis, by):
    size = lax.axis_size(axis)
    return lax.ppermute(x, axis, [(i, (i + by) % size) for i in range(size)])


def after(x, *others):
    return lax.optimization_barrier((x,) + others)[0]


def local(query_feats, key_feats, values, keys_soft, values_soft, norm_gain, doc_ids):
    zs = lax.axis_size("z")
    *chunks, own_kv, counts = states(doc_ids, key_feats, values, keys_soft, values_soft)

    parts = [stash(chunks[0])] + [shift(chunks[s], "x", s) for s in (1, 2, 3)]

    near_kv = lax.ppermute(own_kv, ("phase", "z"), [(zs + i, zs + i + 1) for i in range(zs - 1)])
    far_kv = lax.ppermute(own_kv, ("phase", "z"), [(i, zs + i + 2) for i in range(zs - 2)])

    local_sums = local_part(counts, query_feats, key_feats, values)
    total = row_sum(parts)
    near = lax.ppermute(total, "z", [(i, i + 1) for i in range(zs - 1)])
    far = lax.ppermute(
        total,
        ("phase", "z"),
        [((1 - p) * zs + i, p * zs + i + 2) for p in range(2) for i in range(zs - 2)],
    )

    messages = lax.optimization_barrier((total,) + tuple(pack(own_kv, near_kv, far_kv)))[1:]
    others = [
        lax.ppermute(message, ("phase", "x"), [(4 + i, 4 + (i + s) % 4) for i in range(4)])
        for s, message in zip((1, 2, 3), messages)
    ]

    near = after(near, *local_sums)
    priors = priors_of(parts, near, far)
    arrived = [priors[0]] + [shift(priors[s], "x", s) for s in (1, 2, 3)]
    num, den, feats_hi, feats_lo = local_sums
    linear_out, squares = finish(counts, feats_hi, feats_lo, num, den, arrived)
    total = squares + shift(squares, "core", 1)
    gain = norm_gain[None]
    rows, gauged = gauge(counts, linear_out, gain, own_kv, near_kv, far_kv)
    total = total + lax.ppermute(total, "y", list(enumerate((1, 0, 3, 2))))
    total = after(total, rows)
    total = total + lax.ppermute(total, "y", list(enumerate((3, 2, 1, 0))))
    queries, part, top, stat = soft_open(counts, gauged, linear_out, total, gain, rows, own_kv, near_kv, far_kv)
    return soft_close(counts, stat, linear_out, total, gain, queries, part, top, others)[None]


def solution(mesh):
    fine = Mesh(mesh.devices.reshape(2, 4, 4, 4, 2), ("phase", "z", "x", "y", "core"))
    seq, head = ("z", "x"), ("y", "core")
    return jax.shard_map(
        local,
        mesh=fine,
        in_specs=(
            P(seq, head),
            P(seq, head),
            P(seq, head),
            P(seq, head),
            P(seq, head),
            P(head),
            P(),
        ),
        out_specs=P("phase", seq, head),
        check_vma=False,
    )
```

```python
import math

import jax
import jax.numpy as jnp
from jax import lax
from jax.experimental import pallas as pl
from jax.experimental.pallas import tpu as pltpu
from jax.sharding import Mesh, PartitionSpec as P

DH = 128
F = 16
ROWS = 512
HEADS = 8
WIDE = HEADS * DH
ALL_WIDE = 64 * DH
USED = (F + 1) * (F + 2) // 2
FEATS = 160
QUARTER = HEADS * FEATS // 4
SLOTS = 9
DOC_ROW = USED + 2
LOG2E = math.log2(math.e)
FACTOR = LOG2E / math.sqrt(DH)
SAFE = 110.0
FAR = -1e30

NN = (((1,), (0,)), ((), ()))
NT = (((1,), (1,)), ((), ()))


def dot(a, b, dims=NN):
    return lax.dot_general(a, b, dims, preferred_element_type=jnp.float32)


def split(x):
    hi = x.astype(jnp.bfloat16)
    lo = (x - hi.astype(jnp.float32)).astype(jnp.bfloat16)
    return hi, lo


def doc_of(position, n1, n2):
    return (position >= n1).astype(jnp.int32) + (position >= n2).astype(jnp.int32)


def start_of(position, n1, n2):
    return jnp.where(position >= n2, n2, jnp.where(position >= n1, n1, 0))


def pair_of(e):
    gap = jnp.zeros_like(e)
    for k in range(1, F // 2 + 1):
        gap = gap + (e >= k * (F + 1)).astype(jnp.int32)
    m = e - gap * (F + 1)
    n = m + gap
    n = jnp.where(n > F, n - (F + 1), n)
    times = jnp.where((gap == 0) & (m < F), 1.0, 2.0)
    times = jnp.where(e < USED, times, 0.0)
    return m, n, times


def here():
    return lax.axis_index("z"), lax.axis_index("x")


def row_block(x, s):
    return lax.rem(x - s + 4, 4)


def same(a, b):
    return (a == b).astype(jnp.float32)


def doc_row(ref):
    return ref[DOC_ROW : DOC_ROW + 1, :]


def row_sum_kernel(p0_ref, p1_ref, p2_ref, p3_ref, out_ref):
    parts = (p0_ref, p1_ref, p2_ref, p3_ref)
    end = doc_row(p0_ref)
    for part in parts[1:]:
        end = jnp.maximum(end, doc_row(part))
    total = jnp.zeros((QUARTER, DH), jnp.float32)
    for part in parts:
        total = total + same(doc_row(part), end) * part[...]
    out_ref[...] = total
    out_ref[DOC_ROW : DOC_ROW + 1, :] = end


def prior_kernel(p0_ref, p1_ref, p2_ref, p3_ref, near_ref, far_ref, *outs):
    z, x = here()
    parts = (p0_ref, p1_ref, p2_ref, p3_ref)
    before = doc_row(near_ref)
    incoming = near_ref[...] + same(doc_row(far_ref), before) * far_ref[...]
    for t, out in enumerate(outs):
        target = lax.rem(x + t, 4)
        doc = before
        for s, part in enumerate(parts):
            doc = jnp.where(row_block(x, s) == target - 1, doc_row(part), doc)
        prior = same(before, doc) * incoming
        for s, part in enumerate(parts):
            use = jnp.where(row_block(x, s) < target, same(doc_row(part), doc), 0.0)
            prior = prior + use * part[...]
        out[...] = prior


def stash_kernel(src_hbm, out_ref, sem):
    copy = pltpu.make_async_copy(src_hbm, out_ref, sem)
    copy.start()
    copy.wait()


def pack_kernel(own_hbm, near_hbm, far_hbm, o1_hbm, o2_hbm, o3_hbm, sems):
    z, x = here()
    upper, lower = pl.ds(0, 2 * ROWS), pl.ds(2 * ROWS, 2 * ROWS)
    for s, out in enumerate((o1_hbm, o2_hbm, o3_hbm)):
        later = lax.rem(x + s + 1, 4) > x
        pltpu.make_async_copy(near_hbm, out.at[upper], sems.at[s]).start()
        pl.when(later)(lambda: pltpu.make_async_copy(own_hbm, out.at[lower], sems.at[3 + s]).start())
        pl.when(jnp.logical_not(later))(lambda: pltpu.make_async_copy(far_hbm, out.at[lower], sems.at[3 + s]).start())
    for s, out in enumerate((o1_hbm, o2_hbm, o3_hbm)):
        pltpu.make_async_copy(near_hbm, out.at[upper], sems.at[s]).wait()
        pltpu.make_async_copy(own_hbm, out.at[lower], sems.at[3 + s]).wait()


def states_kernel(doc_hbm, kf_hbm, v_hbm, k_hbm, vs_hbm, c0_ref, c1_ref, c2_ref, c3_ref, kv_ref, n_ref, state_ref, doc_ref, kf_ref, v_ref, sems):
    pairs = [(doc_hbm, doc_ref), (kf_hbm, kf_ref), (v_hbm, v_ref), (k_hbm, kv_ref.at[:ROWS]), (vs_hbm, kv_ref.at[ROWS:])]
    copies = [pltpu.make_async_copy(src, dst, sems.at[i]) for i, (src, dst) in enumerate(pairs)]
    for copy in copies:
        copy.start()
    z, x = here()
    first = (z * 4 + x) * ROWS
    m, n, times = pair_of(lax.broadcasted_iota(jnp.int32, (FEATS, 2 * F), 0))
    col = lax.broadcasted_iota(jnp.int32, (FEATS, 2 * F), 1)
    e1 = ((col == m) & (times > 0)).astype(jnp.float32).astype(jnp.bfloat16)
    e2 = ((col == n) & (times > 0)).astype(jnp.float32).astype(jnp.bfloat16)
    e12 = jnp.concatenate([e1, e2], 0)
    lane = lax.broadcasted_iota(jnp.int32, (ROWS, DH), 1)
    norms = jnp.zeros((FEATS, DH), jnp.float32)
    copies[0].wait()
    n1 = jnp.sum((doc_ref[...] < 1).astype(jnp.int32))
    n2 = jnp.sum((doc_ref[...] < 2).astype(jnp.int32))
    n_ref[0] = n1
    n_ref[1] = n2
    pos = first + lax.broadcasted_iota(jnp.int32, (F, ROWS), 1)
    sel = (doc_of(pos, n1, n2) == doc_of(first + ROWS - 1, n1, n2)).astype(jnp.float32)
    copies[1].wait()
    kt = kf_ref[...].astype(jnp.float32).T
    copies[2].wait()
    for h in range(HEADS):
        rows = jnp.concatenate([kt[h * F : (h + 1) * F] * sel, sel], 0).astype(jnp.bfloat16)
        both = dot(e12, rows)
        hi, lo = split(both[:FEATS] * both[FEATS:])
        unit = (lane == h).astype(jnp.bfloat16)
        rhs = jnp.concatenate([v_ref[:, h * DH : (h + 1) * DH], unit], 1)
        res = dot(jnp.concatenate([hi, lo], 0), rhs)
        res = res[:FEATS] + res[FEATS:]
        state_ref[h * FEATS : (h + 1) * FEATS, :] = res[:, :DH]
        norms = norms + res[:, DH:]
    across = norms.T
    for h in range(HEADS):
        base = h * FEATS + USED
        state_ref[base : base + 1, :] = across[h : h + 1, :DH]
        state_ref[base + 1 : base + 2, : FEATS - DH] = across[h : h + 1, DH:]
        last = doc_of(first + ROWS - 1, n1, n2).astype(jnp.float32)
        state_ref[base + 2 : base + 3, :] = jnp.full((1, DH), last, jnp.float32)
    for s, out in enumerate((c0_ref, c1_ref, c2_ref, c3_ref)):
        chunk = lax.rem(x + s, 4)
        out[...] = state_ref[pl.ds(pl.multiple_of(chunk * QUARTER, QUARTER), QUARTER), :]
    copies[3].wait()
    copies[4].wait()


def local_kernel(n_ref, qf_ref, kf_ref, v_ref, num_ref, den_ref, hi_ref, lo_ref, mask_ref):
    n1, n2 = n_ref[0], n_ref[1]
    z, x = here()
    first = (z * 4 + x) * ROWS
    row = lax.broadcasted_iota(jnp.int32, (ROWS, ROWS), 0)
    col = lax.broadcasted_iota(jnp.int32, (ROWS, ROWS), 1)
    begin = start_of(first + lax.broadcasted_iota(jnp.int32, (ROWS, 1), 0), n1, n2) - first
    mask_ref[...] = ((col <= row) & (col >= begin)).astype(jnp.float32)
    lane = lax.broadcasted_iota(jnp.int32, (ROWS, DH), 1)
    one = (lane == 0).astype(jnp.bfloat16)
    kf = jnp.concatenate([kf_ref[...], one], 1)
    half = ROWS // 2
    dens = [jnp.zeros((half, DH), jnp.float32) for _ in range(2)]
    for h in range(HEADS):
        qh = jnp.where(lane // F == h, qf_ref[...], jnp.zeros((), jnp.bfloat16))
        qh = jnp.concatenate([qh, one], 1)
        unit = (lane == h).astype(jnp.bfloat16)
        rhs = jnp.concatenate([v_ref[:, h * DH : (h + 1) * DH], unit], 1)
        for r in range(2):
            span = (r + 1) * half
            s = dot(qh[r * half : (r + 1) * half], kf[:span], NT)
            w = (s * s + 1.0) * mask_ref[r * half : (r + 1) * half, :span]
            hi, lo = split(w)
            res = dot(hi, rhs[:span]) + dot(lo, rhs[:span])
            num_ref[r * half : (r + 1) * half, h * DH : (h + 1) * DH] = res[:, :DH]
            dens[r] = dens[r] + res[:, DH:]
    for r in range(2):
        den_ref[r * half : (r + 1) * half, :] = dens[r]
    m, n, times = pair_of(lax.broadcasted_iota(jnp.int32, (DH, 256), 1))
    lane_row = lax.broadcasted_iota(jnp.int32, (DH, 256), 0)
    m1, n1_, times1 = pair_of(lax.broadcasted_iota(jnp.int32, (1, 256), 1))
    ones_a = jnp.where(m1 == F, times1, 0.0)
    ones_b = jnp.where((n1_ == F) & (times1 > 0), 1.0, 0.0)
    once = (times > 0).astype(jnp.float32)
    q = qf_ref[...]
    for h in range(HEADS):
        e1 = jnp.where((lane_row == m + h * F) & (m < F), times, 0.0).astype(jnp.bfloat16)
        e2 = jnp.where((lane_row == n + h * F) & (n < F), once, 0.0).astype(jnp.bfloat16)
        hi, lo = split((dot(q, e1) + ones_a) * (dot(q, e2) + ones_b))
        hi_ref[:, h * 256 : (h + 1) * 256] = hi
        lo_ref[:, h * 256 : (h + 1) * 256] = lo


def finish_kernel(n_ref, hi_ref, lo_ref, num_ref, den_ref, p0_ref, p1_ref, p2_ref, p3_ref, out_ref, sq_ref, prior_ref):
    n1, n2 = n_ref[0], n_ref[1]
    z, x = here()
    first = (z * 4 + x) * ROWS
    pos = first + lax.broadcasted_iota(jnp.int32, (ROWS, 1), 0)
    usable = ((doc_of(pos, n1, n2) == doc_of(first - 1, n1, n2)) & (first > 0)).astype(jnp.float32)
    for s, part in enumerate((p0_ref, p1_ref, p2_ref, p3_ref)):
        chunk = lax.rem(x - s + 4, 4)
        prior_ref[pl.ds(pl.multiple_of(chunk * QUARTER, QUARTER), QUARTER), :] = part[...]
    spare = [jnp.zeros((DH - HEADS, DH), jnp.float32)]
    sums = [[prior_ref[h * FEATS + USED + i : h * FEATS + USED + i + 1, :] for h in range(HEADS)] for i in range(2)]
    norm = jnp.concatenate([jnp.concatenate(rows + spare, 0).T for rows in sums], 0)[:FEATS]
    norm_hi, norm_lo = split(norm)
    squares = jnp.zeros((ROWS, DH), jnp.float32)
    for h in range(HEADS):
        hi = hi_ref[:, h * 256 : h * 256 + FEATS]
        lo = lo_ref[:, h * 256 : h * 256 + FEATS]
        s_hi, s_lo = split(prior_ref[h * FEATS : (h + 1) * FEATS, :])
        r_hi = jnp.concatenate([s_hi, norm_hi], 1)
        r_lo = jnp.concatenate([s_lo, norm_lo], 1)
        res = dot(jnp.concatenate([hi, lo], 0), r_hi)
        res = (res[:ROWS] + (res[ROWS:] + dot(hi, r_lo))) * usable
        num = num_ref[:, h * DH : (h + 1) * DH] + res[:, :DH]
        den = den_ref[:, h : h + 1] + res[:, DH + h : DH + h + 1]
        out = (num / den).astype(jnp.bfloat16)
        out_ref[:, h * DH : (h + 1) * DH] = out
        wide = out.astype(jnp.float32)
        squares = squares + wide * wide
    sq_ref[...] = jnp.sum(squares.T, 0, keepdims=True)


def block_of(slot):
    z, x = here()
    src = lax.rem(x + 4 - lax.div(slot - 1, 2), 4)
    behind = jnp.where(lax.rem(slot, 2) == 1, 1, jnp.where(src < x, 0, 2))
    return jnp.where(slot < 3, z * 4 + x - 4 * slot, (z - behind) * 4 + src)


def active(slot, n1, n2):
    z, x = here()
    own = z * 4 + x
    low = start_of(own * ROWS, n1, n2) // ROWS
    return (block_of(slot) >= low) & (block_of(slot) < own) | (slot == 0)


def key_norm(kv_ref, place):
    k = kv_ref[place, :ROWS].astype(jnp.float32)
    return jnp.sum(k * k, 1, keepdims=True)


def gauge_kernel(n_ref, lin_ref, gain_ref, own_ref, near_ref, far_ref, rows_ref, stat_ref):
    most = jnp.zeros((ROWS, 1), jnp.float32)
    for h in range(HEADS):
        lanes = slice(h * DH, (h + 1) * DH)
        q = lin_ref[:, lanes].astype(jnp.float32) * gain_ref[0:1, lanes]
        most = jnp.maximum(most, jnp.sum(q * q, 1, keepdims=True))
    rows_ref[...] = jnp.broadcast_to(most, (ROWS, DH)).T[:8]
    stat_ref[0] = 0.0
    for slot, kv_ref in enumerate((own_ref, near_ref, far_ref)):
        k = kv_ref[:ROWS].astype(jnp.float32)
        norm = jnp.max(jnp.sum(k * k, 1, keepdims=True))
        stat_ref[0] = jnp.where(active(slot, n_ref[0], n_ref[1]), jnp.maximum(stat_ref[0], norm), stat_ref[0])


def scale_of(total_ref):
    return lax.rsqrt(total_ref[...] / ALL_WIDE + 1e-06)


def make_queries(lin_ref, total_ref, gain_ref, q_ref, double):
    scale = jnp.broadcast_to(scale_of(total_ref), (DH, ROWS)).T
    for h in range(HEADS):
        lanes = slice(h * DH, (h + 1) * DH)
        q = (lin_ref[:, lanes].astype(jnp.float32) * scale * gain_ref[0:1, lanes]).astype(jnp.bfloat16)
        lo = jnp.zeros((ROWS, DH), jnp.bfloat16)
        if double:
            q, lo = split(q.astype(jnp.float32) * FACTOR)
        q_ref[h, :, :DH] = q
        q_ref[h, :, DH:] = lo


def ones_beside(v):
    return jnp.concatenate([v, jnp.ones((ROWS, DH), jnp.bfloat16)], 1)


def bounded_tile(kv_ref, place, slot, begin_first, q_ref, acc_ref, keep):
    kk = jnp.concatenate([kv_ref[place, :ROWS]] * 2, 1)
    key = block_of(slot) * ROWS + lax.broadcasted_iota(jnp.int32, (ROWS, 256), 0)
    inside = (key >= begin_first).astype(jnp.float32).astype(jnp.bfloat16)
    v = ones_beside(kv_ref[place, ROWS:]) * inside
    for h in range(HEADS):
        p = jnp.exp2(dot(q_ref[h], kk, NT)).astype(jnp.bfloat16)
        res = dot(p, v)
        acc_ref[h] += res if keep is None else res * keep


def bounded_tiles(slots, kv_ref, base, n1, n2, q_ref, acc_ref, before_use, forms=2):
    first, positions = rows_of()
    begin_first = start_of(first, n1, n2)
    mixed = start_of(first + ROWS - 1, n1, n2) != begin_first

    def run(keep):
        def one(slot):
            before_use(slot)
            bounded_tile(kv_ref, slot - base, slot, begin_first, q_ref, acc_ref, keep)

        def step(slot, carry):
            pl.when(active(slot, n1, n2))(lambda: one(slot))
            return carry

        lax.fori_loop(*slots, step, 0)

    keep = (start_of(positions, n1, n2) == begin_first).astype(jnp.float32)
    if forms == 1:
        run(keep)
    else:
        pl.when(jnp.logical_not(mixed))(lambda: run(None))
        pl.when(mixed)(lambda: run(keep))


def make_mask(mask_ref, block, first, begin):
    row = lax.broadcasted_iota(jnp.int32, (ROWS, ROWS), 0)
    key = block * ROWS + lax.broadcasted_iota(jnp.int32, (ROWS, ROWS), 1)
    mask_ref[...] = jnp.where((key >= begin) & (key <= first + row), 0.0, FAR)


def any_tile(kv_ref, slot, base, first, begin, q_ref, acc_ref, mask_ref, top_ref):
    make_mask(mask_ref, block_of(slot), first, begin)
    kk = jnp.concatenate([kv_ref[slot - base, :ROWS]] * 2, 1)
    v = ones_beside(kv_ref[slot - base, ROWS:])

    def head(h, carry):
        s = jnp.maximum(dot(q_ref[h], kk, NT) * FACTOR + mask_ref[...], FAR)
        old = top_ref[h]
        new = jnp.maximum(old, jnp.max(s, 1, keepdims=True))
        p = jnp.exp2(s - jnp.concatenate([new] * 4, 1)).astype(jnp.bfloat16)
        fade = jnp.exp2(old - new)
        acc_ref[h] = acc_ref[h] * jnp.concatenate([fade] * 2, 1) + dot(p, v)
        top_ref[h] = new
        return carry

    lax.fori_loop(0, HEADS, head, 0)


def in_softmax_phase():
    return lax.axis_index("phase") == 1


def rows_of():
    z, x = here()
    first = (z * 4 + x) * ROWS
    return first, first + lax.broadcasted_iota(jnp.int32, (ROWS, 1), 0)


def open_kernel(
    n_ref, gauge_ref, lin_ref, total_ref, gain_ref, rows_ref, own_hbm, near_hbm, far_hbm,
    q_ref, acc_ref, top_hbm, stat_ref, kv_ref, mask_ref, top_ref, sems,
):
    @pl.when(in_softmax_phase())
    def _():
        n1, n2 = n_ref[0], n_ref[1]
        first, positions = rows_of()
        begin = start_of(positions, n1, n2)
        copies = [
            pltpu.make_async_copy(src, kv_ref.at[i], sems.at[i]) for i, src in enumerate((own_hbm, near_hbm, far_hbm))
        ]
        for copy in copies:
            copy.start()
        scale = scale_of(total_ref)
        q_most = 1.02 * jnp.max(scale * scale * rows_ref[0:1, :])
        safe = q_most * gauge_ref[0] < (SAFE / FACTOR) ** 2
        stat_ref[0] = q_most
        stat_ref[1] = jnp.where(safe, 1.0, 0.0)

        @pl.when(safe)
        def _():
            make_queries(lin_ref, total_ref, gain_ref, q_ref, True)
            make_mask(mask_ref, block_of(0), first, begin)
            for copy in copies:
                copy.wait()
            kk = jnp.concatenate([kv_ref[0, :ROWS]] * 2, 1)
            v = ones_beside(kv_ref[0, ROWS:])
            half = ROWS // 2
            for h in range(HEADS):
                for r in range(2):
                    rows, span = slice(r * half, (r + 1) * half), (r + 1) * half
                    s = dot(q_ref[h, rows, :], kk[:span], NT) + mask_ref[rows, :span]
                    acc_ref[h, rows, :] = dot(jnp.exp2(s).astype(jnp.bfloat16), v[:span])
            bounded_tiles((1, 3), kv_ref, 0, n1, n2, q_ref, acc_ref, lambda slot: None, forms=1)

        @pl.when(jnp.logical_not(safe))
        def _():
            make_queries(lin_ref, total_ref, gain_ref, q_ref, False)
            acc_ref[...] = jnp.zeros_like(acc_ref)
            top_ref[...] = jnp.full(top_ref.shape, FAR, jnp.float32)
            for copy in copies:
                copy.wait()

            def step(slot, carry):
                pl.when(active(slot, n1, n2))(
                    lambda: any_tile(kv_ref, slot, 0, first, begin, q_ref, acc_ref, mask_ref, top_ref)
                )
                return carry

            lax.fori_loop(0, 3, step, 0)
            copy = pltpu.make_async_copy(top_ref, top_hbm, sems.at[0])
            copy.start()
            copy.wait()


def close_kernel(n_ref, stat_ref, lin_ref, total_ref, gain_ref, q_ref, part_ref, top_hbm, *refs):
    kv_hbm, (out_hbm, kv_ref, raw_ref, acc_ref, mask_ref, top_ref, norm_ref, out_ref, kv_sems, out_sems) = refs[:3], refs[3:]

    @pl.when(jnp.logical_not(in_softmax_phase()))
    def _():
        copy = pltpu.make_async_copy(lin_ref, out_hbm, out_sems.at[0])
        copy.start()
        copy.wait()

    @pl.when(in_softmax_phase())
    def _():
        close(
            n_ref, stat_ref, lin_ref, total_ref, gain_ref, q_ref, part_ref, top_hbm, kv_hbm,
            out_hbm, kv_ref, raw_ref, acc_ref, mask_ref, top_ref, norm_ref, out_ref, kv_sems, out_sems,
        )


def close(
    n_ref, stat_ref, lin_ref, total_ref, gain_ref, q_ref, part_ref, top_hbm, kv_hbm,
    out_hbm, kv_ref, raw_ref, acc_ref, mask_ref, top_ref, norm_ref, out_ref, kv_sems, out_sems,
):
    n1, n2 = n_ref[0], n_ref[1]
    base = 3

    def fetch(slot):
        src = kv_hbm[(slot - base) // 2].at[pl.ds((slot - base) % 2 * 2 * ROWS, 2 * ROWS)]
        return pltpu.make_async_copy(src, kv_ref.at[slot - base], kv_sems.at[slot - base])

    def arrived(slot):
        place = kv_ref.at[slot - base]
        pltpu.make_async_copy(place, place, kv_sems.at[slot - base]).wait()

    for slot in range(base, SLOTS):
        pl.when(active(slot, n1, n2))(lambda: fetch(slot).start())
    acc_ref[...] = part_ref[...]
    norm_ref[...] = jnp.zeros_like(norm_ref)
    opened_safe = stat_ref[1] > 0.5

    def before_use(slot):
        arrived(slot)
        norm_ref[...] = jnp.maximum(norm_ref[...], key_norm(kv_ref, slot - base))

    @pl.when(opened_safe)
    def _():
        bounded_tiles((base, SLOTS), kv_ref, base, n1, n2, q_ref, acc_ref, before_use)

    @pl.when(jnp.logical_not(opened_safe))
    def _():
        for slot in range(base, SLOTS):
            pl.when(active(slot, n1, n2))(lambda: arrived(slot))

    safe = opened_safe & (stat_ref[0] * jnp.max(norm_ref[...]) < (SAFE / FACTOR) ** 2)

    @pl.when(jnp.logical_not(safe))
    def _():
        first, positions = rows_of()
        begin = start_of(positions, n1, n2)
        make_queries(lin_ref, total_ref, gain_ref, raw_ref, False)
        acc_ref[...] = part_ref[...]
        top_ref[...] = jnp.zeros_like(top_ref)

        @pl.when(jnp.logical_not(opened_safe))
        def _():
            copy = pltpu.make_async_copy(top_hbm, top_ref, kv_sems.at[0])
            copy.start()
            copy.wait()

        def step(slot, carry):
            pl.when(active(slot, n1, n2))(
                lambda: any_tile(kv_ref, slot, base, first, begin, raw_ref, acc_ref, mask_ref, top_ref)
            )
            return carry

        lax.fori_loop(base, SLOTS, step, 0)

    copies = []
    for h in range(HEADS):
        lanes = slice(h * DH, (h + 1) * DH)
        out_ref[:, lanes] = (acc_ref[h, :, :DH] / acc_ref[h, :, DH:]).astype(jnp.bfloat16)
        copies.append(pltpu.make_async_copy(out_ref.at[:, lanes], out_hbm.at[:, lanes], out_sems.at[h]))
        copies[-1].start()
    for copy in copies:
        copy.wait()


VMEM = pl.BlockSpec(memory_space=pltpu.VMEM)
SMEM = pl.BlockSpec(memory_space=pltpu.SMEM)
ANY = pl.BlockSpec(memory_space=pl.ANY)


def call(kernel, outs, out_specs, args, in_specs, scratch, flops, limit):
    return pl.pallas_call(
        kernel,
        out_shape=tuple(outs),
        in_specs=in_specs,
        out_specs=tuple(out_specs),
        scratch_shapes=scratch,
        compiler_params=pltpu.CompilerParams(vmem_limit_bytes=limit << 20),
        cost_estimate=pl.CostEstimate(flops=flops, bytes_accessed=0, transcendentals=0),
    )(*args)


def shape(dims, dtype=jnp.float32):
    return jax.ShapeDtypeStruct(dims, dtype)


def stash(chunk):
    return call(stash_kernel, [shape(chunk.shape)], [VMEM], (chunk,), [ANY], [pltpu.SemaphoreType.DMA], 0, 4)[0]


def row_sum(parts):
    return call(row_sum_kernel, [shape((QUARTER, DH))], [VMEM], tuple(parts), [VMEM] * 4, [], 0, 8)[0]


def priors_of(parts, near, far):
    return call(
        prior_kernel, [shape((QUARTER, DH))] * 4, [VMEM] * 4, tuple(parts) + (near, far), [VMEM] * 6, [], 1000000000, 8
    )


def pack(own_kv, near_kv, far_kv):
    return call(
        pack_kernel,
        [shape((4 * ROWS, DH), own_kv.dtype)] * 3,
        [ANY] * 3,
        (own_kv, near_kv, far_kv),
        [ANY] * 3,
        [pltpu.SemaphoreType.DMA((6,))],
        5000000000,
        4,
    )


def states(doc_ids, key_feats, values, keys_soft, values_soft):
    bf16 = jnp.bfloat16
    return call(
        states_kernel,
        [shape((QUARTER, DH))] * 4 + [shape((2 * ROWS, DH), bf16), shape((8,), jnp.int32)],
        [VMEM] * 5 + [SMEM],
        (doc_ids.reshape(-1, DH), key_feats, values, keys_soft, values_soft),
        [ANY] * 5,
        [
            pltpu.VMEM((HEADS * FEATS, DH), jnp.float32),
            pltpu.VMEM((doc_ids.shape[0] // DH, DH), jnp.int32),
            pltpu.VMEM((ROWS, DH), bf16),
            pltpu.VMEM((ROWS, WIDE), bf16),
            pltpu.SemaphoreType.DMA((5,)),
        ],
        0,
        60,
    )


def local_part(counts, query_feats, key_feats, values):
    bf16 = jnp.bfloat16
    return call(
        local_kernel,
        [shape((ROWS, WIDE)), shape((ROWS, DH)), shape((ROWS, HEADS * 256), bf16), shape((ROWS, HEADS * 256), bf16)],
        [VMEM] * 4,
        (counts, query_feats, key_feats, values),
        [SMEM] + [VMEM] * 3,
        [pltpu.VMEM((ROWS, ROWS), jnp.float32)],
        0,
        24,
    )


def finish(counts, feats_hi, feats_lo, num, den, parts):
    return call(
        finish_kernel,
        [shape((ROWS, WIDE), jnp.bfloat16), shape((1, ROWS))],
        [VMEM] * 2,
        (counts, feats_hi, feats_lo, num, den) + tuple(parts),
        [SMEM] + [VMEM] * 8,
        [pltpu.VMEM((HEADS * FEATS, DH), jnp.float32)],
        8000000000,
        20,
    )


def gauge(counts, linear_out, gain, own_kv, near_kv, far_kv):
    return call(
        gauge_kernel,
        [shape((8, ROWS)), shape((8,))],
        [VMEM, SMEM],
        (counts, linear_out, gain, own_kv, near_kv, far_kv),
        [SMEM] + [VMEM] * 5,
        [],
        0,
        8,
    )


def soft_open(counts, gauged, linear_out, total, gain, rows, own_kv, near_kv, far_kv):
    bf16 = jnp.bfloat16
    return call(
        open_kernel,
        [shape((HEADS, ROWS, 256), bf16), shape((HEADS, ROWS, 256)), shape((HEADS, ROWS, DH)), shape((8,))],
        [VMEM, VMEM, ANY, SMEM],
        (counts, gauged, linear_out, total, gain, rows, own_kv, near_kv, far_kv),
        [SMEM] * 2 + [VMEM] * 4 + [ANY] * 3,
        [
            pltpu.VMEM((3, 2 * ROWS, DH), bf16),
            pltpu.VMEM((ROWS, ROWS), jnp.float32),
            pltpu.VMEM((HEADS, ROWS, DH), jnp.float32),
            pltpu.SemaphoreType.DMA((3,)),
        ],
        0,
        28,
    )


def soft_close(counts, stat, linear_out, total, gain, queries, part, top, pieces):
    bf16 = jnp.bfloat16
    return call(
        close_kernel,
        [shape((ROWS, WIDE), bf16)],
        [ANY],
        (counts, stat, linear_out, total, gain, queries, part, top) + tuple(pieces),
        [SMEM] * 2 + [VMEM] * 5 + [ANY] * 4,
        [
            pltpu.VMEM((SLOTS - 3, 2 * ROWS, DH), bf16),
            pltpu.VMEM((HEADS, ROWS, 256), bf16),
            pltpu.VMEM((HEADS, ROWS, 256), jnp.float32),
            pltpu.VMEM((ROWS, ROWS), jnp.float32),
            pltpu.VMEM((HEADS, ROWS, DH), jnp.float32),
            pltpu.VMEM((ROWS, 1), jnp.float32),
            pltpu.VMEM((ROWS, WIDE), bf16),
            pltpu.SemaphoreType.DMA((SLOTS - 3,)),
            pltpu.SemaphoreType.DMA((HEADS,)),
        ],
        0,
        32,
    )[0]


def shift(x, axis, by):
    size = lax.axis_size(axis)
    return lax.ppermute(x, axis, [(i, (i + by) % size) for i in range(size)])


def after(x, *others):
    return lax.optimization_barrier((x,) + others)[0]


def local(query_feats, key_feats, values, keys_soft, values_soft, norm_gain, doc_ids):
    zs = lax.axis_size("z")
    *chunks, own_kv, counts = states(doc_ids, key_feats, values, keys_soft, values_soft)

    parts = [stash(chunks[0])] + [shift(chunks[s], "x", s) for s in (1, 2, 3)]

    near_kv = lax.ppermute(own_kv, ("phase", "z"), [(zs + i, zs + i + 1) for i in range(zs - 1)])
    far_kv = lax.ppermute(own_kv, ("phase", "z"), [(i, zs + i + 2) for i in range(zs - 2)])

    local_sums = local_part(counts, query_feats, key_feats, values)
    total = row_sum(parts)
    near = lax.ppermute(total, "z", [(i, i + 1) for i in range(zs - 1)])
    far = lax.ppermute(
        total,
        ("phase", "z"),
        [((1 - p) * zs + i, p * zs + i + 2) for p in range(2) for i in range(zs - 2)],
    )

    messages = lax.optimization_barrier((total,) + tuple(pack(own_kv, near_kv, far_kv)))[1:]
    others = [
        lax.ppermute(message, ("phase", "x"), [(4 + i, 4 + (i + s) % 4) for i in range(4)])
        for s, message in zip((1, 2, 3), messages)
    ]

    near = after(near, *local_sums)
    priors = priors_of(parts, near, far)
    arrived = [priors[0]] + [shift(priors[s], "x", s) for s in (1, 2, 3)]
    num, den, feats_hi, feats_lo = local_sums
    linear_out, squares = finish(counts, feats_hi, feats_lo, num, den, arrived)
    total = squares + shift(squares, "core", 1)
    gain = norm_gain[None]
    rows, gauged = gauge(counts, linear_out, gain, own_kv, near_kv, far_kv)
    total = total + lax.ppermute(total, "y", list(enumerate((1, 0, 3, 2))))
    total = after(total, rows)
    total = total + lax.ppermute(total, "y", list(enumerate((3, 2, 1, 0))))
    queries, part, top, stat = soft_open(counts, gauged, linear_out, total, gain, rows, own_kv, near_kv, far_kv)
    return soft_close(counts, stat, linear_out, total, gain, queries, part, top, others)[None]


def solution(mesh):
    fine = Mesh(mesh.devices.reshape(2, 4, 4, 4, 2), ("phase", "z", "x", "y", "core"))
    seq, head = ("z", "x"), ("y", "core")
    return jax.shard_map(
        local,
        mesh=fine,
        in_specs=(
            P(seq, head),
            P(seq, head),
            P(seq, head),
            P(seq, head),
            P(seq, head),
            P(head),
            P(),
        ),
        out_specs=P("phase", seq, head),
        check_vma=False,
    )
```

```python
import math

import jax
import jax.numpy as jnp
from jax import lax
from jax.experimental import pallas as pl
from jax.experimental.pallas import tpu as pltpu
from jax.sharding import Mesh, PartitionSpec as P

DH = 128
F = 16
ROWS = 512
HEADS = 8
WIDE = HEADS * DH
ALL_WIDE = 64 * DH
USED = (F + 1) * (F + 2) // 2
FEATS = 160
QUARTER = HEADS * FEATS // 4
SLOTS = 9
DOC_ROW = USED + 2
LOG2E = math.log2(math.e)
FACTOR = LOG2E / math.sqrt(DH)
SAFE = 110.0
FAR = -1e30

NN = (((1,), (0,)), ((), ()))
NT = (((1,), (1,)), ((), ()))


def dot(a, b, dims=NN):
    return lax.dot_general(a, b, dims, preferred_element_type=jnp.float32)


def split(x):
    hi = x.astype(jnp.bfloat16)
    lo = (x - hi.astype(jnp.float32)).astype(jnp.bfloat16)
    return hi, lo


def doc_of(position, n1, n2):
    return (position >= n1).astype(jnp.int32) + (position >= n2).astype(jnp.int32)


def start_of(position, n1, n2):
    return jnp.where(position >= n2, n2, jnp.where(position >= n1, n1, 0))


def pair_of(e):
    gap = jnp.zeros_like(e)
    for k in range(1, F // 2 + 1):
        gap = gap + (e >= k * (F + 1)).astype(jnp.int32)
    m = e - gap * (F + 1)
    n = m + gap
    n = jnp.where(n > F, n - (F + 1), n)
    times = jnp.where((gap == 0) & (m < F), 1.0, 2.0)
    times = jnp.where(e < USED, times, 0.0)
    return m, n, times


def here():
    return lax.axis_index("z"), lax.axis_index("x")


def row_block(x, s):
    return lax.rem(x - s + 4, 4)


def same(a, b):
    return (a == b).astype(jnp.float32)


def doc_row(ref):
    return ref[DOC_ROW : DOC_ROW + 1, :]


def row_sum_kernel(p0_ref, p1_ref, p2_ref, p3_ref, out_ref):
    parts = (p0_ref, p1_ref, p2_ref, p3_ref)
    end = doc_row(p0_ref)
    for part in parts[1:]:
        end = jnp.maximum(end, doc_row(part))
    total = jnp.zeros((QUARTER, DH), jnp.float32)
    for part in parts:
        total = total + same(doc_row(part), end) * part[...]
    out_ref[...] = total
    out_ref[DOC_ROW : DOC_ROW + 1, :] = end


def prior_kernel(p0_ref, p1_ref, p2_ref, p3_ref, near_ref, far_ref, *outs):
    z, x = here()
    parts = (p0_ref, p1_ref, p2_ref, p3_ref)
    before = doc_row(near_ref)
    incoming = near_ref[...] + same(doc_row(far_ref), before) * far_ref[...]
    for t, out in enumerate(outs):
        target = lax.rem(x + t, 4)
        doc = before
        for s, part in enumerate(parts):
            doc = jnp.where(row_block(x, s) == target - 1, doc_row(part), doc)
        prior = same(before, doc) * incoming
        for s, part in enumerate(parts):
            use = jnp.where(row_block(x, s) < target, same(doc_row(part), doc), 0.0)
            prior = prior + use * part[...]
        out[...] = prior


def stash_kernel(src_hbm, out_ref, sem):
    copy = pltpu.make_async_copy(src_hbm, out_ref, sem)
    copy.start()
    copy.wait()


def pack_kernel(own_hbm, near_hbm, far_hbm, o1_hbm, o2_hbm, o3_hbm, sems):
    z, x = here()
    upper, lower = pl.ds(0, 2 * ROWS), pl.ds(2 * ROWS, 2 * ROWS)
    for s, out in enumerate((o1_hbm, o2_hbm, o3_hbm)):
        later = lax.rem(x + s + 1, 4) > x
        pltpu.make_async_copy(near_hbm, out.at[upper], sems.at[s]).start()
        pl.when(later)(lambda: pltpu.make_async_copy(own_hbm, out.at[lower], sems.at[3 + s]).start())
        pl.when(jnp.logical_not(later))(lambda: pltpu.make_async_copy(far_hbm, out.at[lower], sems.at[3 + s]).start())
    for s, out in enumerate((o1_hbm, o2_hbm, o3_hbm)):
        pltpu.make_async_copy(near_hbm, out.at[upper], sems.at[s]).wait()
        pltpu.make_async_copy(own_hbm, out.at[lower], sems.at[3 + s]).wait()


def states_kernel(doc_hbm, kf_hbm, v_hbm, k_hbm, vs_hbm, c0_ref, c1_ref, c2_ref, c3_ref, kv_ref, n_ref, state_ref, doc_ref, kf_ref, v_ref, sems):
    pairs = [(doc_hbm, doc_ref), (kf_hbm, kf_ref), (v_hbm, v_ref), (k_hbm, kv_ref.at[:ROWS]), (vs_hbm, kv_ref.at[ROWS:])]
    copies = [pltpu.make_async_copy(src, dst, sems.at[i]) for i, (src, dst) in enumerate(pairs)]
    for copy in copies:
        copy.start()
    z, x = here()
    first = (z * 4 + x) * ROWS
    m, n, times = pair_of(lax.broadcasted_iota(jnp.int32, (FEATS, 2 * F), 0))
    col = lax.broadcasted_iota(jnp.int32, (FEATS, 2 * F), 1)
    e1 = ((col == m) & (times > 0)).astype(jnp.float32).astype(jnp.bfloat16)
    e2 = ((col == n) & (times > 0)).astype(jnp.float32).astype(jnp.bfloat16)
    lane = lax.broadcasted_iota(jnp.int32, (ROWS, DH), 1)
    norms = jnp.zeros((FEATS, DH), jnp.float32)
    copies[0].wait()
    n1 = jnp.sum((doc_ref[...] < 1).astype(jnp.int32))
    n2 = jnp.sum((doc_ref[...] < 2).astype(jnp.int32))
    n_ref[0] = n1
    n_ref[1] = n2
    pos = first + lax.broadcasted_iota(jnp.int32, (F, ROWS), 1)
    sel = (doc_of(pos, n1, n2) == doc_of(first + ROWS - 1, n1, n2)).astype(jnp.float32)
    copies[1].wait()
    kt = kf_ref[...].astype(jnp.float32).T
    copies[2].wait()
    for h in range(HEADS):
        rows = jnp.concatenate([kt[h * F : (h + 1) * F] * sel, sel], 0).astype(jnp.bfloat16)
        hi, lo = split(dot(e1, rows) * dot(e2, rows))
        unit = (lane == h).astype(jnp.bfloat16)
        rhs = jnp.concatenate([v_ref[:, h * DH : (h + 1) * DH], unit], 1)
        res = dot(hi, rhs) + dot(lo, rhs)
        state_ref[h * FEATS : (h + 1) * FEATS, :] = res[:, :DH]
        norms = norms + res[:, DH:]
    across = norms.T
    for h in range(HEADS):
        base = h * FEATS + USED
        state_ref[base : base + 1, :] = across[h : h + 1, :DH]
        state_ref[base + 1 : base + 2, : FEATS - DH] = across[h : h + 1, DH:]
        last = doc_of(first + ROWS - 1, n1, n2).astype(jnp.float32)
        state_ref[base + 2 : base + 3, :] = jnp.full((1, DH), last, jnp.float32)
    for s, out in enumerate((c0_ref, c1_ref, c2_ref, c3_ref)):
        chunk = lax.rem(x + s, 4)
        out[...] = state_ref[pl.ds(pl.multiple_of(chunk * QUARTER, QUARTER), QUARTER), :]
    copies[3].wait()
    copies[4].wait()


def local_kernel(n_ref, qf_ref, kf_ref, v_ref, num_ref, den_ref, hi_ref, lo_ref, mask_ref):
    n1, n2 = n_ref[0], n_ref[1]
    z, x = here()
    first = (z * 4 + x) * ROWS
    row = lax.broadcasted_iota(jnp.int32, (ROWS, ROWS), 0)
    col = lax.broadcasted_iota(jnp.int32, (ROWS, ROWS), 1)
    begin = start_of(first + lax.broadcasted_iota(jnp.int32, (ROWS, 1), 0), n1, n2) - first
    mask_ref[...] = ((col <= row) & (col >= begin)).astype(jnp.float32)
    lane = lax.broadcasted_iota(jnp.int32, (ROWS, DH), 1)
    one = (lane == 0).astype(jnp.bfloat16)
    kf = jnp.concatenate([kf_ref[...], one], 1)
    half = ROWS // 2
    dens = [jnp.zeros((half, DH), jnp.float32) for _ in range(2)]
    for h in range(HEADS):
        qh = jnp.where(lane // F == h, qf_ref[...], jnp.zeros((), jnp.bfloat16))
        qh = jnp.concatenate([qh, one], 1)
        unit = (lane == h).astype(jnp.bfloat16)
        rhs = jnp.concatenate([v_ref[:, h * DH : (h + 1) * DH], unit], 1)
        for r in range(2):
            span = (r + 1) * half
            s = dot(qh[r * half : (r + 1) * half], kf[:span], NT)
            w = (s * s + 1.0) * mask_ref[r * half : (r + 1) * half, :span]
            hi, lo = split(w)
            res = dot(hi, rhs[:span]) + dot(lo, rhs[:span])
            num_ref[r * half : (r + 1) * half, h * DH : (h + 1) * DH] = res[:, :DH]
            dens[r] = dens[r] + res[:, DH:]
    for r in range(2):
        den_ref[r * half : (r + 1) * half, :] = dens[r]
    m, n, times = pair_of(lax.broadcasted_iota(jnp.int32, (DH, 256), 1))
    lane_row = lax.broadcasted_iota(jnp.int32, (DH, 256), 0)
    m1, n1_, times1 = pair_of(lax.broadcasted_iota(jnp.int32, (1, 256), 1))
    ones_a = jnp.where(m1 == F, times1, 0.0)
    ones_b = jnp.where((n1_ == F) & (times1 > 0), 1.0, 0.0)
    once = (times > 0).astype(jnp.float32)
    q = qf_ref[...]
    for h in range(HEADS):
        e1 = jnp.where((lane_row == m + h * F) & (m < F), times, 0.0).astype(jnp.bfloat16)
        e2 = jnp.where((lane_row == n + h * F) & (n < F), once, 0.0).astype(jnp.bfloat16)
        hi, lo = split((dot(q, e1) + ones_a) * (dot(q, e2) + ones_b))
        hi_ref[:, h * 256 : (h + 1) * 256] = hi
        lo_ref[:, h * 256 : (h + 1) * 256] = lo


def finish_kernel(n_ref, hi_ref, lo_ref, num_ref, den_ref, p0_ref, p1_ref, p2_ref, p3_ref, out_ref, sq_ref, prior_ref):
    n1, n2 = n_ref[0], n_ref[1]
    z, x = here()
    first = (z * 4 + x) * ROWS
    pos = first + lax.broadcasted_iota(jnp.int32, (ROWS, 1), 0)
    usable = ((doc_of(pos, n1, n2) == doc_of(first - 1, n1, n2)) & (first > 0)).astype(jnp.float32)
    for s, part in enumerate((p0_ref, p1_ref, p2_ref, p3_ref)):
        chunk = lax.rem(x - s + 4, 4)
        prior_ref[pl.ds(pl.multiple_of(chunk * QUARTER, QUARTER), QUARTER), :] = part[...]
    spare = [jnp.zeros((DH - HEADS, DH), jnp.float32)]
    sums = [[prior_ref[h * FEATS + USED + i : h * FEATS + USED + i + 1, :] for h in range(HEADS)] for i in range(2)]
    norm = jnp.concatenate([jnp.concatenate(rows + spare, 0).T for rows in sums], 0)[:FEATS]
    norm_hi, norm_lo = split(norm)
    squares = jnp.zeros((ROWS, DH), jnp.float32)
    for h in range(HEADS):
        hi = hi_ref[:, h * 256 : h * 256 + FEATS]
        lo = lo_ref[:, h * 256 : h * 256 + FEATS]
        s_hi, s_lo = split(prior_ref[h * FEATS : (h + 1) * FEATS, :])
        r_hi = jnp.concatenate([s_hi, norm_hi], 1)
        r_lo = jnp.concatenate([s_lo, norm_lo], 1)
        res = dot(jnp.concatenate([hi, lo], 0), r_hi)
        res = (res[:ROWS] + (res[ROWS:] + dot(hi, r_lo))) * usable
        num = num_ref[:, h * DH : (h + 1) * DH] + res[:, :DH]
        den = den_ref[:, h : h + 1] + res[:, DH + h : DH + h + 1]
        out = (num / den).astype(jnp.bfloat16)
        out_ref[:, h * DH : (h + 1) * DH] = out
        wide = out.astype(jnp.float32)
        squares = squares + wide * wide
    sq_ref[...] = jnp.sum(squares.T, 0, keepdims=True)


def block_of(slot):
    z, x = here()
    src = lax.rem(x + 4 - lax.div(slot - 1, 2), 4)
    behind = jnp.where(lax.rem(slot, 2) == 1, 1, jnp.where(src < x, 0, 2))
    return jnp.where(slot < 3, z * 4 + x - 4 * slot, (z - behind) * 4 + src)


def active(slot, n1, n2):
    z, x = here()
    own = z * 4 + x
    low = start_of(own * ROWS, n1, n2) // ROWS
    return (block_of(slot) >= low) & (block_of(slot) < own) | (slot == 0)


def key_norm(kv_ref, place):
    k = kv_ref[place, :ROWS].astype(jnp.float32)
    return jnp.sum(k * k, 1, keepdims=True)


def gauge_kernel(n_ref, lin_ref, gain_ref, own_ref, near_ref, far_ref, rows_ref, stat_ref):
    most = jnp.zeros((ROWS, 1), jnp.float32)
    for h in range(HEADS):
        lanes = slice(h * DH, (h + 1) * DH)
        q = lin_ref[:, lanes].astype(jnp.float32) * gain_ref[0:1, lanes]
        most = jnp.maximum(most, jnp.sum(q * q, 1, keepdims=True))
    rows_ref[...] = jnp.broadcast_to(most, (ROWS, DH)).T[:8]
    stat_ref[0] = 0.0
    for slot, kv_ref in enumerate((own_ref, near_ref, far_ref)):
        k = kv_ref[:ROWS].astype(jnp.float32)
        norm = jnp.max(jnp.sum(k * k, 1, keepdims=True))
        stat_ref[0] = jnp.where(active(slot, n_ref[0], n_ref[1]), jnp.maximum(stat_ref[0], norm), stat_ref[0])


def scale_of(total_ref):
    return lax.rsqrt(total_ref[...] / ALL_WIDE + 1e-06)


def make_queries(lin_ref, total_ref, gain_ref, q_ref, double):
    scale = jnp.broadcast_to(scale_of(total_ref), (DH, ROWS)).T
    for h in range(HEADS):
        lanes = slice(h * DH, (h + 1) * DH)
        q = (lin_ref[:, lanes].astype(jnp.float32) * scale * gain_ref[0:1, lanes]).astype(jnp.bfloat16)
        lo = jnp.zeros((ROWS, DH), jnp.bfloat16)
        if double:
            q, lo = split(q.astype(jnp.float32) * FACTOR)
        q_ref[h, :, :DH] = q
        q_ref[h, :, DH:] = lo


def ones_beside(v):
    return jnp.concatenate([v, jnp.ones((ROWS, DH), jnp.bfloat16)], 1)


def bounded_tile(kv_ref, place, slot, begin_first, q_ref, acc_ref, keep):
    kk = jnp.concatenate([kv_ref[place, :ROWS]] * 2, 1)
    key = block_of(slot) * ROWS + lax.broadcasted_iota(jnp.int32, (ROWS, 256), 0)
    inside = (key >= begin_first).astype(jnp.float32).astype(jnp.bfloat16)
    v = ones_beside(kv_ref[place, ROWS:]) * inside
    for h in range(HEADS):
        p = jnp.exp2(dot(q_ref[h], kk, NT)).astype(jnp.bfloat16)
        res = dot(p, v)
        acc_ref[h] += res * keep


def bounded_tiles(slots, kv_ref, base, n1, n2, q_ref, acc_ref, before_use):
    first, positions = rows_of()
    begin_first = start_of(first, n1, n2)

    keep = (start_of(positions, n1, n2) == begin_first).astype(jnp.float32)

    def one(slot):
        before_use(slot)
        bounded_tile(kv_ref, slot - base, slot, begin_first, q_ref, acc_ref, keep)

    def step(slot, carry):
        pl.when(active(slot, n1, n2))(lambda: one(slot))
        return carry

    lax.fori_loop(*slots, step, 0)


def make_mask(mask_ref, block, first, begin):
    row = lax.broadcasted_iota(jnp.int32, (ROWS, ROWS), 0)
    key = block * ROWS + lax.broadcasted_iota(jnp.int32, (ROWS, ROWS), 1)
    mask_ref[...] = jnp.where((key >= begin) & (key <= first + row), 0.0, FAR)


def any_tile(kv_ref, slot, base, first, begin, q_ref, acc_ref, mask_ref, top_ref):
    make_mask(mask_ref, block_of(slot), first, begin)
    kk = jnp.concatenate([kv_ref[slot - base, :ROWS]] * 2, 1)
    v = ones_beside(kv_ref[slot - base, ROWS:])

    def head(h, carry):
        s = jnp.maximum(dot(q_ref[h], kk, NT) * FACTOR + mask_ref[...], FAR)
        old = top_ref[h]
        new = jnp.maximum(old, jnp.max(s, 1, keepdims=True))
        p = jnp.exp2(s - jnp.concatenate([new] * 4, 1)).astype(jnp.bfloat16)
        fade = jnp.exp2(old - new)
        acc_ref[h] = acc_ref[h] * jnp.concatenate([fade] * 2, 1) + dot(p, v)
        top_ref[h] = new
        return carry

    lax.fori_loop(0, HEADS, head, 0)


def in_softmax_phase():
    return lax.axis_index("phase") == 1


def rows_of():
    z, x = here()
    first = (z * 4 + x) * ROWS
    return first, first + lax.broadcasted_iota(jnp.int32, (ROWS, 1), 0)


def open_kernel(
    n_ref, gauge_ref, lin_ref, total_ref, gain_ref, rows_ref, own_hbm, near_hbm, far_hbm,
    q_ref, acc_ref, top_hbm, stat_ref, kv_ref, mask_ref, top_ref, sems,
):
    @pl.when(in_softmax_phase())
    def _():
        n1, n2 = n_ref[0], n_ref[1]
        first, positions = rows_of()
        begin = start_of(positions, n1, n2)
        copies = [
            pltpu.make_async_copy(src, kv_ref.at[i], sems.at[i]) for i, src in enumerate((own_hbm, near_hbm, far_hbm))
        ]
        for copy in copies:
            copy.start()
        scale = scale_of(total_ref)
        q_most = 1.02 * jnp.max(scale * scale * rows_ref[0:1, :])
        safe = q_most * gauge_ref[0] < (SAFE / FACTOR) ** 2
        stat_ref[0] = q_most
        stat_ref[1] = jnp.where(safe, 1.0, 0.0)

        @pl.when(safe)
        def _():
            make_queries(lin_ref, total_ref, gain_ref, q_ref, True)
            make_mask(mask_ref, block_of(0), first, begin)
            for copy in copies:
                copy.wait()
            kk = jnp.concatenate([kv_ref[0, :ROWS]] * 2, 1)
            v = ones_beside(kv_ref[0, ROWS:])
            half = ROWS // 2
            for h in range(HEADS):
                for r in range(2):
                    rows, span = slice(r * half, (r + 1) * half), (r + 1) * half
                    s = dot(q_ref[h, rows, :], kk[:span], NT) + mask_ref[rows, :span]
                    acc_ref[h, rows, :] = dot(jnp.exp2(s).astype(jnp.bfloat16), v[:span])
            bounded_tiles((1, 3), kv_ref, 0, n1, n2, q_ref, acc_ref, lambda slot: None)

        @pl.when(jnp.logical_not(safe))
        def _():
            make_queries(lin_ref, total_ref, gain_ref, q_ref, False)
            acc_ref[...] = jnp.zeros_like(acc_ref)
            top_ref[...] = jnp.full(top_ref.shape, FAR, jnp.float32)
            for copy in copies:
                copy.wait()

            def step(slot, carry):
                pl.when(active(slot, n1, n2))(
                    lambda: any_tile(kv_ref, slot, 0, first, begin, q_ref, acc_ref, mask_ref, top_ref)
                )
                return carry

            lax.fori_loop(0, 3, step, 0)
            copy = pltpu.make_async_copy(top_ref, top_hbm, sems.at[0])
            copy.start()
            copy.wait()


def close_kernel(n_ref, stat_ref, lin_ref, total_ref, gain_ref, q_ref, part_ref, top_hbm, *refs):
    kv_hbm, (out_hbm, kv_ref, raw_ref, acc_ref, mask_ref, top_ref, norm_ref, out_ref, kv_sems, out_sems) = refs[:3], refs[3:]

    @pl.when(jnp.logical_not(in_softmax_phase()))
    def _():
        copy = pltpu.make_async_copy(lin_ref, out_hbm, out_sems.at[0])
        copy.start()
        copy.wait()

    @pl.when(in_softmax_phase())
    def _():
        close(
            n_ref, stat_ref, lin_ref, total_ref, gain_ref, q_ref, part_ref, top_hbm, kv_hbm,
            out_hbm, kv_ref, raw_ref, acc_ref, mask_ref, top_ref, norm_ref, out_ref, kv_sems, out_sems,
        )


def close(
    n_ref, stat_ref, lin_ref, total_ref, gain_ref, q_ref, part_ref, top_hbm, kv_hbm,
    out_hbm, kv_ref, raw_ref, acc_ref, mask_ref, top_ref, norm_ref, out_ref, kv_sems, out_sems,
):
    n1, n2 = n_ref[0], n_ref[1]
    base = 3

    def fetch(slot):
        src = kv_hbm[(slot - base) // 2].at[pl.ds((slot - base) % 2 * 2 * ROWS, 2 * ROWS)]
        return pltpu.make_async_copy(src, kv_ref.at[slot - base], kv_sems.at[slot - base])

    def arrived(slot):
        place = kv_ref.at[slot - base]
        pltpu.make_async_copy(place, place, kv_sems.at[slot - base]).wait()

    for slot in range(base, SLOTS):
        pl.when(active(slot, n1, n2))(lambda: fetch(slot).start())
    acc_ref[...] = part_ref[...]
    norm_ref[...] = jnp.zeros_like(norm_ref)
    opened_safe = stat_ref[1] > 0.5

    def before_use(slot):
        arrived(slot)
        norm_ref[...] = jnp.maximum(norm_ref[...], key_norm(kv_ref, slot - base))

    @pl.when(opened_safe)
    def _():
        bounded_tiles((base, SLOTS), kv_ref, base, n1, n2, q_ref, acc_ref, before_use)

    @pl.when(jnp.logical_not(opened_safe))
    def _():
        for slot in range(base, SLOTS):
            pl.when(active(slot, n1, n2))(lambda: arrived(slot))

    safe = opened_safe & (stat_ref[0] * jnp.max(norm_ref[...]) < (SAFE / FACTOR) ** 2)

    @pl.when(jnp.logical_not(safe))
    def _():
        first, positions = rows_of()
        begin = start_of(positions, n1, n2)
        make_queries(lin_ref, total_ref, gain_ref, raw_ref, False)
        acc_ref[...] = part_ref[...]
        top_ref[...] = jnp.zeros_like(top_ref)

        @pl.when(jnp.logical_not(opened_safe))
        def _():
            copy = pltpu.make_async_copy(top_hbm, top_ref, kv_sems.at[0])
            copy.start()
            copy.wait()

        def step(slot, carry):
            pl.when(active(slot, n1, n2))(
                lambda: any_tile(kv_ref, slot, base, first, begin, raw_ref, acc_ref, mask_ref, top_ref)
            )
            return carry

        lax.fori_loop(base, SLOTS, step, 0)

    copies = []
    for h in range(HEADS):
        lanes = slice(h * DH, (h + 1) * DH)
        out_ref[:, lanes] = (acc_ref[h, :, :DH] / acc_ref[h, :, DH:]).astype(jnp.bfloat16)
        copies.append(pltpu.make_async_copy(out_ref.at[:, lanes], out_hbm.at[:, lanes], out_sems.at[h]))
        copies[-1].start()
    for copy in copies:
        copy.wait()


VMEM = pl.BlockSpec(memory_space=pltpu.VMEM)
SMEM = pl.BlockSpec(memory_space=pltpu.SMEM)
ANY = pl.BlockSpec(memory_space=pl.ANY)


def call(kernel, outs, out_specs, args, in_specs, scratch, flops, limit):
    return pl.pallas_call(
        kernel,
        out_shape=tuple(outs),
        in_specs=in_specs,
        out_specs=tuple(out_specs),
        scratch_shapes=scratch,
        compiler_params=pltpu.CompilerParams(vmem_limit_bytes=limit << 20),
        cost_estimate=pl.CostEstimate(flops=flops, bytes_accessed=0, transcendentals=0),
    )(*args)


def shape(dims, dtype=jnp.float32):
    return jax.ShapeDtypeStruct(dims, dtype)


def stash(chunk):
    return call(stash_kernel, [shape(chunk.shape)], [VMEM], (chunk,), [ANY], [pltpu.SemaphoreType.DMA], 0, 4)[0]


def row_sum(parts):
    return call(row_sum_kernel, [shape((QUARTER, DH))], [VMEM], tuple(parts), [VMEM] * 4, [], 0, 8)[0]


def priors_of(parts, near, far):
    return call(
        prior_kernel, [shape((QUARTER, DH))] * 4, [VMEM] * 4, tuple(parts) + (near, far), [VMEM] * 6, [], 1000000000, 8
    )


def pack(own_kv, near_kv, far_kv):
    return call(
        pack_kernel,
        [shape((4 * ROWS, DH), own_kv.dtype)] * 3,
        [ANY] * 3,
        (own_kv, near_kv, far_kv),
        [ANY] * 3,
        [pltpu.SemaphoreType.DMA((6,))],
        5000000000,
        4,
    )


def states(doc_ids, key_feats, values, keys_soft, values_soft):
    bf16 = jnp.bfloat16
    return call(
        states_kernel,
        [shape((QUARTER, DH))] * 4 + [shape((2 * ROWS, DH), bf16), shape((8,), jnp.int32)],
        [VMEM] * 5 + [SMEM],
        (doc_ids.reshape(-1, DH), key_feats, values, keys_soft, values_soft),
        [ANY] * 5,
        [
            pltpu.VMEM((HEADS * FEATS, DH), jnp.float32),
            pltpu.VMEM((doc_ids.shape[0] // DH, DH), jnp.int32),
            pltpu.VMEM((ROWS, DH), bf16),
            pltpu.VMEM((ROWS, WIDE), bf16),
            pltpu.SemaphoreType.DMA((5,)),
        ],
        0,
        60,
    )


def local_part(counts, query_feats, key_feats, values):
    bf16 = jnp.bfloat16
    return call(
        local_kernel,
        [shape((ROWS, WIDE)), shape((ROWS, DH)), shape((ROWS, HEADS * 256), bf16), shape((ROWS, HEADS * 256), bf16)],
        [VMEM] * 4,
        (counts, query_feats, key_feats, values),
        [SMEM] + [VMEM] * 3,
        [pltpu.VMEM((ROWS, ROWS), jnp.float32)],
        0,
        24,
    )


def finish(counts, feats_hi, feats_lo, num, den, parts):
    return call(
        finish_kernel,
        [shape((ROWS, WIDE), jnp.bfloat16), shape((1, ROWS))],
        [VMEM] * 2,
        (counts, feats_hi, feats_lo, num, den) + tuple(parts),
        [SMEM] + [VMEM] * 8,
        [pltpu.VMEM((HEADS * FEATS, DH), jnp.float32)],
        8000000000,
        20,
    )


def gauge(counts, linear_out, gain, own_kv, near_kv, far_kv):
    return call(
        gauge_kernel,
        [shape((8, ROWS)), shape((8,))],
        [VMEM, SMEM],
        (counts, linear_out, gain, own_kv, near_kv, far_kv),
        [SMEM] + [VMEM] * 5,
        [],
        0,
        8,
    )


def soft_open(counts, gauged, linear_out, total, gain, rows, own_kv, near_kv, far_kv):
    bf16 = jnp.bfloat16
    return call(
        open_kernel,
        [shape((HEADS, ROWS, 256), bf16), shape((HEADS, ROWS, 256)), shape((HEADS, ROWS, DH)), shape((8,))],
        [VMEM, VMEM, ANY, SMEM],
        (counts, gauged, linear_out, total, gain, rows, own_kv, near_kv, far_kv),
        [SMEM] * 2 + [VMEM] * 4 + [ANY] * 3,
        [
            pltpu.VMEM((3, 2 * ROWS, DH), bf16),
            pltpu.VMEM((ROWS, ROWS), jnp.float32),
            pltpu.VMEM((HEADS, ROWS, DH), jnp.float32),
            pltpu.SemaphoreType.DMA((3,)),
        ],
        0,
        28,
    )


def soft_close(counts, stat, linear_out, total, gain, queries, part, top, pieces):
    bf16 = jnp.bfloat16
    return call(
        close_kernel,
        [shape((ROWS, WIDE), bf16)],
        [ANY],
        (counts, stat, linear_out, total, gain, queries, part, top) + tuple(pieces),
        [SMEM] * 2 + [VMEM] * 5 + [ANY] * 4,
        [
            pltpu.VMEM((SLOTS - 3, 2 * ROWS, DH), bf16),
            pltpu.VMEM((HEADS, ROWS, 256), bf16),
            pltpu.VMEM((HEADS, ROWS, 256), jnp.float32),
            pltpu.VMEM((ROWS, ROWS), jnp.float32),
            pltpu.VMEM((HEADS, ROWS, DH), jnp.float32),
            pltpu.VMEM((ROWS, 1), jnp.float32),
            pltpu.VMEM((ROWS, WIDE), bf16),
            pltpu.SemaphoreType.DMA((SLOTS - 3,)),
            pltpu.SemaphoreType.DMA((HEADS,)),
        ],
        0,
        32,
    )[0]


def shift(x, axis, by):
    size = lax.axis_size(axis)
    return lax.ppermute(x, axis, [(i, (i + by) % size) for i in range(size)])


def after(x, *others):
    return lax.optimization_barrier((x,) + others)[0]


def local(query_feats, key_feats, values, keys_soft, values_soft, norm_gain, doc_ids):
    zs = lax.axis_size("z")
    *chunks, own_kv, counts = states(doc_ids, key_feats, values, keys_soft, values_soft)

    parts = [stash(chunks[0])] + [shift(chunks[s], "x", s) for s in (1, 2, 3)]

    near_kv = lax.ppermute(own_kv, ("phase", "z"), [(zs + i, zs + i + 1) for i in range(zs - 1)])
    far_kv = lax.ppermute(own_kv, ("phase", "z"), [(i, zs + i + 2) for i in range(zs - 2)])

    local_sums = local_part(counts, query_feats, key_feats, values)
    total = row_sum(parts)
    near = lax.ppermute(total, "z", [(i, i + 1) for i in range(zs - 1)])
    far = lax.ppermute(
        total,
        ("phase", "z"),
        [((1 - p) * zs + i, p * zs + i + 2) for p in range(2) for i in range(zs - 2)],
    )

    messages = lax.optimization_barrier((total,) + tuple(pack(own_kv, near_kv, far_kv)))[1:]
    others = [
        lax.ppermute(message, ("phase", "x"), [(4 + i, 4 + (i + s) % 4) for i in range(4)])
        for s, message in zip((1, 2, 3), messages)
    ]

    near = after(near, *local_sums)
    priors = priors_of(parts, near, far)
    arrived = [priors[0]] + [shift(priors[s], "x", s) for s in (1, 2, 3)]
    num, den, feats_hi, feats_lo = local_sums
    linear_out, squares = finish(counts, feats_hi, feats_lo, num, den, arrived)
    total = squares + shift(squares, "core", 1)
    gain = norm_gain[None]
    rows, gauged = gauge(counts, linear_out, gain, own_kv, near_kv, far_kv)
    total = total + lax.ppermute(total, "y", list(enumerate((1, 0, 3, 2))))
    total = after(total, rows)
    total = total + lax.ppermute(total, "y", list(enumerate((2, 3, 0, 1))))
    queries, part, top, stat = soft_open(counts, gauged, linear_out, total, gain, rows, own_kv, near_kv, far_kv)
    return soft_close(counts, stat, linear_out, total, gain, queries, part, top, others)[None]


def solution(mesh):
    fine = Mesh(mesh.devices.reshape(2, 4, 4, 4, 2), ("phase", "z", "x", "y", "core"))
    seq, head = ("z", "x"), ("y", "core")
    return jax.shard_map(
        local,
        mesh=fine,
        in_specs=(
            P(seq, head),
            P(seq, head),
            P(seq, head),
            P(seq, head),
            P(seq, head),
            P(head),
            P(),
        ),
        out_specs=P("phase", seq, head),
        check_vma=False,
    )
```

```python
import math

import jax
import jax.numpy as jnp
from jax import lax
from jax.experimental import pallas as pl
from jax.experimental.pallas import tpu as pltpu
from jax.sharding import Mesh, PartitionSpec as P

DH = 128
F = 16
ROWS = 512
HEADS = 8
WIDE = HEADS * DH
ALL_WIDE = 64 * DH
USED = (F + 1) * (F + 2) // 2
FEATS = 160
QUARTER = HEADS * FEATS // 4
SLOTS = 9
DOC_ROW = USED + 2
LOG2E = math.log2(math.e)
FACTOR = LOG2E / math.sqrt(DH)
SAFE = 110.0
FAR = -1e30

NN = (((1,), (0,)), ((), ()))
NT = (((1,), (1,)), ((), ()))


def dot(a, b, dims=NN):
    return lax.dot_general(a, b, dims, preferred_element_type=jnp.float32)


def split(x):
    hi = x.astype(jnp.bfloat16)
    lo = (x - hi.astype(jnp.float32)).astype(jnp.bfloat16)
    return hi, lo


def doc_of(position, n1, n2):
    return (position >= n1).astype(jnp.int32) + (position >= n2).astype(jnp.int32)


def start_of(position, n1, n2):
    return jnp.where(position >= n2, n2, jnp.where(position >= n1, n1, 0))


def pair_of(e):
    gap = jnp.zeros_like(e)
    for k in range(1, F // 2 + 1):
        gap = gap + (e >= k * (F + 1)).astype(jnp.int32)
    m = e - gap * (F + 1)
    n = m + gap
    n = jnp.where(n > F, n - (F + 1), n)
    times = jnp.where((gap == 0) & (m < F), 1.0, 2.0)
    times = jnp.where(e < USED, times, 0.0)
    return m, n, times


def here():
    return lax.axis_index("z"), lax.axis_index("x")


def row_block(x, s):
    return lax.rem(x - s + 4, 4)


def same(a, b):
    return (a == b).astype(jnp.float32)


def doc_row(ref):
    return ref[DOC_ROW : DOC_ROW + 1, :]


def row_sum_kernel(p0_ref, p1_ref, p2_ref, p3_ref, out_ref):
    parts = (p0_ref, p1_ref, p2_ref, p3_ref)
    end = doc_row(p0_ref)
    for part in parts[1:]:
        end = jnp.maximum(end, doc_row(part))
    total = jnp.zeros((QUARTER, DH), jnp.float32)
    for part in parts:
        total = total + same(doc_row(part), end) * part[...]
    out_ref[...] = total
    out_ref[DOC_ROW : DOC_ROW + 1, :] = end


def prior_kernel(p0_ref, p1_ref, p2_ref, p3_ref, near_ref, far_ref, *outs):
    z, x = here()
    parts = (p0_ref, p1_ref, p2_ref, p3_ref)
    before = doc_row(near_ref)
    incoming = near_ref[...] + same(doc_row(far_ref), before) * far_ref[...]
    for t, out in enumerate(outs):
        target = lax.rem(x + t, 4)
        doc = before
        for s, part in enumerate(parts):
            doc = jnp.where(row_block(x, s) == target - 1, doc_row(part), doc)
        prior = same(before, doc) * incoming
        for s, part in enumerate(parts):
            use = jnp.where(row_block(x, s) < target, same(doc_row(part), doc), 0.0)
            prior = prior + use * part[...]
        out[...] = prior


def stash_kernel(src_hbm, out_ref, sem):
    copy = pltpu.make_async_copy(src_hbm, out_ref, sem)
    copy.start()
    copy.wait()


def pack_kernel(own_hbm, near_hbm, far_hbm, o1_hbm, o2_hbm, o3_hbm, sems):
    z, x = here()
    upper, lower = pl.ds(0, 2 * ROWS), pl.ds(2 * ROWS, 2 * ROWS)
    for s, out in enumerate((o1_hbm, o2_hbm, o3_hbm)):
        later = lax.rem(x + s + 1, 4) > x
        pltpu.make_async_copy(near_hbm, out.at[upper], sems.at[s]).start()
        pl.when(later)(lambda: pltpu.make_async_copy(own_hbm, out.at[lower], sems.at[3 + s]).start())
        pl.when(jnp.logical_not(later))(lambda: pltpu.make_async_copy(far_hbm, out.at[lower], sems.at[3 + s]).start())
    for s, out in enumerate((o1_hbm, o2_hbm, o3_hbm)):
        pltpu.make_async_copy(near_hbm, out.at[upper], sems.at[s]).wait()
        pltpu.make_async_copy(own_hbm, out.at[lower], sems.at[3 + s]).wait()


def states_kernel(doc_hbm, kf_hbm, v_hbm, k_hbm, vs_hbm, c0_ref, c1_ref, c2_ref, c3_ref, kv_ref, n_ref, state_ref, doc_ref, kf_ref, v_ref, sems):
    pairs = [(doc_hbm, doc_ref), (kf_hbm, kf_ref), (v_hbm, v_ref), (k_hbm, kv_ref.at[:ROWS]), (vs_hbm, kv_ref.at[ROWS:])]
    copies = [pltpu.make_async_copy(src, dst, sems.at[i]) for i, (src, dst) in enumerate(pairs)]
    for copy in copies:
        copy.start()
    z, x = here()
    first = (z * 4 + x) * ROWS
    m, n, times = pair_of(lax.broadcasted_iota(jnp.int32, (FEATS, 2 * F), 0))
    col = lax.broadcasted_iota(jnp.int32, (FEATS, 2 * F), 1)
    e1 = ((col == m) & (times > 0)).astype(jnp.float32).astype(jnp.bfloat16)
    e2 = ((col == n) & (times > 0)).astype(jnp.float32).astype(jnp.bfloat16)
    lane = lax.broadcasted_iota(jnp.int32, (ROWS, DH), 1)
    norms = jnp.zeros((FEATS, DH), jnp.float32)
    copies[0].wait()
    n1 = jnp.sum((doc_ref[...] < 1).astype(jnp.int32))
    n2 = jnp.sum((doc_ref[...] < 2).astype(jnp.int32))
    n_ref[0] = n1
    n_ref[1] = n2
    pos = first + lax.broadcasted_iota(jnp.int32, (F, ROWS), 1)
    sel = (doc_of(pos, n1, n2) == doc_of(first + ROWS - 1, n1, n2)).astype(jnp.float32)
    copies[1].wait()
    kt = kf_ref[...].astype(jnp.float32).T
    copies[2].wait()
    for h in range(HEADS):
        rows = jnp.concatenate([kt[h * F : (h + 1) * F] * sel, sel], 0).astype(jnp.bfloat16)
        hi, lo = split(dot(e1, rows) * dot(e2, rows))
        unit = (lane == h).astype(jnp.bfloat16)
        rhs = jnp.concatenate([v_ref[:, h * DH : (h + 1) * DH], unit], 1)
        res = dot(hi, rhs) + dot(lo, rhs)
        state_ref[h * FEATS : (h + 1) * FEATS, :] = res[:, :DH]
        norms = norms + res[:, DH:]
    across = norms.T
    for h in range(HEADS):
        base = h * FEATS + USED
        state_ref[base : base + 1, :] = across[h : h + 1, :DH]
        state_ref[base + 1 : base + 2, : FEATS - DH] = across[h : h + 1, DH:]
        last = doc_of(first + ROWS - 1, n1, n2).astype(jnp.float32)
        state_ref[base + 2 : base + 3, :] = jnp.full((1, DH), last, jnp.float32)
    for s, out in enumerate((c0_ref, c1_ref, c2_ref, c3_ref)):
        chunk = lax.rem(x + s, 4)
        out[...] = state_ref[pl.ds(pl.multiple_of(chunk * QUARTER, QUARTER), QUARTER), :]
    copies[3].wait()
    copies[4].wait()


def local_kernel(n_ref, qf_ref, kf_ref, v_ref, num_ref, den_ref, hi_ref, lo_ref, mask_ref):
    n1, n2 = n_ref[0], n_ref[1]
    z, x = here()
    first = (z * 4 + x) * ROWS
    row = lax.broadcasted_iota(jnp.int32, (ROWS, ROWS), 0)
    col = lax.broadcasted_iota(jnp.int32, (ROWS, ROWS), 1)
    begin = start_of(first + lax.broadcasted_iota(jnp.int32, (ROWS, 1), 0), n1, n2) - first
    mask_ref[...] = ((col <= row) & (col >= begin)).astype(jnp.float32)
    lane = lax.broadcasted_iota(jnp.int32, (ROWS, DH), 1)
    one = (lane == 0).astype(jnp.bfloat16)
    kf = jnp.concatenate([kf_ref[...], one], 1)
    half = ROWS // 2
    dens = [jnp.zeros((half, DH), jnp.float32) for _ in range(2)]
    for h in range(HEADS):
        qh = jnp.where(lane // F == h, qf_ref[...], jnp.zeros((), jnp.bfloat16))
        qh = jnp.concatenate([qh, one], 1)
        unit = (lane == h).astype(jnp.bfloat16)
        rhs = jnp.concatenate([v_ref[:, h * DH : (h + 1) * DH], unit], 1)
        for r in range(2):
            span = (r + 1) * half
            s = dot(qh[r * half : (r + 1) * half], kf[:span], NT)
            w = (s * s + 1.0) * mask_ref[r * half : (r + 1) * half, :span]
            hi, lo = split(w)
            res = dot(hi, rhs[:span]) + dot(lo, rhs[:span])
            num_ref[r * half : (r + 1) * half, h * DH : (h + 1) * DH] = res[:, :DH]
            dens[r] = dens[r] + res[:, DH:]
    for r in range(2):
        den_ref[r * half : (r + 1) * half, :] = dens[r]
    m, n, times = pair_of(lax.broadcasted_iota(jnp.int32, (DH, 256), 1))
    lane_row = lax.broadcasted_iota(jnp.int32, (DH, 256), 0)
    m1, n1_, times1 = pair_of(lax.broadcasted_iota(jnp.int32, (1, 256), 1))
    ones_a = jnp.where(m1 == F, times1, 0.0)
    ones_b = jnp.where((n1_ == F) & (times1 > 0), 1.0, 0.0)
    once = (times > 0).astype(jnp.float32)
    q = qf_ref[...]
    for h in range(HEADS):
        e1 = jnp.where((lane_row == m + h * F) & (m < F), times, 0.0).astype(jnp.bfloat16)
        e2 = jnp.where((lane_row == n + h * F) & (n < F), once, 0.0).astype(jnp.bfloat16)
        hi, lo = split((dot(q, e1) + ones_a) * (dot(q, e2) + ones_b))
        hi_ref[:, h * 256 : (h + 1) * 256] = hi
        lo_ref[:, h * 256 : (h + 1) * 256] = lo


def finish_kernel(n_ref, hi_ref, lo_ref, num_ref, den_ref, p0_ref, p1_ref, p2_ref, p3_ref, out_ref, sq_ref, prior_ref):
    n1, n2 = n_ref[0], n_ref[1]
    z, x = here()
    first = (z * 4 + x) * ROWS
    pos = first + lax.broadcasted_iota(jnp.int32, (ROWS, 1), 0)
    usable = ((doc_of(pos, n1, n2) == doc_of(first - 1, n1, n2)) & (first > 0)).astype(jnp.float32)
    for s, part in enumerate((p0_ref, p1_ref, p2_ref, p3_ref)):
        chunk = lax.rem(x - s + 4, 4)
        prior_ref[pl.ds(pl.multiple_of(chunk * QUARTER, QUARTER), QUARTER), :] = part[...]
    spare = [jnp.zeros((DH - HEADS, DH), jnp.float32)]
    sums = [[prior_ref[h * FEATS + USED + i : h * FEATS + USED + i + 1, :] for h in range(HEADS)] for i in range(2)]
    norm = jnp.concatenate([jnp.concatenate(rows + spare, 0).T for rows in sums], 0)[:FEATS]
    norm_hi, norm_lo = split(norm)
    squares = jnp.zeros((ROWS, DH), jnp.float32)
    for h in range(HEADS):
        hi = hi_ref[:, h * 256 : h * 256 + FEATS]
        lo = lo_ref[:, h * 256 : h * 256 + FEATS]
        s_hi, s_lo = split(prior_ref[h * FEATS : (h + 1) * FEATS, :])
        r_hi = jnp.concatenate([s_hi, norm_hi], 1)
        r_lo = jnp.concatenate([s_lo, norm_lo], 1)
        res = dot(jnp.concatenate([hi, lo], 0), r_hi)
        res = (res[:ROWS] + (res[ROWS:] + dot(hi, r_lo))) * usable
        num = num_ref[:, h * DH : (h + 1) * DH] + res[:, :DH]
        den = den_ref[:, h : h + 1] + res[:, DH + h : DH + h + 1]
        out = (num / den).astype(jnp.bfloat16)
        out_ref[:, h * DH : (h + 1) * DH] = out
        wide = out.astype(jnp.float32)
        squares = squares + wide * wide
    sq_ref[...] = jnp.sum(squares.T, 0, keepdims=True)


def block_of(slot):
    z, x = here()
    src = lax.rem(x + 4 - lax.div(slot - 1, 2), 4)
    behind = jnp.where(lax.rem(slot, 2) == 1, 1, jnp.where(src < x, 0, 2))
    return jnp.where(slot < 3, z * 4 + x - 4 * slot, (z - behind) * 4 + src)


def active(slot, n1, n2):
    z, x = here()
    own = z * 4 + x
    low = start_of(own * ROWS, n1, n2) // ROWS
    return (block_of(slot) >= low) & (block_of(slot) < own) | (slot == 0)


def key_norm(kv_ref, place):
    k = kv_ref[place, :ROWS].astype(jnp.float32)
    return jnp.sum(k * k, 1, keepdims=True)


def gauge_kernel(n_ref, lin_ref, gain_ref, own_ref, near_ref, far_ref, rows_ref, stat_ref):
    most = jnp.zeros((ROWS, 1), jnp.float32)
    for h in range(HEADS):
        lanes = slice(h * DH, (h + 1) * DH)
        q = lin_ref[:, lanes].astype(jnp.float32) * gain_ref[0:1, lanes]
        most = jnp.maximum(most, jnp.sum(q * q, 1, keepdims=True))
    rows_ref[...] = jnp.broadcast_to(most, (ROWS, DH)).T[:8]
    stat_ref[0] = 0.0
    for slot, kv_ref in enumerate((own_ref, near_ref, far_ref)):
        k = kv_ref[:ROWS].astype(jnp.float32)
        norm = jnp.max(jnp.sum(k * k, 1, keepdims=True))
        stat_ref[0] = jnp.where(active(slot, n_ref[0], n_ref[1]), jnp.maximum(stat_ref[0], norm), stat_ref[0])


def scale_of(total_ref):
    return lax.rsqrt(total_ref[...] / ALL_WIDE + 1e-06)


def make_queries(lin_ref, total_ref, gain_ref, q_ref, double):
    scale = jnp.broadcast_to(scale_of(total_ref), (DH, ROWS)).T
    for h in range(HEADS):
        lanes = slice(h * DH, (h + 1) * DH)
        q = (lin_ref[:, lanes].astype(jnp.float32) * scale * gain_ref[0:1, lanes]).astype(jnp.bfloat16)
        lo = jnp.zeros((ROWS, DH), jnp.bfloat16)
        if double:
            q, lo = split(q.astype(jnp.float32) * FACTOR)
        q_ref[h, :, :DH] = q
        q_ref[h, :, DH:] = lo


def ones_beside(v):
    return jnp.concatenate([v, jnp.ones((ROWS, DH), jnp.bfloat16)], 1)


def bounded_tile(kv_ref, place, slot, begin_first, q_ref, acc_ref, keep):
    kk = jnp.concatenate([kv_ref[place, :ROWS]] * 2, 1)
    key = block_of(slot) * ROWS + lax.broadcasted_iota(jnp.int32, (ROWS, 256), 0)
    inside = (key >= begin_first).astype(jnp.float32).astype(jnp.bfloat16)
    v = ones_beside(kv_ref[place, ROWS:]) * inside
    for h in range(HEADS):
        p = jnp.exp2(dot(q_ref[h], kk, NT)).astype(jnp.bfloat16)
        res = dot(p, v)
        acc_ref[h] += res * keep


def bounded_tiles(slots, kv_ref, base, n1, n2, q_ref, acc_ref, before_use):
    first, positions = rows_of()
    begin_first = start_of(first, n1, n2)

    keep = (start_of(positions, n1, n2) == begin_first).astype(jnp.float32)

    def one(slot):
        before_use(slot)
        bounded_tile(kv_ref, slot - base, slot, begin_first, q_ref, acc_ref, keep)

    def step(slot, carry):
        pl.when(active(slot, n1, n2))(lambda: one(slot))
        return carry

    lax.fori_loop(*slots, step, 0)


def make_mask(mask_ref, block, first, begin):
    row = lax.broadcasted_iota(jnp.int32, (ROWS, ROWS), 0)
    key = block * ROWS + lax.broadcasted_iota(jnp.int32, (ROWS, ROWS), 1)
    mask_ref[...] = jnp.where((key >= begin) & (key <= first + row), 0.0, FAR)


def any_tile(kv_ref, slot, base, first, begin, q_ref, acc_ref, mask_ref, top_ref):
    make_mask(mask_ref, block_of(slot), first, begin)
    kk = jnp.concatenate([kv_ref[slot - base, :ROWS]] * 2, 1)
    v = ones_beside(kv_ref[slot - base, ROWS:])

    def head(h, carry):
        s = jnp.maximum(dot(q_ref[h], kk, NT) * FACTOR + mask_ref[...], FAR)
        old = top_ref[h]
        new = jnp.maximum(old, jnp.max(s, 1, keepdims=True))
        p = jnp.exp2(s - jnp.concatenate([new] * 4, 1)).astype(jnp.bfloat16)
        fade = jnp.exp2(old - new)
        acc_ref[h] = acc_ref[h] * jnp.concatenate([fade] * 2, 1) + dot(p, v)
        top_ref[h] = new
        return carry

    lax.fori_loop(0, HEADS, head, 0)


def in_softmax_phase():
    return lax.axis_index("phase") == 1


def rows_of():
    z, x = here()
    first = (z * 4 + x) * ROWS
    return first, first + lax.broadcasted_iota(jnp.int32, (ROWS, 1), 0)


def open_kernel(
    n_ref, gauge_ref, lin_ref, total_ref, gain_ref, rows_ref, own_hbm, near_hbm, far_hbm,
    q_ref, acc_ref, top_hbm, stat_ref, kv_ref, mask_ref, top_ref, sems,
):
    @pl.when(in_softmax_phase())
    def _():
        n1, n2 = n_ref[0], n_ref[1]
        first, positions = rows_of()
        begin = start_of(positions, n1, n2)
        copies = [
            pltpu.make_async_copy(src, kv_ref.at[i], sems.at[i]) for i, src in enumerate((own_hbm, near_hbm, far_hbm))
        ]
        for copy in copies:
            copy.start()
        scale = scale_of(total_ref)
        q_most = 1.02 * jnp.max(scale * scale * rows_ref[0:1, :])
        safe = q_most * gauge_ref[0] < (SAFE / FACTOR) ** 2
        stat_ref[0] = q_most
        stat_ref[1] = jnp.where(safe, 1.0, 0.0)

        @pl.when(safe)
        def _():
            make_queries(lin_ref, total_ref, gain_ref, q_ref, True)
            make_mask(mask_ref, block_of(0), first, begin)
            for copy in copies:
                copy.wait()
            kk = jnp.concatenate([kv_ref[0, :ROWS]] * 2, 1)
            v = ones_beside(kv_ref[0, ROWS:])
            half = ROWS // 2
            for h in range(HEADS):
                for r in range(2):
                    rows, span = slice(r * half, (r + 1) * half), (r + 1) * half
                    s = dot(q_ref[h, rows, :], kk[:span], NT) + mask_ref[rows, :span]
                    acc_ref[h, rows, :] = dot(jnp.exp2(s).astype(jnp.bfloat16), v[:span])
            bounded_tiles((1, 3), kv_ref, 0, n1, n2, q_ref, acc_ref, lambda slot: None)

        @pl.when(jnp.logical_not(safe))
        def _():
            make_queries(lin_ref, total_ref, gain_ref, q_ref, False)
            acc_ref[...] = jnp.zeros_like(acc_ref)
            top_ref[...] = jnp.full(top_ref.shape, FAR, jnp.float32)
            for copy in copies:
                copy.wait()

            def step(slot, carry):
                pl.when(active(slot, n1, n2))(
                    lambda: any_tile(kv_ref, slot, 0, first, begin, q_ref, acc_ref, mask_ref, top_ref)
                )
                return carry

            lax.fori_loop(0, 3, step, 0)
            copy = pltpu.make_async_copy(top_ref, top_hbm, sems.at[0])
            copy.start()
            copy.wait()


def close_kernel(n_ref, stat_ref, lin_ref, total_ref, gain_ref, q_ref, part_ref, top_hbm, *refs):
    kv_hbm, (out_hbm, kv_ref, raw_ref, acc_ref, mask_ref, top_ref, norm_ref, out_ref, kv_sems, out_sems) = refs[:3], refs[3:]

    @pl.when(jnp.logical_not(in_softmax_phase()))
    def _():
        copy = pltpu.make_async_copy(lin_ref, out_hbm, out_sems.at[0])
        copy.start()
        copy.wait()

    @pl.when(in_softmax_phase())
    def _():
        close(
            n_ref, stat_ref, lin_ref, total_ref, gain_ref, q_ref, part_ref, top_hbm, kv_hbm,
            out_hbm, kv_ref, raw_ref, acc_ref, mask_ref, top_ref, norm_ref, out_ref, kv_sems, out_sems,
        )


def close(
    n_ref, stat_ref, lin_ref, total_ref, gain_ref, q_ref, part_ref, top_hbm, kv_hbm,
    out_hbm, kv_ref, raw_ref, acc_ref, mask_ref, top_ref, norm_ref, out_ref, kv_sems, out_sems,
):
    n1, n2 = n_ref[0], n_ref[1]
    base = 3

    def fetch(slot):
        src = kv_hbm[(slot - base) // 2].at[pl.ds((slot - base) % 2 * 2 * ROWS, 2 * ROWS)]
        return pltpu.make_async_copy(src, kv_ref.at[slot - base], kv_sems.at[slot - base])

    def arrived(slot):
        place = kv_ref.at[slot - base]
        pltpu.make_async_copy(place, place, kv_sems.at[slot - base]).wait()

    for slot in range(base, SLOTS):
        pl.when(active(slot, n1, n2))(lambda: fetch(slot).start())
    acc_ref[...] = part_ref[...]
    norm_ref[...] = jnp.zeros_like(norm_ref)
    opened_safe = stat_ref[1] > 0.5

    def before_use(slot):
        arrived(slot)
        norm_ref[...] = jnp.maximum(norm_ref[...], key_norm(kv_ref, slot - base))

    @pl.when(opened_safe)
    def _():
        bounded_tiles((base, SLOTS), kv_ref, base, n1, n2, q_ref, acc_ref, before_use)

    @pl.when(jnp.logical_not(opened_safe))
    def _():
        for slot in range(base, SLOTS):
            pl.when(active(slot, n1, n2))(lambda: arrived(slot))

    safe = opened_safe & (stat_ref[0] * jnp.max(norm_ref[...]) < (SAFE / FACTOR) ** 2)

    @pl.when(jnp.logical_not(safe))
    def _():
        first, positions = rows_of()
        begin = start_of(positions, n1, n2)
        make_queries(lin_ref, total_ref, gain_ref, raw_ref, False)
        acc_ref[...] = part_ref[...]
        top_ref[...] = jnp.zeros_like(top_ref)

        @pl.when(jnp.logical_not(opened_safe))
        def _():
            copy = pltpu.make_async_copy(top_hbm, top_ref, kv_sems.at[0])
            copy.start()
            copy.wait()

        def step(slot, carry):
            pl.when(active(slot, n1, n2))(
                lambda: any_tile(kv_ref, slot, base, first, begin, raw_ref, acc_ref, mask_ref, top_ref)
            )
            return carry

        lax.fori_loop(base, SLOTS, step, 0)

    copies = []
    for h in range(HEADS):
        lanes = slice(h * DH, (h + 1) * DH)
        out_ref[:, lanes] = (acc_ref[h, :, :DH] / acc_ref[h, :, DH:]).astype(jnp.bfloat16)
        copies.append(pltpu.make_async_copy(out_ref.at[:, lanes], out_hbm.at[:, lanes], out_sems.at[h]))
        copies[-1].start()
    for copy in copies:
        copy.wait()


VMEM = pl.BlockSpec(memory_space=pltpu.VMEM)
SMEM = pl.BlockSpec(memory_space=pltpu.SMEM)
ANY = pl.BlockSpec(memory_space=pl.ANY)


def call(kernel, outs, out_specs, args, in_specs, scratch, flops, limit):
    return pl.pallas_call(
        kernel,
        out_shape=tuple(outs),
        in_specs=in_specs,
        out_specs=tuple(out_specs),
        scratch_shapes=scratch,
        compiler_params=pltpu.CompilerParams(vmem_limit_bytes=limit << 20),
        cost_estimate=pl.CostEstimate(flops=flops, bytes_accessed=0, transcendentals=0),
    )(*args)


def shape(dims, dtype=jnp.float32):
    return jax.ShapeDtypeStruct(dims, dtype)


def stash(chunk):
    return call(stash_kernel, [shape(chunk.shape)], [VMEM], (chunk,), [ANY], [pltpu.SemaphoreType.DMA], 0, 4)[0]


def row_sum(parts):
    return call(row_sum_kernel, [shape((QUARTER, DH))], [VMEM], tuple(parts), [VMEM] * 4, [], 0, 8)[0]


def priors_of(parts, near, far):
    return call(
        prior_kernel, [shape((QUARTER, DH))] * 4, [VMEM] * 4, tuple(parts) + (near, far), [VMEM] * 6, [], 1000000000, 8
    )


def pack(own_kv, near_kv, far_kv):
    return call(
        pack_kernel,
        [shape((4 * ROWS, DH), own_kv.dtype)] * 3,
        [ANY] * 3,
        (own_kv, near_kv, far_kv),
        [ANY] * 3,
        [pltpu.SemaphoreType.DMA((6,))],
        5000000000,
        4,
    )


def states(doc_ids, key_feats, values, keys_soft, values_soft):
    bf16 = jnp.bfloat16
    return call(
        states_kernel,
        [shape((QUARTER, DH))] * 4 + [shape((2 * ROWS, DH), bf16), shape((8,), jnp.int32)],
        [VMEM] * 5 + [SMEM],
        (doc_ids.reshape(-1, DH), key_feats, values, keys_soft, values_soft),
        [ANY] * 5,
        [
            pltpu.VMEM((HEADS * FEATS, DH), jnp.float32),
            pltpu.VMEM((doc_ids.shape[0] // DH, DH), jnp.int32),
            pltpu.VMEM((ROWS, DH), bf16),
            pltpu.VMEM((ROWS, WIDE), bf16),
            pltpu.SemaphoreType.DMA((5,)),
        ],
        0,
        60,
    )


def local_part(counts, query_feats, key_feats, values):
    bf16 = jnp.bfloat16
    return call(
        local_kernel,
        [shape((ROWS, WIDE)), shape((ROWS, DH)), shape((ROWS, HEADS * 256), bf16), shape((ROWS, HEADS * 256), bf16)],
        [VMEM] * 4,
        (counts, query_feats, key_feats, values),
        [SMEM] + [VMEM] * 3,
        [pltpu.VMEM((ROWS, ROWS), jnp.float32)],
        0,
        24,
    )


def finish(counts, feats_hi, feats_lo, num, den, parts):
    return call(
        finish_kernel,
        [shape((ROWS, WIDE), jnp.bfloat16), shape((1, ROWS))],
        [VMEM] * 2,
        (counts, feats_hi, feats_lo, num, den) + tuple(parts),
        [SMEM] + [VMEM] * 8,
        [pltpu.VMEM((HEADS * FEATS, DH), jnp.float32)],
        8000000000,
        20,
    )


def gauge(counts, linear_out, gain, own_kv, near_kv, far_kv):
    return call(
        gauge_kernel,
        [shape((8, ROWS)), shape((8,))],
        [VMEM, SMEM],
        (counts, linear_out, gain, own_kv, near_kv, far_kv),
        [SMEM] + [VMEM] * 5,
        [],
        0,
        8,
    )


def soft_open(counts, gauged, linear_out, total, gain, rows, own_kv, near_kv, far_kv):
    bf16 = jnp.bfloat16
    return call(
        open_kernel,
        [shape((HEADS, ROWS, 256), bf16), shape((HEADS, ROWS, 256)), shape((HEADS, ROWS, DH)), shape((8,))],
        [VMEM, VMEM, ANY, SMEM],
        (counts, gauged, linear_out, total, gain, rows, own_kv, near_kv, far_kv),
        [SMEM] * 2 + [VMEM] * 4 + [ANY] * 3,
        [
            pltpu.VMEM((3, 2 * ROWS, DH), bf16),
            pltpu.VMEM((ROWS, ROWS), jnp.float32),
            pltpu.VMEM((HEADS, ROWS, DH), jnp.float32),
            pltpu.SemaphoreType.DMA((3,)),
        ],
        0,
        28,
    )


def soft_close(counts, stat, linear_out, total, gain, queries, part, top, pieces):
    bf16 = jnp.bfloat16
    return call(
        close_kernel,
        [shape((ROWS, WIDE), bf16)],
        [ANY],
        (counts, stat, linear_out, total, gain, queries, part, top) + tuple(pieces),
        [SMEM] * 2 + [VMEM] * 5 + [ANY] * 4,
        [
            pltpu.VMEM((SLOTS - 3, 2 * ROWS, DH), bf16),
            pltpu.VMEM((HEADS, ROWS, 256), bf16),
            pltpu.VMEM((HEADS, ROWS, 256), jnp.float32),
            pltpu.VMEM((ROWS, ROWS), jnp.float32),
            pltpu.VMEM((HEADS, ROWS, DH), jnp.float32),
            pltpu.VMEM((ROWS, 1), jnp.float32),
            pltpu.VMEM((ROWS, WIDE), bf16),
            pltpu.SemaphoreType.DMA((SLOTS - 3,)),
            pltpu.SemaphoreType.DMA((HEADS,)),
        ],
        0,
        32,
    )[0]


def shift(x, axis, by):
    size = lax.axis_size(axis)
    return lax.ppermute(x, axis, [(i, (i + by) % size) for i in range(size)])


def after(x, *others):
    return lax.optimization_barrier((x,) + others)[0]


def local(query_feats, key_feats, values, keys_soft, values_soft, norm_gain, doc_ids):
    zs = lax.axis_size("z")
    *chunks, own_kv, counts = states(doc_ids, key_feats, values, keys_soft, values_soft)

    parts = [stash(chunks[0])] + [shift(chunks[s], "x", s) for s in (1, 2, 3)]

    near_kv = lax.ppermute(own_kv, ("phase", "z"), [(zs + i, zs + i + 1) for i in range(zs - 1)])
    far_kv = lax.ppermute(own_kv, ("phase", "z"), [(i, zs + i + 2) for i in range(zs - 2)])

    local_sums = local_part(counts, query_feats, key_feats, values)
    total = row_sum(parts)
    far = lax.ppermute(
        total,
        ("phase", "z"),
        [((1 - p) * zs + i, p * zs + i + 2) for p in range(2) for i in range(zs - 2)],
    )
    near = lax.ppermute(total, "z", [(i, i + 1) for i in range(zs - 1)])

    messages = lax.optimization_barrier((total,) + tuple(pack(own_kv, near_kv, far_kv)))[1:]
    others = [
        lax.ppermute(message, ("phase", "x"), [(4 + i, 4 + (i + s) % 4) for i in range(4)])
        for s, message in zip((1, 2, 3), messages)
    ]

    far = after(far, *local_sums)
    priors = priors_of(parts, near, far)
    arrived = [priors[0]] + [shift(priors[s], "x", s) for s in (1, 2, 3)]
    num, den, feats_hi, feats_lo = local_sums
    linear_out, squares = finish(counts, feats_hi, feats_lo, num, den, arrived)
    total = squares + shift(squares, "core", 1)
    gain = norm_gain[None]
    rows, gauged = gauge(counts, linear_out, gain, own_kv, near_kv, far_kv)
    total = total + lax.ppermute(total, "y", list(enumerate((1, 0, 3, 2))))
    total = after(total, rows)
    total = total + lax.ppermute(total, "y", list(enumerate((3, 2, 1, 0))))
    queries, part, top, stat = soft_open(counts, gauged, linear_out, total, gain, rows, own_kv, near_kv, far_kv)
    return soft_close(counts, stat, linear_out, total, gain, queries, part, top, others)[None]


def solution(mesh):
    fine = Mesh(mesh.devices.reshape(2, 4, 4, 4, 2), ("phase", "z", "x", "y", "core"))
    seq, head = ("z", "x"), ("y", "core")
    return jax.shard_map(
        local,
        mesh=fine,
        in_specs=(
            P(seq, head),
            P(seq, head),
            P(seq, head),
            P(seq, head),
            P(seq, head),
            P(head),
            P(),
        ),
        out_specs=P("phase", seq, head),
        check_vma=False,
    )
```

```python
import math

import jax
import jax.numpy as jnp
from jax import lax
from jax.experimental import pallas as pl
from jax.experimental.pallas import tpu as pltpu
from jax.sharding import Mesh, PartitionSpec as P

DH = 128
F = 16
ROWS = 512
HEADS = 8
WIDE = HEADS * DH
ALL_WIDE = 64 * DH
USED = (F + 1) * (F + 2) // 2
FEATS = 160
QUARTER = HEADS * FEATS // 4
SLOTS = 9
DOC_ROW = USED + 2
LOG2E = math.log2(math.e)
FACTOR = LOG2E / math.sqrt(DH)
SAFE = 110.0
FAR = -1e30

NN = (((1,), (0,)), ((), ()))
NT = (((1,), (1,)), ((), ()))


def dot(a, b, dims=NN):
    return lax.dot_general(a, b, dims, preferred_element_type=jnp.float32)


def split(x):
    hi = x.astype(jnp.bfloat16)
    lo = (x - hi.astype(jnp.float32)).astype(jnp.bfloat16)
    return hi, lo


def doc_of(position, n1, n2):
    return (position >= n1).astype(jnp.int32) + (position >= n2).astype(jnp.int32)


def start_of(position, n1, n2):
    return jnp.where(position >= n2, n2, jnp.where(position >= n1, n1, 0))


def pair_of(e):
    gap = jnp.zeros_like(e)
    for k in range(1, F // 2 + 1):
        gap = gap + (e >= k * (F + 1)).astype(jnp.int32)
    m = e - gap * (F + 1)
    n = m + gap
    n = jnp.where(n > F, n - (F + 1), n)
    times = jnp.where((gap == 0) & (m < F), 1.0, 2.0)
    times = jnp.where(e < USED, times, 0.0)
    return m, n, times


def here():
    return lax.axis_index("z"), lax.axis_index("x")


def row_block(x, s):
    return lax.rem(x - s + 4, 4)


def same(a, b):
    return (a == b).astype(jnp.float32)


def doc_row(ref):
    return ref[DOC_ROW : DOC_ROW + 1, :]


def row_sum_kernel(p0_ref, p1_ref, p2_ref, p3_ref, out_ref):
    parts = (p0_ref, p1_ref, p2_ref, p3_ref)
    end = doc_row(p0_ref)
    for part in parts[1:]:
        end = jnp.maximum(end, doc_row(part))
    total = jnp.zeros((QUARTER, DH), jnp.float32)
    for part in parts:
        total = total + same(doc_row(part), end) * part[...]
    out_ref[...] = total
    out_ref[DOC_ROW : DOC_ROW + 1, :] = end


def prior_kernel(p0_ref, p1_ref, p2_ref, p3_ref, near_ref, far_ref, *outs):
    z, x = here()
    parts = (p0_ref, p1_ref, p2_ref, p3_ref)
    before = doc_row(near_ref)
    incoming = near_ref[...] + same(doc_row(far_ref), before) * far_ref[...]
    for t, out in enumerate(outs):
        target = lax.rem(x + t, 4)
        doc = before
        for s, part in enumerate(parts):
            doc = jnp.where(row_block(x, s) == target - 1, doc_row(part), doc)
        prior = same(before, doc) * incoming
        for s, part in enumerate(parts):
            use = jnp.where(row_block(x, s) < target, same(doc_row(part), doc), 0.0)
            prior = prior + use * part[...]
        out[...] = prior


def stash_kernel(src_hbm, out_ref, sem):
    copy = pltpu.make_async_copy(src_hbm, out_ref, sem)
    copy.start()
    copy.wait()


def pack_kernel(own_hbm, near_hbm, far_hbm, o1_hbm, o2_hbm, o3_hbm, sems):
    z, x = here()
    upper, lower = pl.ds(0, 2 * ROWS), pl.ds(2 * ROWS, 2 * ROWS)
    for s, out in enumerate((o1_hbm, o2_hbm, o3_hbm)):
        later = lax.rem(x + s + 1, 4) > x
        pltpu.make_async_copy(near_hbm, out.at[upper], sems.at[s]).start()
        pl.when(later)(lambda: pltpu.make_async_copy(own_hbm, out.at[lower], sems.at[3 + s]).start())
        pl.when(jnp.logical_not(later))(lambda: pltpu.make_async_copy(far_hbm, out.at[lower], sems.at[3 + s]).start())
    for s, out in enumerate((o1_hbm, o2_hbm, o3_hbm)):
        pltpu.make_async_copy(near_hbm, out.at[upper], sems.at[s]).wait()
        pltpu.make_async_copy(own_hbm, out.at[lower], sems.at[3 + s]).wait()


def states_kernel(doc_hbm, kf_hbm, v_hbm, k_hbm, vs_hbm, c0_ref, c1_ref, c2_ref, c3_ref, kv_ref, n_ref, state_ref, doc_ref, kf_ref, v_ref, sems):
    pairs = [(doc_hbm, doc_ref), (kf_hbm, kf_ref), (v_hbm, v_ref), (k_hbm, kv_ref.at[:ROWS]), (vs_hbm, kv_ref.at[ROWS:])]
    copies = [pltpu.make_async_copy(src, dst, sems.at[i]) for i, (src, dst) in enumerate(pairs)]
    for copy in copies:
        copy.start()
    z, x = here()
    first = (z * 4 + x) * ROWS
    m, n, times = pair_of(lax.broadcasted_iota(jnp.int32, (FEATS, 2 * F), 0))
    col = lax.broadcasted_iota(jnp.int32, (FEATS, 2 * F), 1)
    e1 = ((col == m) & (times > 0)).astype(jnp.float32).astype(jnp.bfloat16)
    e2 = ((col == n) & (times > 0)).astype(jnp.float32).astype(jnp.bfloat16)
    lane = lax.broadcasted_iota(jnp.int32, (ROWS, DH), 1)
    norms = jnp.zeros((FEATS, DH), jnp.float32)
    copies[0].wait()
    n1 = jnp.sum((doc_ref[...] < 1).astype(jnp.int32))
    n2 = jnp.sum((doc_ref[...] < 2).astype(jnp.int32))
    n_ref[0] = n1
    n_ref[1] = n2
    pos = first + lax.broadcasted_iota(jnp.int32, (F, ROWS), 1)
    sel = (doc_of(pos, n1, n2) == doc_of(first + ROWS - 1, n1, n2)).astype(jnp.float32)
    copies[1].wait()
    kt = kf_ref[...].astype(jnp.float32).T
    copies[2].wait()
    for h in range(HEADS):
        rows = jnp.concatenate([kt[h * F : (h + 1) * F] * sel, sel], 0).astype(jnp.bfloat16)
        hi, lo = split(dot(e1, rows) * dot(e2, rows))
        unit = (lane == h).astype(jnp.bfloat16)
        rhs = jnp.concatenate([v_ref[:, h * DH : (h + 1) * DH], unit], 1)
        res = dot(hi, rhs) + dot(lo, rhs)
        state_ref[h * FEATS : (h + 1) * FEATS, :] = res[:, :DH]
        norms = norms + res[:, DH:]
    across = norms.T
    for h in range(HEADS):
        base = h * FEATS + USED
        state_ref[base : base + 1, :] = across[h : h + 1, :DH]
        state_ref[base + 1 : base + 2, : FEATS - DH] = across[h : h + 1, DH:]
        last = doc_of(first + ROWS - 1, n1, n2).astype(jnp.float32)
        state_ref[base + 2 : base + 3, :] = jnp.full((1, DH), last, jnp.float32)
    for s, out in enumerate((c0_ref, c1_ref, c2_ref, c3_ref)):
        chunk = lax.rem(x + s, 4)
        out[...] = state_ref[pl.ds(pl.multiple_of(chunk * QUARTER, QUARTER), QUARTER), :]
    copies[3].wait()
    copies[4].wait()


def local_kernel(n_ref, qf_ref, kf_ref, v_ref, num_ref, den_ref, hi_ref, lo_ref, mask_ref):
    n1, n2 = n_ref[0], n_ref[1]
    z, x = here()
    first = (z * 4 + x) * ROWS
    row = lax.broadcasted_iota(jnp.int32, (ROWS, ROWS), 0)
    col = lax.broadcasted_iota(jnp.int32, (ROWS, ROWS), 1)
    begin = start_of(first + lax.broadcasted_iota(jnp.int32, (ROWS, 1), 0), n1, n2) - first
    mask_ref[...] = ((col <= row) & (col >= begin)).astype(jnp.float32)
    lane = lax.broadcasted_iota(jnp.int32, (ROWS, DH), 1)
    one = (lane == 0).astype(jnp.bfloat16)
    kf = jnp.concatenate([kf_ref[...], one], 1)
    half = ROWS // 2
    dens = [jnp.zeros((half, DH), jnp.float32) for _ in range(2)]
    for h in range(HEADS):
        qh = jnp.where(lane // F == h, qf_ref[...], jnp.zeros((), jnp.bfloat16))
        qh = jnp.concatenate([qh, one], 1)
        unit = (lane == h).astype(jnp.bfloat16)
        rhs = jnp.concatenate([v_ref[:, h * DH : (h + 1) * DH], unit], 1)
        for r in range(2):
            span = (r + 1) * half
            s = dot(qh[r * half : (r + 1) * half], kf[:span], NT)
            w = (s * s + 1.0) * mask_ref[r * half : (r + 1) * half, :span]
            hi, lo = split(w)
            res = dot(hi, rhs[:span]) + dot(lo, rhs[:span])
            num_ref[r * half : (r + 1) * half, h * DH : (h + 1) * DH] = res[:, :DH]
            dens[r] = dens[r] + res[:, DH:]
    for r in range(2):
        den_ref[r * half : (r + 1) * half, :] = dens[r]
    m, n, times = pair_of(lax.broadcasted_iota(jnp.int32, (DH, 256), 1))
    lane_row = lax.broadcasted_iota(jnp.int32, (DH, 256), 0)
    m1, n1_, times1 = pair_of(lax.broadcasted_iota(jnp.int32, (1, 256), 1))
    ones_a = jnp.where(m1 == F, times1, 0.0)
    ones_b = jnp.where((n1_ == F) & (times1 > 0), 1.0, 0.0)
    once = (times > 0).astype(jnp.float32)
    q = qf_ref[...]
    for h in range(HEADS):
        e1 = jnp.where((lane_row == m + h * F) & (m < F), times, 0.0).astype(jnp.bfloat16)
        e2 = jnp.where((lane_row == n + h * F) & (n < F), once, 0.0).astype(jnp.bfloat16)
        hi, lo = split((dot(q, e1) + ones_a) * (dot(q, e2) + ones_b))
        hi_ref[:, h * 256 : (h + 1) * 256] = hi
        lo_ref[:, h * 256 : (h + 1) * 256] = lo


def finish_kernel(n_ref, hi_ref, lo_ref, num_ref, den_ref, p0_ref, p1_ref, p2_ref, p3_ref, out_ref, sq_ref, prior_ref):
    n1, n2 = n_ref[0], n_ref[1]
    z, x = here()
    first = (z * 4 + x) * ROWS
    pos = first + lax.broadcasted_iota(jnp.int32, (ROWS, 1), 0)
    usable = ((doc_of(pos, n1, n2) == doc_of(first - 1, n1, n2)) & (first > 0)).astype(jnp.float32)
    for s, part in enumerate((p0_ref, p1_ref, p2_ref, p3_ref)):
        chunk = lax.rem(x - s + 4, 4)
        prior_ref[pl.ds(pl.multiple_of(chunk * QUARTER, QUARTER), QUARTER), :] = part[...]
    spare = [jnp.zeros((DH - HEADS, DH), jnp.float32)]
    sums = [[prior_ref[h * FEATS + USED + i : h * FEATS + USED + i + 1, :] for h in range(HEADS)] for i in range(2)]
    norm = jnp.concatenate([jnp.concatenate(rows + spare, 0).T for rows in sums], 0)[:FEATS]
    norm_hi, norm_lo = split(norm)
    squares = jnp.zeros((ROWS, DH), jnp.float32)
    for h in range(HEADS):
        hi = hi_ref[:, h * 256 : h * 256 + FEATS]
        lo = lo_ref[:, h * 256 : h * 256 + FEATS]
        s_hi, s_lo = split(prior_ref[h * FEATS : (h + 1) * FEATS, :])
        r_hi = jnp.concatenate([s_hi, norm_hi], 1)
        r_lo = jnp.concatenate([s_lo, norm_lo], 1)
        res = dot(jnp.concatenate([hi, lo], 0), r_hi)
        res = (res[:ROWS] + (res[ROWS:] + dot(hi, r_lo))) * usable
        num = num_ref[:, h * DH : (h + 1) * DH] + res[:, :DH]
        den = den_ref[:, h : h + 1] + res[:, DH + h : DH + h + 1]
        out = (num / den).astype(jnp.bfloat16)
        out_ref[:, h * DH : (h + 1) * DH] = out
        wide = out.astype(jnp.float32)
        squares = squares + wide * wide
    sq_ref[...] = jnp.sum(squares.T, 0, keepdims=True)


def block_of(slot):
    z, x = here()
    src = lax.rem(x + 4 - lax.div(slot - 1, 2), 4)
    behind = jnp.where(lax.rem(slot, 2) == 1, 1, jnp.where(src < x, 0, 2))
    return jnp.where(slot < 3, z * 4 + x - 4 * slot, (z - behind) * 4 + src)


def active(slot, n1, n2):
    z, x = here()
    own = z * 4 + x
    low = start_of(own * ROWS, n1, n2) // ROWS
    return (block_of(slot) >= low) & (block_of(slot) < own) | (slot == 0)


def key_norm(kv_ref, place):
    k = kv_ref[place, :ROWS].astype(jnp.float32)
    return jnp.sum(k * k, 1, keepdims=True)


def gauge_kernel(n_ref, lin_ref, gain_ref, own_ref, near_ref, far_ref, rows_ref, stat_ref):
    most = jnp.zeros((ROWS, 1), jnp.float32)
    for h in range(HEADS):
        lanes = slice(h * DH, (h + 1) * DH)
        q = lin_ref[:, lanes].astype(jnp.float32) * gain_ref[0:1, lanes]
        most = jnp.maximum(most, jnp.sum(q * q, 1, keepdims=True))
    rows_ref[...] = jnp.broadcast_to(most, (ROWS, DH)).T[:8]
    stat_ref[0] = 0.0
    for slot, kv_ref in enumerate((own_ref, near_ref, far_ref)):
        k = kv_ref[:ROWS].astype(jnp.float32)
        norm = jnp.max(jnp.sum(k * k, 1, keepdims=True))
        stat_ref[0] = jnp.where(active(slot, n_ref[0], n_ref[1]), jnp.maximum(stat_ref[0], norm), stat_ref[0])


def scale_of(total_ref):
    return lax.rsqrt(total_ref[...] / ALL_WIDE + 1e-06)


def make_queries(lin_ref, total_ref, gain_ref, q_ref, double):
    scale = jnp.broadcast_to(scale_of(total_ref), (DH, ROWS)).T
    for h in range(HEADS):
        lanes = slice(h * DH, (h + 1) * DH)
        q = (lin_ref[:, lanes].astype(jnp.float32) * scale * gain_ref[0:1, lanes]).astype(jnp.bfloat16)
        lo = jnp.zeros((ROWS, DH), jnp.bfloat16)
        if double:
            q, lo = split(q.astype(jnp.float32) * FACTOR)
        q_ref[h, :, :DH] = q
        q_ref[h, :, DH:] = lo


def ones_beside(v):
    return jnp.concatenate([v, jnp.ones((ROWS, DH), jnp.bfloat16)], 1)


def bounded_tile(kv_ref, place, slot, begin_first, q_ref, acc_ref, keep):
    kk = jnp.concatenate([kv_ref[place, :ROWS]] * 2, 1)
    key = block_of(slot) * ROWS + lax.broadcasted_iota(jnp.int32, (ROWS, 256), 0)
    inside = (key >= begin_first).astype(jnp.float32).astype(jnp.bfloat16)
    v = ones_beside(kv_ref[place, ROWS:]) * inside
    for h in range(HEADS):
        p = jnp.exp2(dot(q_ref[h], kk, NT)).astype(jnp.bfloat16)
        res = dot(p, v)
        acc_ref[h] += res * keep


def bounded_tiles(slots, kv_ref, base, n1, n2, q_ref, acc_ref, before_use):
    first, positions = rows_of()
    begin_first = start_of(first, n1, n2)

    keep = (start_of(positions, n1, n2) == begin_first).astype(jnp.float32)

    def one(slot):
        before_use(slot)
        bounded_tile(kv_ref, slot - base, slot, begin_first, q_ref, acc_ref, keep)

    def step(slot, carry):
        pl.when(active(slot, n1, n2))(lambda: one(slot))
        return carry

    lax.fori_loop(*slots, step, 0)


def make_mask(mask_ref, block, first, begin):
    row = lax.broadcasted_iota(jnp.int32, (ROWS, ROWS), 0)
    key = block * ROWS + lax.broadcasted_iota(jnp.int32, (ROWS, ROWS), 1)
    mask_ref[...] = jnp.where((key >= begin) & (key <= first + row), 0.0, FAR)


def any_tile(kv_ref, slot, base, first, begin, q_ref, acc_ref, mask_ref, top_ref):
    make_mask(mask_ref, block_of(slot), first, begin)
    kk = jnp.concatenate([kv_ref[slot - base, :ROWS]] * 2, 1)
    v = ones_beside(kv_ref[slot - base, ROWS:])

    def head(h, carry):
        s = jnp.maximum(dot(q_ref[h], kk, NT) * FACTOR + mask_ref[...], FAR)
        old = top_ref[h]
        new = jnp.maximum(old, jnp.max(s, 1, keepdims=True))
        p = jnp.exp2(s - jnp.concatenate([new] * 4, 1)).astype(jnp.bfloat16)
        fade = jnp.exp2(old - new)
        acc_ref[h] = acc_ref[h] * jnp.concatenate([fade] * 2, 1) + dot(p, v)
        top_ref[h] = new
        return carry

    lax.fori_loop(0, HEADS, head, 0)


def in_softmax_phase():
    return lax.axis_index("phase") == 1


def rows_of():
    z, x = here()
    first = (z * 4 + x) * ROWS
    return first, first + lax.broadcasted_iota(jnp.int32, (ROWS, 1), 0)


def open_kernel(
    n_ref, gauge_ref, lin_ref, total_ref, gain_ref, rows_ref, own_hbm, near_hbm, far_hbm,
    q_ref, acc_ref, top_hbm, stat_ref, kv_ref, mask_ref, top_ref, sems,
):
    @pl.when(in_softmax_phase())
    def _():
        n1, n2 = n_ref[0], n_ref[1]
        first, positions = rows_of()
        begin = start_of(positions, n1, n2)
        copies = [
            pltpu.make_async_copy(src, kv_ref.at[i], sems.at[i]) for i, src in enumerate((own_hbm, near_hbm, far_hbm))
        ]
        for copy in copies:
            copy.start()
        scale = scale_of(total_ref)
        q_most = 1.02 * jnp.max(scale * scale * rows_ref[0:1, :])
        safe = q_most * gauge_ref[0] < (SAFE / FACTOR) ** 2
        stat_ref[0] = q_most
        stat_ref[1] = jnp.where(safe, 1.0, 0.0)

        @pl.when(safe)
        def _():
            make_queries(lin_ref, total_ref, gain_ref, q_ref, True)
            make_mask(mask_ref, block_of(0), first, begin)
            for copy in copies:
                copy.wait()
            kk = jnp.concatenate([kv_ref[0, :ROWS]] * 2, 1)
            v = ones_beside(kv_ref[0, ROWS:])
            half = ROWS // 2
            for h in range(HEADS):
                for r in range(2):
                    rows, span = slice(r * half, (r + 1) * half), (r + 1) * half
                    s = dot(q_ref[h, rows, :], kk[:span], NT) + mask_ref[rows, :span]
                    acc_ref[h, rows, :] = dot(jnp.exp2(s).astype(jnp.bfloat16), v[:span])
            bounded_tiles((1, 3), kv_ref, 0, n1, n2, q_ref, acc_ref, lambda slot: None)

        @pl.when(jnp.logical_not(safe))
        def _():
            make_queries(lin_ref, total_ref, gain_ref, q_ref, False)
            acc_ref[...] = jnp.zeros_like(acc_ref)
            top_ref[...] = jnp.full(top_ref.shape, FAR, jnp.float32)
            for copy in copies:
                copy.wait()

            def step(slot, carry):
                pl.when(active(slot, n1, n2))(
                    lambda: any_tile(kv_ref, slot, 0, first, begin, q_ref, acc_ref, mask_ref, top_ref)
                )
                return carry

            lax.fori_loop(0, 3, step, 0)
            copy = pltpu.make_async_copy(top_ref, top_hbm, sems.at[0])
            copy.start()
            copy.wait()


def close_kernel(n_ref, stat_ref, lin_ref, total_ref, gain_ref, q_ref, part_ref, top_hbm, *refs):
    kv_hbm, (out_hbm, kv_ref, raw_ref, acc_ref, mask_ref, top_ref, norm_ref, out_ref, kv_sems, out_sems) = refs[:3], refs[3:]

    @pl.when(jnp.logical_not(in_softmax_phase()))
    def _():
        copy = pltpu.make_async_copy(lin_ref, out_hbm, out_sems.at[0])
        copy.start()
        copy.wait()

    @pl.when(in_softmax_phase())
    def _():
        close(
            n_ref, stat_ref, lin_ref, total_ref, gain_ref, q_ref, part_ref, top_hbm, kv_hbm,
            out_hbm, kv_ref, raw_ref, acc_ref, mask_ref, top_ref, norm_ref, out_ref, kv_sems, out_sems,
        )


def close(
    n_ref, stat_ref, lin_ref, total_ref, gain_ref, q_ref, part_ref, top_hbm, kv_hbm,
    out_hbm, kv_ref, raw_ref, acc_ref, mask_ref, top_ref, norm_ref, out_ref, kv_sems, out_sems,
):
    n1, n2 = n_ref[0], n_ref[1]
    base = 3

    def fetch(slot):
        src = kv_hbm[(slot - base) // 2].at[pl.ds((slot - base) % 2 * 2 * ROWS, 2 * ROWS)]
        return pltpu.make_async_copy(src, kv_ref.at[slot - base], kv_sems.at[slot - base])

    def arrived(slot):
        place = kv_ref.at[slot - base]
        pltpu.make_async_copy(place, place, kv_sems.at[slot - base]).wait()

    for slot in range(base, SLOTS):
        pl.when(active(slot, n1, n2))(lambda: fetch(slot).start())
    acc_ref[...] = part_ref[...]
    norm_ref[...] = jnp.zeros_like(norm_ref)
    opened_safe = stat_ref[1] > 0.5

    def before_use(slot):
        arrived(slot)
        norm_ref[...] = jnp.maximum(norm_ref[...], key_norm(kv_ref, slot - base))

    @pl.when(opened_safe)
    def _():
        bounded_tiles((base, SLOTS), kv_ref, base, n1, n2, q_ref, acc_ref, before_use)

    @pl.when(jnp.logical_not(opened_safe))
    def _():
        for slot in range(base, SLOTS):
            pl.when(active(slot, n1, n2))(lambda: arrived(slot))

    safe = opened_safe & (stat_ref[0] * jnp.max(norm_ref[...]) < (SAFE / FACTOR) ** 2)

    @pl.when(jnp.logical_not(safe))
    def _():
        first, positions = rows_of()
        begin = start_of(positions, n1, n2)
        make_queries(lin_ref, total_ref, gain_ref, raw_ref, False)
        acc_ref[...] = part_ref[...]
        top_ref[...] = jnp.zeros_like(top_ref)

        @pl.when(jnp.logical_not(opened_safe))
        def _():
            copy = pltpu.make_async_copy(top_hbm, top_ref, kv_sems.at[0])
            copy.start()
            copy.wait()

        def step(slot, carry):
            pl.when(active(slot, n1, n2))(
                lambda: any_tile(kv_ref, slot, base, first, begin, raw_ref, acc_ref, mask_ref, top_ref)
            )
            return carry

        lax.fori_loop(base, SLOTS, step, 0)

    copies = []
    for h in range(HEADS):
        lanes = slice(h * DH, (h + 1) * DH)
        out_ref[:, lanes] = (acc_ref[h, :, :DH] / acc_ref[h, :, DH:]).astype(jnp.bfloat16)
        copies.append(pltpu.make_async_copy(out_ref.at[:, lanes], out_hbm.at[:, lanes], out_sems.at[h]))
        copies[-1].start()
    for copy in copies:
        copy.wait()


VMEM = pl.BlockSpec(memory_space=pltpu.VMEM)
SMEM = pl.BlockSpec(memory_space=pltpu.SMEM)
ANY = pl.BlockSpec(memory_space=pl.ANY)


def call(kernel, outs, out_specs, args, in_specs, scratch, flops, limit):
    return pl.pallas_call(
        kernel,
        out_shape=tuple(outs),
        in_specs=in_specs,
        out_specs=tuple(out_specs),
        scratch_shapes=scratch,
        compiler_params=pltpu.CompilerParams(vmem_limit_bytes=limit << 20),
        cost_estimate=pl.CostEstimate(flops=flops, bytes_accessed=0, transcendentals=0),
    )(*args)


def shape(dims, dtype=jnp.float32):
    return jax.ShapeDtypeStruct(dims, dtype)


def stash(chunk):
    return call(stash_kernel, [shape(chunk.shape)], [VMEM], (chunk,), [ANY], [pltpu.SemaphoreType.DMA], 0, 4)[0]


def row_sum(parts):
    return call(row_sum_kernel, [shape((QUARTER, DH))], [VMEM], tuple(parts), [VMEM] * 4, [], 0, 8)[0]


def priors_of(parts, near, far):
    return call(
        prior_kernel, [shape((QUARTER, DH))] * 4, [VMEM] * 4, tuple(parts) + (near, far), [VMEM] * 6, [], 1000000000, 8
    )


def pack(own_kv, near_kv, far_kv):
    return call(
        pack_kernel,
        [shape((4 * ROWS, DH), own_kv.dtype)] * 3,
        [ANY] * 3,
        (own_kv, near_kv, far_kv),
        [ANY] * 3,
        [pltpu.SemaphoreType.DMA((6,))],
        5000000000,
        4,
    )


def states(doc_ids, key_feats, values, keys_soft, values_soft):
    bf16 = jnp.bfloat16
    return call(
        states_kernel,
        [shape((QUARTER, DH))] * 4 + [shape((2 * ROWS, DH), bf16), shape((8,), jnp.int32)],
        [VMEM] * 5 + [SMEM],
        (doc_ids.reshape(-1, DH), key_feats, values, keys_soft, values_soft),
        [ANY] * 5,
        [
            pltpu.VMEM((HEADS * FEATS, DH), jnp.float32),
            pltpu.VMEM((doc_ids.shape[0] // DH, DH), jnp.int32),
            pltpu.VMEM((ROWS, DH), bf16),
            pltpu.VMEM((ROWS, WIDE), bf16),
            pltpu.SemaphoreType.DMA((5,)),
        ],
        0,
        60,
    )


def local_part(counts, query_feats, key_feats, values):
    bf16 = jnp.bfloat16
    return call(
        local_kernel,
        [shape((ROWS, WIDE)), shape((ROWS, DH)), shape((ROWS, HEADS * 256), bf16), shape((ROWS, HEADS * 256), bf16)],
        [VMEM] * 4,
        (counts, query_feats, key_feats, values),
        [SMEM] + [VMEM] * 3,
        [pltpu.VMEM((ROWS, ROWS), jnp.float32)],
        0,
        24,
    )


def finish(counts, feats_hi, feats_lo, num, den, parts):
    return call(
        finish_kernel,
        [shape((ROWS, WIDE), jnp.bfloat16), shape((1, ROWS))],
        [VMEM] * 2,
        (counts, feats_hi, feats_lo, num, den) + tuple(parts),
        [SMEM] + [VMEM] * 8,
        [pltpu.VMEM((HEADS * FEATS, DH), jnp.float32)],
        8000000000,
        20,
    )


def gauge(counts, linear_out, gain, own_kv, near_kv, far_kv):
    return call(
        gauge_kernel,
        [shape((8, ROWS)), shape((8,))],
        [VMEM, SMEM],
        (counts, linear_out, gain, own_kv, near_kv, far_kv),
        [SMEM] + [VMEM] * 5,
        [],
        0,
        8,
    )


def soft_open(counts, gauged, linear_out, total, gain, rows, own_kv, near_kv, far_kv):
    bf16 = jnp.bfloat16
    return call(
        open_kernel,
        [shape((HEADS, ROWS, 256), bf16), shape((HEADS, ROWS, 256)), shape((HEADS, ROWS, DH)), shape((8,))],
        [VMEM, VMEM, ANY, SMEM],
        (counts, gauged, linear_out, total, gain, rows, own_kv, near_kv, far_kv),
        [SMEM] * 2 + [VMEM] * 4 + [ANY] * 3,
        [
            pltpu.VMEM((3, 2 * ROWS, DH), bf16),
            pltpu.VMEM((ROWS, ROWS), jnp.float32),
            pltpu.VMEM((HEADS, ROWS, DH), jnp.float32),
            pltpu.SemaphoreType.DMA((3,)),
        ],
        0,
        28,
    )


def soft_close(counts, stat, linear_out, total, gain, queries, part, top, pieces):
    bf16 = jnp.bfloat16
    return call(
        close_kernel,
        [shape((ROWS, WIDE), bf16)],
        [ANY],
        (counts, stat, linear_out, total, gain, queries, part, top) + tuple(pieces),
        [SMEM] * 2 + [VMEM] * 5 + [ANY] * 4,
        [
            pltpu.VMEM((SLOTS - 3, 2 * ROWS, DH), bf16),
            pltpu.VMEM((HEADS, ROWS, 256), bf16),
            pltpu.VMEM((HEADS, ROWS, 256), jnp.float32),
            pltpu.VMEM((ROWS, ROWS), jnp.float32),
            pltpu.VMEM((HEADS, ROWS, DH), jnp.float32),
            pltpu.VMEM((ROWS, 1), jnp.float32),
            pltpu.VMEM((ROWS, WIDE), bf16),
            pltpu.SemaphoreType.DMA((SLOTS - 3,)),
            pltpu.SemaphoreType.DMA((HEADS,)),
        ],
        0,
        32,
    )[0]


def shift(x, axis, by):
    size = lax.axis_size(axis)
    return lax.ppermute(x, axis, [(i, (i + by) % size) for i in range(size)])


def after(x, *others):
    return lax.optimization_barrier((x,) + others)[0]


def local(query_feats, key_feats, values, keys_soft, values_soft, norm_gain, doc_ids):
    zs = lax.axis_size("z")
    *chunks, own_kv, counts = states(doc_ids, key_feats, values, keys_soft, values_soft)

    parts = [stash(chunks[0])] + [shift(chunks[s], "x", s) for s in (1, 2, 3)]

    near_kv = lax.ppermute(own_kv, ("phase", "z"), [(zs + i, zs + i + 1) for i in range(zs - 1)])
    far_kv = lax.ppermute(own_kv, ("phase", "z"), [(i if i % 2 else zs + i, zs + i + 2) for i in range(zs - 2)])

    local_sums = local_part(counts, query_feats, key_feats, values)
    total = row_sum(parts)
    far = lax.ppermute(
        total,
        ("phase", "z"),
        [((1 - p) * zs + i, p * zs + i + 2) for p in range(2) for i in range(zs - 2)],
    )
    near = lax.ppermute(total, "z", [(i, i + 1) for i in range(zs - 1)])

    messages = lax.optimization_barrier((total,) + tuple(pack(own_kv, near_kv, far_kv)))[1:]
    others = [
        lax.ppermute(message, ("phase", "x"), [(4 + i, 4 + (i + s) % 4) for i in range(4)])
        for s, message in zip((1, 2, 3), messages)
    ]

    far = after(far, *local_sums)
    priors = priors_of(parts, near, far)
    arrived = [priors[0]] + [shift(priors[s], "x", s) for s in (1, 2, 3)]
    num, den, feats_hi, feats_lo = local_sums
    linear_out, squares = finish(counts, feats_hi, feats_lo, num, den, arrived)
    total = squares + shift(squares, "core", 1)
    gain = norm_gain[None]
    rows, gauged = gauge(counts, linear_out, gain, own_kv, near_kv, far_kv)
    total = total + lax.ppermute(total, "y", list(enumerate((1, 0, 3, 2))))
    total = after(total, rows)
    total = total + lax.ppermute(total, "y", list(enumerate((3, 2, 1, 0))))
    queries, part, top, stat = soft_open(counts, gauged, linear_out, total, gain, rows, own_kv, near_kv, far_kv)
    return soft_close(counts, stat, linear_out, total, gain, queries, part, top, others)[None]


def solution(mesh):
    fine = Mesh(mesh.devices.reshape(2, 4, 4, 4, 2), ("phase", "z", "x", "y", "core"))
    seq, head = ("z", "x"), ("y", "core")
    return jax.shard_map(
        local,
        mesh=fine,
        in_specs=(
            P(seq, head),
            P(seq, head),
            P(seq, head),
            P(seq, head),
            P(seq, head),
            P(head),
            P(),
        ),
        out_specs=P("phase", seq, head),
        check_vma=False,
    )
```

```python
import math

import jax
import jax.numpy as jnp
from jax import lax
from jax.experimental import pallas as pl
from jax.experimental.pallas import tpu as pltpu
from jax.sharding import Mesh, PartitionSpec as P

DH = 128
F = 16
ROWS = 512
HEADS = 8
WIDE = HEADS * DH
ALL_WIDE = 64 * DH
USED = (F + 1) * (F + 2) // 2
FEATS = 160
QUARTER = HEADS * FEATS // 4
SLOTS = 9
DOC_ROW = USED + 2
LOG2E = math.log2(math.e)
FACTOR = LOG2E / math.sqrt(DH)
SAFE = 110.0
FAR = -1e30

NN = (((1,), (0,)), ((), ()))
NT = (((1,), (1,)), ((), ()))


def dot(a, b, dims=NN):
    return lax.dot_general(a, b, dims, preferred_element_type=jnp.float32)


def split(x):
    hi = x.astype(jnp.bfloat16)
    lo = (x - hi.astype(jnp.float32)).astype(jnp.bfloat16)
    return hi, lo


def doc_of(position, n1, n2):
    return (position >= n1).astype(jnp.int32) + (position >= n2).astype(jnp.int32)


def start_of(position, n1, n2):
    return jnp.where(position >= n2, n2, jnp.where(position >= n1, n1, 0))


def pair_of(e):
    gap = jnp.zeros_like(e)
    for k in range(1, F // 2 + 1):
        gap = gap + (e >= k * (F + 1)).astype(jnp.int32)
    m = e - gap * (F + 1)
    n = m + gap
    n = jnp.where(n > F, n - (F + 1), n)
    times = jnp.where((gap == 0) & (m < F), 1.0, 2.0)
    times = jnp.where(e < USED, times, 0.0)
    return m, n, times


def here():
    return lax.axis_index("z"), lax.axis_index("x")


def row_block(x, s):
    return lax.rem(x - s + 4, 4)


def same(a, b):
    return (a == b).astype(jnp.float32)


def doc_row(ref):
    return ref[DOC_ROW : DOC_ROW + 1, :]


def row_sum_kernel(p0_ref, p1_ref, p2_ref, p3_ref, out_ref):
    parts = (p0_ref, p1_ref, p2_ref, p3_ref)
    end = doc_row(p0_ref)
    for part in parts[1:]:
        end = jnp.maximum(end, doc_row(part))
    total = jnp.zeros((QUARTER, DH), jnp.float32)
    for part in parts:
        total = total + same(doc_row(part), end) * part[...]
    out_ref[...] = total
    out_ref[DOC_ROW : DOC_ROW + 1, :] = end


def prior_kernel(p0_ref, p1_ref, p2_ref, p3_ref, near_ref, far_ref, *outs):
    z, x = here()
    parts = (p0_ref, p1_ref, p2_ref, p3_ref)
    before = doc_row(near_ref)
    incoming = near_ref[...] + same(doc_row(far_ref), before) * far_ref[...]
    for t, out in enumerate(outs):
        target = lax.rem(x + t, 4)
        doc = before
        for s, part in enumerate(parts):
            doc = jnp.where(row_block(x, s) == target - 1, doc_row(part), doc)
        prior = same(before, doc) * incoming
        for s, part in enumerate(parts):
            use = jnp.where(row_block(x, s) < target, same(doc_row(part), doc), 0.0)
            prior = prior + use * part[...]
        out[...] = prior


def stash_kernel(src_hbm, out_ref, sem):
    copy = pltpu.make_async_copy(src_hbm, out_ref, sem)
    copy.start()
    copy.wait()


def pack_kernel(own_hbm, near_hbm, far_hbm, o1_hbm, o2_hbm, o3_hbm, sems):
    z, x = here()
    upper, lower = pl.ds(0, 2 * ROWS), pl.ds(2 * ROWS, 2 * ROWS)
    for s, out in enumerate((o1_hbm, o2_hbm, o3_hbm)):
        later = lax.rem(x + s + 1, 4) > x
        pltpu.make_async_copy(near_hbm, out.at[upper], sems.at[s]).start()
        pl.when(later)(lambda: pltpu.make_async_copy(own_hbm, out.at[lower], sems.at[3 + s]).start())
        pl.when(jnp.logical_not(later))(lambda: pltpu.make_async_copy(far_hbm, out.at[lower], sems.at[3 + s]).start())
    for s, out in enumerate((o1_hbm, o2_hbm, o3_hbm)):
        pltpu.make_async_copy(near_hbm, out.at[upper], sems.at[s]).wait()
        pltpu.make_async_copy(own_hbm, out.at[lower], sems.at[3 + s]).wait()


def states_kernel(doc_hbm, kf_hbm, v_hbm, k_hbm, vs_hbm, c0_ref, c1_ref, c2_ref, c3_ref, kv_ref, n_ref, state_ref, doc_ref, kf_ref, v_ref, sems):
    pairs = [(doc_hbm, doc_ref), (kf_hbm, kf_ref), (v_hbm, v_ref), (k_hbm, kv_ref.at[:ROWS]), (vs_hbm, kv_ref.at[ROWS:])]
    copies = [pltpu.make_async_copy(src, dst, sems.at[i]) for i, (src, dst) in enumerate(pairs)]
    for copy in copies:
        copy.start()
    z, x = here()
    first = (z * 4 + x) * ROWS
    m, n, times = pair_of(lax.broadcasted_iota(jnp.int32, (FEATS, 2 * F), 0))
    col = lax.broadcasted_iota(jnp.int32, (FEATS, 2 * F), 1)
    e1 = ((col == m) & (times > 0)).astype(jnp.float32).astype(jnp.bfloat16)
    e2 = ((col == n) & (times > 0)).astype(jnp.float32).astype(jnp.bfloat16)
    lane = lax.broadcasted_iota(jnp.int32, (ROWS, DH), 1)
    norms = jnp.zeros((FEATS, DH), jnp.float32)
    copies[0].wait()
    n1 = jnp.sum((doc_ref[...] < 1).astype(jnp.int32))
    n2 = jnp.sum((doc_ref[...] < 2).astype(jnp.int32))
    n_ref[0] = n1
    n_ref[1] = n2
    pos = first + lax.broadcasted_iota(jnp.int32, (F, ROWS), 1)
    sel = (doc_of(pos, n1, n2) == doc_of(first + ROWS - 1, n1, n2)).astype(jnp.float32)
    copies[1].wait()
    kt = kf_ref[...].astype(jnp.float32).T
    copies[2].wait()
    for h in range(HEADS):
        rows = jnp.concatenate([kt[h * F : (h + 1) * F] * sel, sel], 0).astype(jnp.bfloat16)
        hi, lo = split(dot(e1, rows) * dot(e2, rows))
        unit = (lane == h).astype(jnp.bfloat16)
        rhs = jnp.concatenate([v_ref[:, h * DH : (h + 1) * DH], unit], 1)
        res = dot(hi, rhs) + dot(lo, rhs)
        state_ref[h * FEATS : (h + 1) * FEATS, :] = res[:, :DH]
        norms = norms + res[:, DH:]
    across = norms.T
    for h in range(HEADS):
        base = h * FEATS + USED
        state_ref[base : base + 1, :] = across[h : h + 1, :DH]
        state_ref[base + 1 : base + 2, : FEATS - DH] = across[h : h + 1, DH:]
        last = doc_of(first + ROWS - 1, n1, n2).astype(jnp.float32)
        state_ref[base + 2 : base + 3, :] = jnp.full((1, DH), last, jnp.float32)
    for s, out in enumerate((c0_ref, c1_ref, c2_ref, c3_ref)):
        chunk = lax.rem(x + s, 4)
        out[...] = state_ref[pl.ds(pl.multiple_of(chunk * QUARTER, QUARTER), QUARTER), :]
    copies[3].wait()
    copies[4].wait()


def local_kernel(n_ref, qf_ref, kf_ref, v_ref, num_ref, den_ref, hi_ref, lo_ref, mask_ref):
    n1, n2 = n_ref[0], n_ref[1]
    z, x = here()
    first = (z * 4 + x) * ROWS
    row = lax.broadcasted_iota(jnp.int32, (ROWS, ROWS), 0)
    col = lax.broadcasted_iota(jnp.int32, (ROWS, ROWS), 1)
    begin = start_of(first + lax.broadcasted_iota(jnp.int32, (ROWS, 1), 0), n1, n2) - first
    mask_ref[...] = ((col <= row) & (col >= begin)).astype(jnp.float32)
    lane = lax.broadcasted_iota(jnp.int32, (ROWS, DH), 1)
    one = (lane == 0).astype(jnp.bfloat16)
    kf = jnp.concatenate([kf_ref[...], one], 1)
    half = ROWS // 2
    dens = [jnp.zeros((half, DH), jnp.float32) for _ in range(2)]
    for h in range(HEADS):
        qh = jnp.where(lane // F == h, qf_ref[...], jnp.zeros((), jnp.bfloat16))
        qh = jnp.concatenate([qh, one], 1)
        unit = (lane == h).astype(jnp.bfloat16)
        rhs = jnp.concatenate([v_ref[:, h * DH : (h + 1) * DH], unit], 1)
        for r in range(2):
            span = (r + 1) * half
            s = dot(qh[r * half : (r + 1) * half], kf[:span], NT)
            w = (s * s + 1.0) * mask_ref[r * half : (r + 1) * half, :span]
            hi, lo = split(w)
            res = dot(hi, rhs[:span]) + dot(lo, rhs[:span])
            num_ref[r * half : (r + 1) * half, h * DH : (h + 1) * DH] = res[:, :DH]
            dens[r] = dens[r] + res[:, DH:]
    for r in range(2):
        den_ref[r * half : (r + 1) * half, :] = dens[r]
    m, n, times = pair_of(lax.broadcasted_iota(jnp.int32, (DH, 256), 1))
    lane_row = lax.broadcasted_iota(jnp.int32, (DH, 256), 0)
    m1, n1_, times1 = pair_of(lax.broadcasted_iota(jnp.int32, (1, 256), 1))
    ones_a = jnp.where(m1 == F, times1, 0.0)
    ones_b = jnp.where((n1_ == F) & (times1 > 0), 1.0, 0.0)
    once = (times > 0).astype(jnp.float32)
    q = qf_ref[...]
    for h in range(HEADS):
        e1 = jnp.where((lane_row == m + h * F) & (m < F), times, 0.0).astype(jnp.bfloat16)
        e2 = jnp.where((lane_row == n + h * F) & (n < F), once, 0.0).astype(jnp.bfloat16)
        hi, lo = split((dot(q, e1) + ones_a) * (dot(q, e2) + ones_b))
        hi_ref[:, h * 256 : (h + 1) * 256] = hi
        lo_ref[:, h * 256 : (h + 1) * 256] = lo


def finish_kernel(n_ref, hi_ref, lo_ref, num_ref, den_ref, p0_ref, p1_ref, p2_ref, p3_ref, out_ref, sq_ref, prior_ref):
    n1, n2 = n_ref[0], n_ref[1]
    z, x = here()
    first = (z * 4 + x) * ROWS
    pos = first + lax.broadcasted_iota(jnp.int32, (ROWS, 1), 0)
    usable = ((doc_of(pos, n1, n2) == doc_of(first - 1, n1, n2)) & (first > 0)).astype(jnp.float32)
    for s, part in enumerate((p0_ref, p1_ref, p2_ref, p3_ref)):
        chunk = lax.rem(x - s + 4, 4)
        prior_ref[pl.ds(pl.multiple_of(chunk * QUARTER, QUARTER), QUARTER), :] = part[...]
    spare = [jnp.zeros((DH - HEADS, DH), jnp.float32)]
    sums = [[prior_ref[h * FEATS + USED + i : h * FEATS + USED + i + 1, :] for h in range(HEADS)] for i in range(2)]
    norm = jnp.concatenate([jnp.concatenate(rows + spare, 0).T for rows in sums], 0)[:FEATS]
    norm_hi, norm_lo = split(norm)
    squares = jnp.zeros((ROWS, DH), jnp.float32)
    for h in range(HEADS):
        hi = hi_ref[:, h * 256 : h * 256 + FEATS]
        lo = lo_ref[:, h * 256 : h * 256 + FEATS]
        s_hi, s_lo = split(prior_ref[h * FEATS : (h + 1) * FEATS, :])
        r_hi = jnp.concatenate([s_hi, norm_hi], 1)
        r_lo = jnp.concatenate([s_lo, norm_lo], 1)
        res = dot(jnp.concatenate([hi, lo], 0), r_hi)
        res = (res[:ROWS] + (res[ROWS:] + dot(hi, r_lo))) * usable
        num = num_ref[:, h * DH : (h + 1) * DH] + res[:, :DH]
        den = den_ref[:, h : h + 1] + res[:, DH + h : DH + h + 1]
        out = (num / den).astype(jnp.bfloat16)
        out_ref[:, h * DH : (h + 1) * DH] = out
        wide = out.astype(jnp.float32)
        squares = squares + wide * wide
    sq_ref[...] = jnp.sum(squares.T, 0, keepdims=True)


def block_of(slot):
    z, x = here()
    src = lax.rem(x + 4 - lax.div(slot - 1, 2), 4)
    behind = jnp.where(lax.rem(slot, 2) == 1, 1, jnp.where(src < x, 0, 2))
    return jnp.where(slot < 3, z * 4 + x - 4 * slot, (z - behind) * 4 + src)


def active(slot, n1, n2):
    z, x = here()
    own = z * 4 + x
    low = start_of(own * ROWS, n1, n2) // ROWS
    return (block_of(slot) >= low) & (block_of(slot) < own) | (slot == 0)


def key_norm(kv_ref, place):
    k = kv_ref[place, :ROWS].astype(jnp.float32)
    return jnp.sum(k * k, 1, keepdims=True)


def gauge_kernel(n_ref, lin_ref, gain_ref, own_ref, near_ref, far_ref, rows_ref, stat_ref):
    most = jnp.zeros((ROWS, 1), jnp.float32)
    for h in range(HEADS):
        lanes = slice(h * DH, (h + 1) * DH)
        q = lin_ref[:, lanes].astype(jnp.float32) * gain_ref[0:1, lanes]
        most = jnp.maximum(most, jnp.sum(q * q, 1, keepdims=True))
    rows_ref[...] = jnp.broadcast_to(most, (ROWS, DH)).T[:8]
    stat_ref[0] = 0.0
    for slot, kv_ref in enumerate((own_ref, near_ref, far_ref)):
        k = kv_ref[:ROWS].astype(jnp.float32)
        norm = jnp.max(jnp.sum(k * k, 1, keepdims=True))
        stat_ref[0] = jnp.where(active(slot, n_ref[0], n_ref[1]), jnp.maximum(stat_ref[0], norm), stat_ref[0])


def scale_of(total_ref):
    return lax.rsqrt(total_ref[...] / ALL_WIDE + 1e-06)


def make_queries(lin_ref, total_ref, gain_ref, q_ref, double):
    scale = jnp.broadcast_to(scale_of(total_ref), (DH, ROWS)).T
    for h in range(HEADS):
        lanes = slice(h * DH, (h + 1) * DH)
        q = (lin_ref[:, lanes].astype(jnp.float32) * scale * gain_ref[0:1, lanes]).astype(jnp.bfloat16)
        lo = jnp.zeros((ROWS, DH), jnp.bfloat16)
        if double:
            q, lo = split(q.astype(jnp.float32) * FACTOR)
        q_ref[h, :, :DH] = q
        q_ref[h, :, DH:] = lo


def ones_beside(v):
    return jnp.concatenate([v, jnp.ones((ROWS, DH), jnp.bfloat16)], 1)


def bounded_tile(kv_ref, place, slot, begin_first, q_ref, acc_ref, keep):
    kk = jnp.concatenate([kv_ref[place, :ROWS]] * 2, 1)
    key = block_of(slot) * ROWS + lax.broadcasted_iota(jnp.int32, (ROWS, 256), 0)
    inside = (key >= begin_first).astype(jnp.float32).astype(jnp.bfloat16)
    v = ones_beside(kv_ref[place, ROWS:]) * inside
    for h in range(HEADS):
        p = jnp.exp2(dot(q_ref[h], kk, NT)).astype(jnp.bfloat16)
        res = dot(p, v)
        acc_ref[h] += res * keep


def bounded_tiles(slots, kv_ref, base, n1, n2, q_ref, acc_ref, before_use):
    first, positions = rows_of()
    begin_first = start_of(first, n1, n2)

    keep = (start_of(positions, n1, n2) == begin_first).astype(jnp.float32)

    def one(slot):
        before_use(slot)
        bounded_tile(kv_ref, slot - base, slot, begin_first, q_ref, acc_ref, keep)

    def step(slot, carry):
        pl.when(active(slot, n1, n2))(lambda: one(slot))
        return carry

    lax.fori_loop(*slots, step, 0)


def make_mask(mask_ref, block, first, begin):
    row = lax.broadcasted_iota(jnp.int32, (ROWS, ROWS), 0)
    key = block * ROWS + lax.broadcasted_iota(jnp.int32, (ROWS, ROWS), 1)
    mask_ref[...] = jnp.where((key >= begin) & (key <= first + row), 0.0, FAR)


def any_tile(kv_ref, slot, base, first, begin, q_ref, acc_ref, mask_ref, top_ref):
    make_mask(mask_ref, block_of(slot), first, begin)
    kk = jnp.concatenate([kv_ref[slot - base, :ROWS]] * 2, 1)
    v = ones_beside(kv_ref[slot - base, ROWS:])

    def head(h, carry):
        s = jnp.maximum(dot(q_ref[h], kk, NT) * FACTOR + mask_ref[...], FAR)
        old = top_ref[h]
        new = jnp.maximum(old, jnp.max(s, 1, keepdims=True))
        p = jnp.exp2(s - jnp.concatenate([new] * 4, 1)).astype(jnp.bfloat16)
        fade = jnp.exp2(old - new)
        acc_ref[h] = acc_ref[h] * jnp.concatenate([fade] * 2, 1) + dot(p, v)
        top_ref[h] = new
        return carry

    lax.fori_loop(0, HEADS, head, 0)


def in_softmax_phase():
    return lax.axis_index("phase") == 1


def rows_of():
    z, x = here()
    first = (z * 4 + x) * ROWS
    return first, first + lax.broadcasted_iota(jnp.int32, (ROWS, 1), 0)


def open_kernel(
    n_ref, gauge_ref, lin_ref, total_ref, gain_ref, rows_ref, own_hbm, near_hbm, far_hbm,
    q_ref, acc_ref, top_hbm, stat_ref, kv_ref, mask_ref, top_ref, sems,
):
    @pl.when(in_softmax_phase())
    def _():
        n1, n2 = n_ref[0], n_ref[1]
        first, positions = rows_of()
        begin = start_of(positions, n1, n2)
        copies = [
            pltpu.make_async_copy(src, kv_ref.at[i], sems.at[i]) for i, src in enumerate((own_hbm, near_hbm, far_hbm))
        ]
        for copy in copies:
            copy.start()
        scale = scale_of(total_ref)
        q_most = 1.02 * jnp.max(scale * scale * rows_ref[0:1, :])
        safe = q_most * gauge_ref[0] < (SAFE / FACTOR) ** 2
        stat_ref[0] = q_most
        stat_ref[1] = jnp.where(safe, 1.0, 0.0)

        @pl.when(safe)
        def _():
            make_queries(lin_ref, total_ref, gain_ref, q_ref, True)
            make_mask(mask_ref, block_of(0), first, begin)
            for copy in copies:
                copy.wait()
            kk = jnp.concatenate([kv_ref[0, :ROWS]] * 2, 1)
            v = ones_beside(kv_ref[0, ROWS:])
            half = ROWS // 2
            for h in range(HEADS):
                for r in range(2):
                    rows, span = slice(r * half, (r + 1) * half), (r + 1) * half
                    s = dot(q_ref[h, rows, :], kk[:span], NT) + mask_ref[rows, :span]
                    acc_ref[h, rows, :] = dot(jnp.exp2(s).astype(jnp.bfloat16), v[:span])
            bounded_tiles((1, 3), kv_ref, 0, n1, n2, q_ref, acc_ref, lambda slot: None)

        @pl.when(jnp.logical_not(safe))
        def _():
            make_queries(lin_ref, total_ref, gain_ref, q_ref, False)
            acc_ref[...] = jnp.zeros_like(acc_ref)
            top_ref[...] = jnp.full(top_ref.shape, FAR, jnp.float32)
            for copy in copies:
                copy.wait()

            def step(slot, carry):
                pl.when(active(slot, n1, n2))(
                    lambda: any_tile(kv_ref, slot, 0, first, begin, q_ref, acc_ref, mask_ref, top_ref)
                )
                return carry

            lax.fori_loop(0, 3, step, 0)
            copy = pltpu.make_async_copy(top_ref, top_hbm, sems.at[0])
            copy.start()
            copy.wait()


def close_kernel(n_ref, stat_ref, lin_ref, total_ref, gain_ref, q_ref, part_ref, top_hbm, *refs):
    kv_hbm, (out_hbm, kv_ref, raw_ref, acc_ref, mask_ref, top_ref, norm_ref, out_ref, kv_sems, out_sems) = refs[:3], refs[3:]

    @pl.when(jnp.logical_not(in_softmax_phase()))
    def _():
        copy = pltpu.make_async_copy(lin_ref, out_hbm, out_sems.at[0])
        copy.start()
        copy.wait()

    @pl.when(in_softmax_phase())
    def _():
        close(
            n_ref, stat_ref, lin_ref, total_ref, gain_ref, q_ref, part_ref, top_hbm, kv_hbm,
            out_hbm, kv_ref, raw_ref, acc_ref, mask_ref, top_ref, norm_ref, out_ref, kv_sems, out_sems,
        )


def close(
    n_ref, stat_ref, lin_ref, total_ref, gain_ref, q_ref, part_ref, top_hbm, kv_hbm,
    out_hbm, kv_ref, raw_ref, acc_ref, mask_ref, top_ref, norm_ref, out_ref, kv_sems, out_sems,
):
    n1, n2 = n_ref[0], n_ref[1]
    base = 3

    def fetch(slot):
        src = kv_hbm[(slot - base) // 2].at[pl.ds((slot - base) % 2 * 2 * ROWS, 2 * ROWS)]
        return pltpu.make_async_copy(src, kv_ref.at[slot - base], kv_sems.at[slot - base])

    def arrived(slot):
        place = kv_ref.at[slot - base]
        pltpu.make_async_copy(place, place, kv_sems.at[slot - base]).wait()

    for slot in range(base, SLOTS):
        pl.when(active(slot, n1, n2))(lambda: fetch(slot).start())
    acc_ref[...] = part_ref[...]
    norm_ref[...] = jnp.zeros_like(norm_ref)
    opened_safe = stat_ref[1] > 0.5

    def before_use(slot):
        arrived(slot)
        norm_ref[...] = jnp.maximum(norm_ref[...], key_norm(kv_ref, slot - base))

    @pl.when(opened_safe)
    def _():
        bounded_tiles((base, SLOTS), kv_ref, base, n1, n2, q_ref, acc_ref, before_use)

    @pl.when(jnp.logical_not(opened_safe))
    def _():
        for slot in range(base, SLOTS):
            pl.when(active(slot, n1, n2))(lambda: arrived(slot))

    safe = opened_safe & (stat_ref[0] * jnp.max(norm_ref[...]) < (SAFE / FACTOR) ** 2)

    @pl.when(jnp.logical_not(safe))
    def _():
        first, positions = rows_of()
        begin = start_of(positions, n1, n2)
        make_queries(lin_ref, total_ref, gain_ref, raw_ref, False)
        acc_ref[...] = part_ref[...]
        top_ref[...] = jnp.zeros_like(top_ref)

        @pl.when(jnp.logical_not(opened_safe))
        def _():
            copy = pltpu.make_async_copy(top_hbm, top_ref, kv_sems.at[0])
            copy.start()
            copy.wait()

        def step(slot, carry):
            pl.when(active(slot, n1, n2))(
                lambda: any_tile(kv_ref, slot, base, first, begin, raw_ref, acc_ref, mask_ref, top_ref)
            )
            return carry

        lax.fori_loop(base, SLOTS, step, 0)

    copies = []
    for h in range(HEADS):
        lanes = slice(h * DH, (h + 1) * DH)
        out_ref[:, lanes] = (acc_ref[h, :, :DH] / acc_ref[h, :, DH:]).astype(jnp.bfloat16)
        copies.append(pltpu.make_async_copy(out_ref.at[:, lanes], out_hbm.at[:, lanes], out_sems.at[h]))
        copies[-1].start()
    for copy in copies:
        copy.wait()


VMEM = pl.BlockSpec(memory_space=pltpu.VMEM)
SMEM = pl.BlockSpec(memory_space=pltpu.SMEM)
ANY = pl.BlockSpec(memory_space=pl.ANY)


def call(kernel, outs, out_specs, args, in_specs, scratch, flops, limit):
    return pl.pallas_call(
        kernel,
        out_shape=tuple(outs),
        in_specs=in_specs,
        out_specs=tuple(out_specs),
        scratch_shapes=scratch,
        compiler_params=pltpu.CompilerParams(vmem_limit_bytes=limit << 20),
        cost_estimate=pl.CostEstimate(flops=flops, bytes_accessed=0, transcendentals=0),
    )(*args)


def shape(dims, dtype=jnp.float32):
    return jax.ShapeDtypeStruct(dims, dtype)


def stash(chunk):
    return call(stash_kernel, [shape(chunk.shape)], [VMEM], (chunk,), [ANY], [pltpu.SemaphoreType.DMA], 0, 4)[0]


def row_sum(parts):
    return call(row_sum_kernel, [shape((QUARTER, DH))], [VMEM], tuple(parts), [VMEM] * 4, [], 0, 8)[0]


def priors_of(parts, near, far):
    return call(
        prior_kernel, [shape((QUARTER, DH))] * 4, [VMEM] * 4, tuple(parts) + (near, far), [VMEM] * 6, [], 1000000000, 8
    )


def pack(own_kv, near_kv, far_kv):
    return call(
        pack_kernel,
        [shape((4 * ROWS, DH), own_kv.dtype)] * 3,
        [ANY] * 3,
        (own_kv, near_kv, far_kv),
        [ANY] * 3,
        [pltpu.SemaphoreType.DMA((6,))],
        5000000000,
        4,
    )


def states(doc_ids, key_feats, values, keys_soft, values_soft):
    bf16 = jnp.bfloat16
    return call(
        states_kernel,
        [shape((QUARTER, DH))] * 4 + [shape((2 * ROWS, DH), bf16), shape((8,), jnp.int32)],
        [VMEM] * 5 + [SMEM],
        (doc_ids.reshape(-1, DH), key_feats, values, keys_soft, values_soft),
        [ANY] * 5,
        [
            pltpu.VMEM((HEADS * FEATS, DH), jnp.float32),
            pltpu.VMEM((doc_ids.shape[0] // DH, DH), jnp.int32),
            pltpu.VMEM((ROWS, DH), bf16),
            pltpu.VMEM((ROWS, WIDE), bf16),
            pltpu.SemaphoreType.DMA((5,)),
        ],
        0,
        60,
    )


def local_part(counts, query_feats, key_feats, values):
    bf16 = jnp.bfloat16
    return call(
        local_kernel,
        [shape((ROWS, WIDE)), shape((ROWS, DH)), shape((ROWS, HEADS * 256), bf16), shape((ROWS, HEADS * 256), bf16)],
        [VMEM] * 4,
        (counts, query_feats, key_feats, values),
        [SMEM] + [VMEM] * 3,
        [pltpu.VMEM((ROWS, ROWS), jnp.float32)],
        0,
        24,
    )


def finish(counts, feats_hi, feats_lo, num, den, parts):
    return call(
        finish_kernel,
        [shape((ROWS, WIDE), jnp.bfloat16), shape((1, ROWS))],
        [VMEM] * 2,
        (counts, feats_hi, feats_lo, num, den) + tuple(parts),
        [SMEM] + [VMEM] * 8,
        [pltpu.VMEM((HEADS * FEATS, DH), jnp.float32)],
        8000000000,
        20,
    )


def gauge(counts, linear_out, gain, own_kv, near_kv, far_kv):
    return call(
        gauge_kernel,
        [shape((8, ROWS)), shape((8,))],
        [VMEM, SMEM],
        (counts, linear_out, gain, own_kv, near_kv, far_kv),
        [SMEM] + [VMEM] * 5,
        [],
        0,
        8,
    )


def soft_open(counts, gauged, linear_out, total, gain, rows, own_kv, near_kv, far_kv):
    bf16 = jnp.bfloat16
    return call(
        open_kernel,
        [shape((HEADS, ROWS, 256), bf16), shape((HEADS, ROWS, 256)), shape((HEADS, ROWS, DH)), shape((8,))],
        [VMEM, VMEM, ANY, SMEM],
        (counts, gauged, linear_out, total, gain, rows, own_kv, near_kv, far_kv),
        [SMEM] * 2 + [VMEM] * 4 + [ANY] * 3,
        [
            pltpu.VMEM((3, 2 * ROWS, DH), bf16),
            pltpu.VMEM((ROWS, ROWS), jnp.float32),
            pltpu.VMEM((HEADS, ROWS, DH), jnp.float32),
            pltpu.SemaphoreType.DMA((3,)),
        ],
        0,
        28,
    )


def soft_close(counts, stat, linear_out, total, gain, queries, part, top, pieces):
    bf16 = jnp.bfloat16
    return call(
        close_kernel,
        [shape((ROWS, WIDE), bf16)],
        [ANY],
        (counts, stat, linear_out, total, gain, queries, part, top) + tuple(pieces),
        [SMEM] * 2 + [VMEM] * 5 + [ANY] * 4,
        [
            pltpu.VMEM((SLOTS - 3, 2 * ROWS, DH), bf16),
            pltpu.VMEM((HEADS, ROWS, 256), bf16),
            pltpu.VMEM((HEADS, ROWS, 256), jnp.float32),
            pltpu.VMEM((ROWS, ROWS), jnp.float32),
            pltpu.VMEM((HEADS, ROWS, DH), jnp.float32),
            pltpu.VMEM((ROWS, 1), jnp.float32),
            pltpu.VMEM((ROWS, WIDE), bf16),
            pltpu.SemaphoreType.DMA((SLOTS - 3,)),
            pltpu.SemaphoreType.DMA((HEADS,)),
        ],
        0,
        32,
    )[0]


def shift(x, axis, by):
    size = lax.axis_size(axis)
    return lax.ppermute(x, axis, [(i, (i + by) % size) for i in range(size)])


def after(x, *others):
    return lax.optimization_barrier((x,) + others)[0]


def local(query_feats, key_feats, values, keys_soft, values_soft, norm_gain, doc_ids):
    zs = lax.axis_size("z")
    *chunks, own_kv, counts = states(doc_ids, key_feats, values, keys_soft, values_soft)

    parts = [stash(chunks[0])] + [shift(chunks[s], "x", s) for s in (1, 2, 3)]

    near_kv = lax.ppermute(own_kv, ("phase", "z"), [(zs + i, zs + i + 1) for i in range(zs - 1)])
    far_kv = lax.ppermute(own_kv, ("phase", "z"), [(i, zs + i + 2) for i in range(zs - 2)])

    local_sums = local_part(counts, query_feats, key_feats, values)
    total = row_sum(parts)
    far = lax.ppermute(
        total,
        ("phase", "z"),
        [((p if i == 0 else 1 - p) * zs + i, p * zs + i + 2) for p in range(2) for i in range(zs - 2)],
    )
    near = lax.ppermute(total, "z", [(i, i + 1) for i in range(zs - 1)])

    messages = lax.optimization_barrier((total,) + tuple(pack(own_kv, near_kv, far_kv)))[1:]
    others = [
        lax.ppermute(message, ("phase", "x"), [(4 + i, 4 + (i + s) % 4) for i in range(4)])
        for s, message in zip((1, 2, 3), messages)
    ]

    far = after(far, *local_sums)
    priors = priors_of(parts, near, far)
    arrived = [priors[0]] + [shift(priors[s], "x", s) for s in (1, 2, 3)]
    num, den, feats_hi, feats_lo = local_sums
    linear_out, squares = finish(counts, feats_hi, feats_lo, num, den, arrived)
    total = squares + shift(squares, "core", 1)
    gain = norm_gain[None]
    rows, gauged = gauge(counts, linear_out, gain, own_kv, near_kv, far_kv)
    total = total + lax.ppermute(total, "y", list(enumerate((1, 0, 3, 2))))
    total = after(total, rows)
    total = total + lax.ppermute(total, "y", list(enumerate((3, 2, 1, 0))))
    queries, part, top, stat = soft_open(counts, gauged, linear_out, total, gain, rows, own_kv, near_kv, far_kv)
    return soft_close(counts, stat, linear_out, total, gain, queries, part, top, others)[None]


def solution(mesh):
    fine = Mesh(mesh.devices.reshape(2, 4, 4, 4, 2), ("phase", "z", "x", "y", "core"))
    seq, head = ("z", "x"), ("y", "core")
    return jax.shard_map(
        local,
        mesh=fine,
        in_specs=(
            P(seq, head),
            P(seq, head),
            P(seq, head),
            P(seq, head),
            P(seq, head),
            P(head),
            P(),
        ),
        out_specs=P("phase", seq, head),
        check_vma=False,
    )
```
